128 devices in a mesh: seq: 64 (over x, y, z), ch: 2 (over core).
Axes of the slice: x: 4, y: 4, z: 4, core: 2. Of those that a mesh axis runs over, the one named last changes fastest.
Arguments:
- tokens: bfloat16 [8192, 1536], P('seq'), may hold values from -16 to 16
- cotangent: bfloat16 [8192, 1536], P('seq'), may hold values from -16 to 16
- seq_lengths: int32 [4], replicated, may hold values from 1 to 4096, 8192 in all
- block_slots: int32 [64], replicated, may hold values from 0 to 63, each once
- mixgain: float32 [1536], replicated, may hold values from 0.25 to 1.75
- inproj: bfloat16 [3, 1536, 1536], P(None, None, 'ch'), may hold values from -0.15625 to 0.15625
- conv_taps: float32 [3, 1536], P(None, 'ch'), may hold values from -3 to 3
- outproj: bfloat16 [1536, 1536], P('ch'), may hold values from -0.15625 to 0.15625
- glugain: float32 [1536], replicated, may hold values from 0.25 to 1.75
- gate_weight: bfloat16 [1536, 6912], P(None, 'ch'), may hold values from -0.15625 to 0.15625
- lift_weight: bfloat16 [1536, 6912], P(None, 'ch'), may hold values from -0.15625 to 0.15625
- down_weight: bfloat16 [6912, 1536], P('ch'), may hold values from -0.078125 to 0.078125
Outputs:
- layer_out: bfloat16 [8192, 1536], P('seq')
- input_grad: bfloat16 [8192, 1536], P('seq')
- mixgain_grad: float32 [1536], P('ch')
- inproj_grad: float32 [3, 1536, 1536], P(None, 'seq', 'ch')
- taps_grad: float32 [3, 1536], P(None, 'ch')
- outproj_grad: float32 [1536, 1536], P('ch', 'seq')
- glugain_grad: float32 [1536], P('ch')
- gate_grad: float32 [1536, 6912], P('seq', 'ch')
- lift_grad: float32 [1536, 6912], P('seq', 'ch')
- down_grad: float32 [6912, 1536], P('ch', 'seq')
The draws below stay inside these ranges and needn't reach their ends.
Inputs may be any that keep to these rules, and one draw needn't show every extreme that they name: `seq_lengths`: the lengths sum to 8192 and the longest is 4096. `block_slots`: A permutation of the 64 blocks; held slot j lies on index j // 1 of seq.
All inputs are finite; a program needn't handle non-finite values.
Results may differ from the reference program's by a relative error of at most 0.014.
Values may be sent and summed in bfloat16 or wider, within the bound.
A program may use at most 512 MiB of HBM per device.

```python
import math
from functools import partial
import jax
import jax.numpy as jnp
import numpy as np
from jax import lax

D = 1536
FF = 6912
TAPS = 3
BLK = 128
TOKENS = 8192
MAXLEN = 4096
NB = 64
NSEQS = 4


def with_spikes(values, stream_key, source, target, parts, factor):
    def block_of(axis_at):
        return (jnp.arange(values.shape[axis_at]) // (values.shape[axis_at] // parts)).reshape((-1,) + (1,) * (values.ndim - 1 - axis_at))

    one_side = jax.random.permutation(stream_key, parts)[block_of(target)]
    second = (block_of(target) + parts // 2) % parts
    return jnp.where((block_of(source) == one_side) | (block_of(source) == second), factor * values, values)


def shard_levels(own_key, extent, shards, smallest, top_value):
    factor_of, own = 1.0, jax.random.fold_in(own_key, 6)
    for position, blocks in shards:
        heights = jnp.exp(jax.random.uniform(jax.random.fold_in(own, position), (blocks,), jnp.float32, smallest / len(shards), top_value / len(shards)))
        factor_of = factor_of * jnp.repeat(heights, extent[position] // blocks).reshape([-1 if axis == position else 1 for axis in range(len(extent))])
    return factor_of


def split_up(number_of, total, limit, skew):
    weights = [(1 << 20) // math.isqrt(rank ** skew) + 1 for rank in range(2, number_of + 1)]
    spare, counts = total - limit - (number_of - 1), [1] * (number_of - 1)
    while spare > 0:
        candidates = [i for i in range(number_of - 1) if counts[i] < limit]
        mass, budget = sum([weights[i] for i in candidates]), spare
        for i in candidates:
            more = min(limit - counts[i], max(1, budget * weights[i] // mass), spare)
            counts[i] = counts[i] + more
            spare = spare - more
    return np.array([limit] + counts)


def ragged_sizes(own_key, count, total, reach, skew):
    if count == 2:
        one = jax.random.randint(own_key, (), max(1, total - reach), min(reach, total - 1) + 1)
        return jnp.stack([one, total - one])
    sizes = jnp.asarray(split_up(count, total, reach, skew), jnp.int32)
    twos = (count - 1) // 2
    giver, sink = sizes[1:1 + 2 * twos:2], sizes[2:2 + 2 * twos:2]
    slack = jnp.minimum(giver - 1, reach - sink)
    moved = jax.random.randint(jax.random.fold_in(own_key, 1), (twos,), 0, 1 << 20) % (slack + 1)
    sizes = sizes.at[1:1 + 2 * twos:2].set(giver - moved).at[2:2 + 2 * twos:2].set(sink + moved)
    return sizes[jax.random.permutation(jax.random.fold_in(own_key, 2), count)]


def scatter_about(stream_key, shape, scale, bound, shards=(), kind=jnp.bfloat16):
    level = shard_levels(stream_key, shape, shards, -0.22, 0.18) if shards else 1.0
    entries = jax.random.normal(stream_key, shape, jnp.float32) * scale * level
    return jnp.minimum(jnp.maximum(entries, -bound), bound).astype(kind)


def noise_with(stream_key, extent, deviation, limit, pieces, heavy, kind=jnp.bfloat16):
    drawn = deviation * jax.random.normal(stream_key, extent, jnp.float32)
    if pieces:
        drawn = drawn * shard_levels(stream_key, extent, pieces, -0.22, 0.18)
    return jnp.clip(with_spikes(drawn, jax.random.fold_in(stream_key, 3), *heavy), -limit, limit).astype(kind)


def setup_inputs(seed: int = 0) -> dict:
    key_list = jax.random.split(jax.random.key(seed), 13)
    return {
        "tokens": noise_with(key_list[0], (TOKENS, D), 1.0, 16.0, ((0, 64),), (0, 1, 64, 4.0)),
        "cotangent": noise_with(key_list[1], (TOKENS, D), 1.0, 16.0, ((0, 64),), (0, 1, 64, 4.0)),
        "seq_lengths": ragged_sizes(key_list[2], NSEQS, TOKENS, MAXLEN, 2).astype(jnp.int32),
        "block_slots": jax.random.permutation(key_list[3], NB).astype(jnp.int32),
        "mixgain": jnp.clip(1.0 + 0.15 * jax.random.normal(key_list[4], (D,), jnp.float32), 0.25, 1.75),
        "inproj": scatter_about(key_list[5], (TAPS, D, D), D ** -0.5, 0.15625, ((2, 2),)),
        "conv_taps": scatter_about(key_list[6], (TAPS, D), 0.6, 3.0, ((1, 2),), jnp.float32),
        "outproj": scatter_about(key_list[7], (D, D), D ** -0.5, 0.15625, ((0, 2),)),
        "glugain": jnp.clip(1.0 + 0.15 * jax.random.normal(key_list[8], (D,), jnp.float32), 0.25, 1.75),
        "gate_weight": scatter_about(key_list[9], (D, FF), D ** -0.5, 0.15625, ((1, 2),)),
        "lift_weight": scatter_about(key_list[10], (D, FF), D ** -0.5, 0.15625, ((1, 2),)),
        "down_weight": scatter_about(key_list[11], (FF, D), FF ** -0.5, 0.078125, ((0, 2),)),
    }


epsilon = 1e-05

@jax.custom_vjp
def low(v):
    return lax.optimization_barrier(v.astype(jnp.bfloat16)).astype(jnp.float32)

@jax.custom_vjp
def low_back(v):
    return v

def low_keep(v):
    return (low(v), None)

def low_pass(kept, grad):
    return (grad,)

def back_keep(v):
    return (v, None)

def back_low(kept, grad):
    return (low(grad),)
low.defvjp(low_keep, low_pass)
low_back.defvjp(back_keep, back_low)

def matmul(left, right):
    return jnp.dot(left, right, precision=lax.Precision.HIGHEST, preferred_element_type=jnp.float32)

def rms_scale(values):
    return lax.rsqrt(lax.optimization_barrier(jnp.mean(values * values, axis=1, keepdims=True)) + epsilon)

def forward(stream, mixgain, inproj, conv_taps, outproj, glugain, gate_weight, lift_weight, down_weight, starts):
    rows_step = min(4096, TOKENS)
    groups = TOKENS // rows_step
    positions = jnp.arange(TOKENS, dtype=jnp.int32)

    def group_step(carry, item):
        resid, first_pos, here_pos = item
        normed = low(resid * rms_scale(resid) * mixgain)
        b_proj = low_back(matmul(normed, inproj[0]))
        c_proj = low_back(matmul(normed, inproj[1]))
        x_proj = low_back(matmul(normed, inproj[2]))
        signal = low(b_proj * x_proj)
        extended = jnp.concatenate([carry, signal], axis=0)
        conv_out = jnp.zeros_like(signal)
        for shift_by in range(3):
            masked = (here_pos - shift_by >= first_pos).astype(jnp.float32)[:, None]
            conv_out = conv_out + conv_taps[shift_by][None, :] * extended[2 - shift_by:2 - shift_by + rows_step] * masked
        gated = low(c_proj * conv_out)
        mixed = low_back(matmul(gated, outproj))
        middle = resid + mixed
        glu_in = low(middle * rms_scale(middle) * glugain)
        gate_pre = low_back(matmul(glu_in, gate_weight))
        lift_pre = low_back(matmul(glu_in, lift_weight))
        hidden = low(jax.nn.silu(gate_pre) * lift_pre)
        result = middle + matmul(hidden, down_weight)
        return (signal[rows_step - 2:], result)
    _, outputs = lax.scan(jax.checkpoint(group_step), jnp.zeros((2, D), jnp.float32), (stream.reshape(groups, rows_step, D), starts.reshape(groups, rows_step), positions.reshape(groups, rows_step)))
    return outputs.reshape(TOKENS, D)

def reference(tokens, cotangent, seq_lengths, block_slots, mixgain, inproj, conv_taps, outproj, glugain, gate_weight, lift_weight, down_weight):

    def to_stream(values):
        return values.astype(jnp.float32).reshape(NB, BLK, D)[block_slots].reshape(TOKENS, D)

    def to_held(values):
        blocks = values.reshape(NB, BLK, D)
        return jnp.zeros((NB, BLK, D), values.dtype).at[block_slots].set(blocks).reshape(TOKENS, D)
    offsets = (jnp.cumsum(seq_lengths) - seq_lengths).astype(jnp.int32)
    positions = jnp.arange(TOKENS, dtype=jnp.int32)
    starts = lax.optimization_barrier(jnp.max(jnp.where(offsets[None, :] <= positions[:, None], offsets[None, :], 0), axis=1)).astype(jnp.int32)
    stream = to_stream(tokens)
    layer, pullback = jax.vjp(partial(forward, starts=starts), stream, mixgain, inproj.astype(jnp.float32), conv_taps, outproj.astype(jnp.float32), glugain, gate_weight.astype(jnp.float32), lift_weight.astype(jnp.float32), down_weight.astype(jnp.float32))
    grads = pullback(to_stream(cotangent))
    return (to_held(layer).astype(jnp.bfloat16), to_held(grads[0]).astype(jnp.bfloat16), grads[1], grads[2], grads[3], grads[4], grads[5], grads[6], grads[7], grads[8])
```

```python
import jax
import jax.numpy as jnp
from jax import lax
from jax.experimental import pallas as pl
from jax.experimental.pallas import tpu as pltpu

from jax.sharding import PartitionSpec as P

MESH = pl.DeviceIdType.MESH
F32, BF16 = jnp.float32, jnp.bfloat16
WS, WM = 896, 256


def spots():
    s = lax.axis_index("seq")
    return (s // 16, (s // 4) % 4, s % 4), lax.axis_index("ch")


def peer(place, axis, step):
    moved = [(place[i] + step) % 4 if i == axis else place[i] for i in range(3)]
    return moved[0] * 16 + moved[1] * 4 + moved[2]


def wide_start(i):
    return pl.multiple_of(jnp.minimum(i * WS, 3456 - WS), 128)


def grads_kernel(
    n2t, cott, n1t, d_gate, d_lift, hidden, mixed_r,
    o_gate, o_lift, o_down, o_in, o_out,
    s_left, s_right, s_bsend, s_bland, s_csend, s_cland, s_dsend, s_dland,
    m_left, m_right, m_bsend, m_bland, m_csend, m_cland, m_dsend, m_dland,
    l_send, l_recv, f_send, f_recv, r_send, r_recv,
    b_send, b_recv, c_send, c_recv, d_send, d_recv, own_sem,
):
    place, core = spots()
    barrier = pltpu.get_barrier_semaphore()
    for axis in range(3):
        for step in range(1, 4):
            pl.semaphore_signal(barrier, inc=1, device_id=(peer(place, axis, step), core), device_id_type=MESH)
    pl.semaphore_signal(barrier, inc=1, device_id=(lax.axis_index("seq"), 1 - core), device_id_type=MESH)
    pl.semaphore_wait(barrier, 10)

    def push(src, dst, send, recv, axis, step):
        copy = pltpu.make_async_remote_copy(
            src_ref=src, dst_ref=dst, send_sem=send, recv_sem=recv,
            device_id=(peer(place, axis, step), core), device_id_type=MESH)
        copy.start()
        return copy

    def cross(src, dst, send, recv):
        copy = pltpu.make_async_remote_copy(
            src_ref=src, dst_ref=dst, send_sem=send, recv_sem=recv,
            device_id=(lax.axis_index("seq"), 1 - core), device_id_type=MESH)
        copy.start()
        return copy

    half = pl.ds(pl.multiple_of(core * 768, 768), 768)
    bufs = (
        (WS, s_left, s_right, s_bsend, s_bland, s_csend, s_cland, s_dsend, s_dland),
        (WM, m_left, m_right, m_bsend, m_bland, m_csend, m_cland, m_dsend, m_dland),
    )

    def start_a(job, k):
        width, left, right = bufs[job][:3]
        me = place[k]
        sent, own = [], []
        for step in range(4):
            target = (me + step) % 4
            lanes = pl.ds(128 * step, 128)
            if job == 0:
                src_l = (n2t, n2t, cott)[k]
                src_r = (d_gate, d_lift, hidden)[k].at[:, pl.ds(wide_start(target), WS)]
            else:
                src_l = n1t.at[jnp.where(target == 3, 1, 0)]
                src_r = mixed_r.at[k, :, pl.ds(pl.multiple_of(target * WM, WM), WM)]
            if step == 0:
                a = pltpu.make_async_copy(src_l, left.at[k, :, lanes], own_sem.at[job, k, 0])
                b = pltpu.make_async_copy(src_r, right.at[k, pl.ds(0, 128), :], own_sem.at[job, k, 1])
                a.start()
                b.start()
                own += [a, b]
            else:
                sent.append((
                    push(src_l.at[half, :], left.at[k, half, lanes], l_send.at[job, k, step - 1], l_recv.at[job, k, step - 1], k, step),
                    push(src_r, right.at[k, pl.ds(128 * step, 128), :], r_send.at[job, k, step - 1], r_recv.at[job, k, step - 1], k, step),
                ))
        return sent, own

    def forward_a(job, k, started):
        left = bufs[job][1]
        out = []
        for step, (lc, rc) in zip(range(1, 4), started[0]):
            lc.wait()
            view = left.at[k, half, pl.ds(128 * step, 128)]
            out.append(cross(view, view, f_send.at[job, k, step - 1], f_recv.at[job, k, step - 1]))
        return out

    def finish_a(started, forwarded):
        for c in started[1]:
            c.wait()
        for lc, rc in started[0]:
            rc.wait()
        for c in forwarded:
            c.wait()

    def start_b(job, k):
        width, left, right, bsend, bland = bufs[job][:5]

        def slab(x, carry):
            acc = jnp.dot(left[k, pl.ds(pl.multiple_of(x * 384, 384), 384), :], right[k], preferred_element_type=F32)
            for j in range(4):
                if k == 0:
                    bsend[k, j, x] = acc[96 * j:96 * j + 96].astype(BF16)
                elif k == 1:
                    bsend[k, j, x] = jnp.concatenate([acc[96 * y + 24 * j:96 * y + 24 * j + 24] for y in range(4)], axis=0).astype(BF16)
                else:
                    bsend[k, x, j] = acc[96 * j:96 * j + 96].astype(BF16)
            return carry

        lax.fori_loop(0, 4, slab, 0)
        axis = (k + 1) % 3
        return [
            push(bsend.at[k, (place[axis] + step) % 4], bland.at[k, step - 1], b_send.at[job, k, step - 1], b_recv.at[job, k, step - 1], axis, step)
            for step in range(1, 4)
        ]

    def start_c(job, k, started):
        width, _, _, bsend, bland, csend, cland = bufs[job][:7]
        for c in started:
            c.wait()
        me = place[(k + 1) % 3]

        def summed(q):
            return (bsend[k, me, q].astype(F32) + bland[k, 0, q].astype(F32)
                    + bland[k, 1, q].astype(F32) + bland[k, 2, q].astype(F32))

        if k == 0:
            for p in range(2):
                a, b = summed(2 * p), summed(2 * p + 1)
                for j in range(4):
                    csend[k, j, 48 * p:48 * p + 48] = jnp.concatenate([a[24 * j:24 * j + 24], b[24 * j:24 * j + 24]], axis=0).astype(BF16)
        else:
            for q in range(4):
                csend[k, q] = summed(q).astype(BF16)
        axis = (k + 2) % 3
        return [
            push(csend.at[k, (place[axis] + step) % 4], cland.at[k, step - 1], c_send.at[job, k, step - 1], c_recv.at[job, k, step - 1], axis, step)
            for step in range(1, 4)
        ]

    def start_d(job, k, started):
        width, _, _, _, _, csend, cland, dsend, dland = bufs[job]
        for c in started:
            c.wait()
        total = (csend[k, place[(k + 2) % 3]].astype(F32) + cland[k, 0].astype(F32)
                 + cland[k, 1].astype(F32) + cland[k, 2].astype(F32))
        for j in range(4):
            dsend[k, j] = total[24 * j:24 * j + 24]
        dland[k, 0] = dsend[k, place[k]]
        return [
            push(dsend.at[k, (place[k] + step) % 4], dland.at[k, step], d_send.at[job, k, step - 1], d_recv.at[job, k, step - 1], k, step)
            for step in range(1, 4)
        ]

    def finish(job, k, started):
        dland = bufs[job][8]
        for c in started:
            c.wait()
        me = place[k]
        for i in range(4):
            slot = (me - i + 4) % 4
            if job == 0:
                out = (o_gate, o_lift, o_down)[k]
                if i < 3:
                    out[:, WS * i:WS * i + WS] = dland[k, slot]
                else:
                    out[:, WS * 3:3456] = dland[k, slot, :, 128:WS]
            elif i < 3:
                o_in[k, :, WM * i:WM * i + WM] = dland[k, slot]
            else:
                o_out[:, WM * k:WM * k + WM] = dland[k, slot]

    a = {(j, k): start_a(j, k) for j in range(2) for k in range(3)}
    b, c, d = {}, {}, {}
    for j in range(2):
        f = {k: forward_a(j, k, a[j, k]) for k in range(3)}
        for k in range(3):
            finish_a(a[j, k], f[k])
            b[j, k] = start_b(j, k)
    for j in range(2):
        for k in range(3):
            c[j, k] = start_c(j, k, b[j, k])
    for j in range(2):
        for k in range(3):
            d[j, k] = start_d(j, k, c[j, k])
    for j in range(2):
        for k in range(3):
            finish(j, k, d[j, k])


def job_scratch(w):
    return [
        pltpu.VMEM((3, 1536, 512), BF16),
        pltpu.VMEM((3, 512, w), BF16),
        pltpu.VMEM((3, 4, 4, 96, w), BF16),
        pltpu.VMEM((3, 3, 4, 96, w), BF16),
        pltpu.VMEM((3, 4, 96, w), BF16),
        pltpu.VMEM((3, 3, 96, w), BF16),
        pltpu.VMEM((3, 4, 24, w), F32),
        pltpu.VMEM((3, 4, 24, w), F32),
    ]


def weight_grads(n2t, cott, n1t, d_gate, d_lift, hidden, mixed_r):
    vm = pl.BlockSpec(memory_space=pltpu.VMEM)
    dma = pltpu.SemaphoreType.DMA
    return pl.pallas_call(
        grads_kernel,
        out_shape=[jax.ShapeDtypeStruct(s, F32) for s in ((24, 3456), (24, 3456), (24, 3456), (3, 24, 768), (24, 768))],
        in_specs=[vm] * 7,
        out_specs=[vm] * 5,
        scratch_shapes=job_scratch(WS) + job_scratch(WM) + [dma((2, 3, 3))] * 12 + [dma((2, 3, 2))],
        compiler_params=pltpu.CompilerParams(collective_id=1, has_side_effects=True, vmem_limit_bytes=62 << 20),
        name="weight_grads",
    )(n2t, cott, n1t, d_gate, d_lift, hidden, mixed_r)


BLK = 128


epsilon = 1e-05


def from_everyone(value, axis):
    copies = jnp.broadcast_to(value, (lax.axis_size(axis), *value.shape))
    return lax.all_to_all(copies, axis, split_axis=0, concat_axis=0, tiled=True)


def laid_out(tiles, dim):
    tiles = jnp.moveaxis(tiles, 0, dim)
    shape = tiles.shape
    return tiles.reshape(*shape[:dim], shape[dim] * shape[dim + 1], *shape[dim + 2 :])


def collect(value, axis, dim):
    tiles = from_everyone(value, axis)
    return laid_out(tiles, dim)


def over_copies(value, axis):
    everything = from_everyone(value, axis)
    return jnp.sum(everything, axis=0)


def taken_together(value, axis):
    everything = from_everyone(value, axis)
    return jnp.sum(everything.astype(jnp.float32), axis=0)


def together(arrays, axis):
    vector, at, finished = (jnp.concatenate([a.reshape(-1) for a in arrays]), 0, [])
    subtotal = over_copies(vector, axis)
    for a in arrays:
        finished.append(subtotal[at : at + a.size].reshape(a.shape))
        at += a.size
    return tuple(finished)


def rms_scale(values):
    return lax.rsqrt(jnp.mean(values * values, axis=1, keepdims=True) + epsilon)


def norm_back(grad_normed, normed, scale, gain):
    scaled = grad_normed * gain
    return scale * (scaled - normed * jnp.mean(scaled * normed, axis=1, keepdims=True))


def on_device(
    tokens,
    cotangent,
    seq_lengths,
    block_slots,
    mixgain,
    inproj,
    conv_taps,
    outproj,
    glugain,
    gate_weight,
    lift_weight,
    down_weight,
):
    rows_here, width = tokens.shape
    channels = inproj.shape[2]
    hidden_units = gate_weight.shape[1]
    local_blocks = rows_here // BLK
    total_blocks = block_slots.shape[0]
    seq_index = lax.axis_index("seq")
    ch_index = lax.axis_index("ch")
    slots = seq_index * local_blocks + jnp.arange(local_blocks, dtype=jnp.int32)
    matches = (block_slots[None, :] == slots[:, None]).astype(jnp.int32)
    block_ids = jnp.sum(matches * jnp.arange(total_blocks, dtype=jnp.int32)[None, :], axis=1)
    before_slot = jnp.take(block_slots, jnp.maximum(block_ids - 1, 0))
    after_slot = jnp.take(block_slots, jnp.minimum(block_ids + 1, total_blocks - 1))
    has_after = block_ids + 1 < total_blocks
    offsets = jnp.cumsum(seq_lengths) - seq_lengths
    positions = block_ids[:, None] * BLK + jnp.arange(BLK, dtype=jnp.int32)[None, :]
    starts = jnp.max(
        jnp.where(offsets[None, None, :] <= positions[:, :, None], offsets[None, None, :], 0),
        axis=2,
    )
    tap_masks = [
        (positions - shift_by >= starts).astype(jnp.float32)[:, :, None] for shift_by in range(3)
    ]
    resid = tokens.astype(jnp.float32)
    scale_a = rms_scale(resid)
    normed_a = resid * scale_a
    mixer_in = (normed_a * mixgain).astype(jnp.bfloat16)
    projected = jnp.einsum("td,kde->kte", mixer_in, inproj, preferred_element_type=jnp.float32)
    b_proj, c_proj, x_proj = (projected[0], projected[1], projected[2])
    signal = (b_proj * x_proj).astype(jnp.bfloat16)
    blocked = signal.reshape(local_blocks, BLK, channels)
    tails = blocked[:, BLK - 2 :, :]
    all_tails = collect(tails, "seq", 0)
    carried = jnp.take(all_tails, before_slot, axis=0)
    extended = jnp.concatenate([carried, blocked], axis=1).astype(jnp.float32)
    conv_out = jnp.zeros((local_blocks, BLK, channels), jnp.float32)
    for shift_by in range(3):
        conv_out = (
            conv_out
            + conv_taps[shift_by][None, None, :]
            * extended[:, 2 - shift_by : 2 - shift_by + BLK, :]
            * tap_masks[shift_by]
        )
    conv_flat = conv_out.reshape(rows_here, channels)
    gated = (c_proj * conv_flat).astype(jnp.bfloat16)
    mixed = over_copies(jnp.dot(gated, outproj, preferred_element_type=jnp.float32), "ch")
    middle = resid + mixed
    scale_b = rms_scale(middle)
    normed_b = middle * scale_b
    glu_in = (normed_b * glugain).astype(jnp.bfloat16)
    gate_pre = jnp.dot(glu_in, gate_weight, preferred_element_type=jnp.float32)
    lift_pre = jnp.dot(glu_in, lift_weight, preferred_element_type=jnp.float32)
    sigmoid_gate = jax.nn.sigmoid(gate_pre)
    silu_gate = gate_pre * sigmoid_gate
    hidden = (silu_gate * lift_pre).astype(jnp.bfloat16)
    glu_out = taken_together(
        jnp.dot(hidden, down_weight, preferred_element_type=jnp.float32).astype(jnp.bfloat16), "ch"
    ).astype(jnp.float32)
    layer_out = (middle + glu_out).astype(jnp.bfloat16)
    upstream = cotangent.astype(jnp.float32)
    hidden_grad = jnp.dot(cotangent, down_weight.T, preferred_element_type=jnp.float32)
    lift_act = (hidden_grad * silu_gate).astype(jnp.bfloat16)
    gate_act = (
        hidden_grad * lift_pre * sigmoid_gate * (1.0 + gate_pre * (1.0 - sigmoid_gate))
    ).astype(jnp.bfloat16)
    glu_in_grad = taken_together(
        (
            jnp.dot(gate_act, gate_weight.T, preferred_element_type=jnp.float32)
            + jnp.dot(lift_act, lift_weight.T, preferred_element_type=jnp.float32)
        ).astype(jnp.bfloat16),
        "ch",
    ).astype(jnp.float32)
    glugain_term = jnp.sum(glu_in_grad * normed_b, axis=0)
    middle_grad = upstream + norm_back(glu_in_grad, normed_b, scale_b, glugain)
    mixed_grad = middle_grad.astype(jnp.bfloat16)
    gated_grad = jnp.dot(mixed_grad, outproj.T, preferred_element_type=jnp.float32)
    c_grad = (gated_grad * conv_flat).astype(jnp.bfloat16)
    conv_grad = (gated_grad * c_proj).reshape(local_blocks, BLK, channels)
    extended_grad = jnp.zeros((local_blocks, BLK + 2, channels), jnp.float32)
    tap_terms = []
    for shift_by in range(3):
        weighted = conv_grad * tap_masks[shift_by]
        tap_terms.append(
            jnp.sum(weighted * extended[:, 2 - shift_by : 2 - shift_by + BLK, :], axis=(0, 1))
        )
        extended_grad = extended_grad + jnp.pad(
            conv_taps[shift_by][None, None, :] * weighted,
            ((0, 0), (2 - shift_by, shift_by), (0, 0)),
        )
    heads = extended_grad[:, :2, :]
    all_heads = collect(heads, "seq", 0)
    incoming = jnp.where(has_after[:, None, None], jnp.take(all_heads, after_slot, axis=0), 0.0)
    signal_grad = (
        extended_grad[:, 2:, :] + jnp.pad(incoming, ((0, 0), (BLK - 2, 0), (0, 0)))
    ).reshape(rows_here, channels)
    proj_grads = jnp.stack(
        [
            (signal_grad * x_proj).astype(jnp.bfloat16),
            c_grad,
            (signal_grad * b_proj).astype(jnp.bfloat16),
        ]
    )
    mixer_in_grad = taken_together(
        jnp.einsum("kte,kde->td", proj_grads, inproj, preferred_element_type=jnp.float32).astype(
            jnp.bfloat16
        ),
        "ch",
    ).astype(jnp.float32)
    mixgain_term = jnp.sum(mixer_in_grad * normed_a, axis=0)
    input_grad = (middle_grad + norm_back(mixer_in_grad, normed_a, scale_a, mixgain)).astype(
        jnp.bfloat16
    )
    mixed_right = jnp.stack(
        [jnp.concatenate([proj_grads[k], gated[:, 256 * k : 256 * k + 256]], axis=1) for k in range(3)]
    )
    gate_grad, lift_grad, down_rows, inproj_grad, out_rows = weight_grads(
        glu_in.T,
        cotangent.T,
        jnp.stack([mixer_in.T, mixed_grad.T]),
        gate_act,
        lift_act,
        hidden,
        mixed_right,
    )
    down_grad = down_rows.T
    outproj_grad = out_rows.T
    mix_half = lax.dynamic_slice_in_dim(mixgain_term, ch_index * channels, channels, 0)
    glu_half = lax.dynamic_slice_in_dim(glugain_term, ch_index * channels, channels, 0)
    mixgain_grad, glugain_grad, taps_grad = together(
        (mix_half, glu_half, jnp.stack(tap_terms)), "seq"
    )
    return (
        layer_out,
        input_grad,
        mixgain_grad,
        inproj_grad,
        taps_grad,
        outproj_grad,
        glugain_grad,
        gate_grad,
        lift_grad,
        down_grad,
    )


def solution(mesh):
    in_specs = (
        P("seq", None),
        P("seq", None),
        P(),
        P(),
        P(),
        P(None, None, "ch"),
        P(None, "ch"),
        P("ch", None),
        P(),
        P(None, "ch"),
        P(None, "ch"),
        P("ch", None),
    )
    out_specs = (
        P("seq", None),
        P("seq", None),
        P("ch"),
        P(None, "seq", "ch"),
        P(None, "ch"),
        P("ch", "seq"),
        P("ch"),
        P("seq", "ch"),
        P("seq", "ch"),
        P("ch", "seq"),
    )
    return jax.shard_map(
        on_device, mesh=mesh, in_specs=in_specs, out_specs=out_specs, check_vma=False
    )
```

```python
import jax
import jax.numpy as jnp
from jax import lax
from jax.experimental import pallas as pl
from jax.experimental.pallas import tpu as pltpu
from jax.sharding import PartitionSpec as P

MESH = pl.DeviceIdType.MESH
F32, BF16 = jnp.float32, jnp.bfloat16
BLK, D, HALF, FF = 128, 1536, 768, 3456
WS, WM, TILE = 896, 256, 384
TILES = FF // TILE
EPS = 1e-05
ROUTES = ((2, 1, 0), (0, 2, 1), (1, 0, 2))
READY = ((0, 3), (3, 5), (5, 7), (7, 9))


def dot_nt(a, b):
    return lax.dot_general(a, b, (((1,), (1,)), ((), ())), preferred_element_type=F32)


def dot_nn(a, b):
    return jnp.dot(a, b, preferred_element_type=F32)


def slice_start(i):
    return pl.multiple_of(jnp.minimum(i * WS, FF - WS), 128)


def layer_kernel(
    seq_lengths, block_slots, mixgain, glugain, taps,
    tokens, cotangent, inproj, outproj, gate_w, lift_w, down_w,
    o_layer, o_input, o_gains, o_gate, o_lift, o_down, o_in, o_out,
    tok_v, cot_v, n1_v, b_v, c_v, x_v, v_v, u_v, y_v, h2_v, n2_v, glu_v, dn2_v,
    col, down_ring, out_v, act, mixed_r, s_src, m_src,
    xh_send, xh_recv, tails, heads, gain_land,
    s_left, s_right, s_bsend, s_bland, s_cland, s_dsend, s_dland, m_left, m_right, m_dsend, m_dland,
    load_sem, col_sem, down_sem, x_send, x_recv, halo_send, halo_recv, gain_send, gain_recv,
    l_send, l_recv, f_send, f_recv, r_send, r_recv,
    b_send, b_recv, c_send, c_recv, d_send, d_recv, own_sem,
):
    seq, core = lax.axis_index("seq"), lax.axis_index("ch")
    place = (seq // 16, (seq // 4) % 4, seq % 4)

    def peer(axis, step):
        at = [(place[i] + step) % 4 if i == axis else place[i] for i in range(3)]
        return at[0] * 16 + at[1] * 4 + at[2]

    def local(src, dst, sem):
        return pltpu.make_async_copy(src, dst, sem)

    def link(src, dst, send, recv, axis, step):
        return pltpu.make_async_remote_copy(
            src_ref=src, dst_ref=dst, send_sem=send, recv_sem=recv,
            device_id=(peer(axis, step), core), device_id_type=MESH)

    def cross(src, dst, send, recv):
        return pltpu.make_async_remote_copy(
            src_ref=src, dst_ref=dst, send_sem=send, recv_sem=recv,
            device_id=(seq, 1 - core), device_id_type=MESH)

    def started(copies):
        for c in copies:
            c.start()
        return copies

    def waited(copies):
        for c in copies:
            c.wait()

    tok_load = local(tokens, tok_v, load_sem.at[0])
    cot_load = local(cotangent, cot_v, load_sem.at[1])
    out_load = local(outproj, out_v, load_sem.at[2])
    in_loads = [local(inproj.at[k], col.at[k], col_sem.at[k, 0]) for k in range(3)]
    tok_load.start()
    in_loads[0].start()
    in_loads[2].start()
    in_loads[1].start()

    def pair_loads(j):
        slot = (j + 3) % 4
        lanes = pl.ds(pl.multiple_of(j * TILE, 128), TILE)
        return [
            local(gate_w.at[:, lanes], col.at[slot, :, pl.ds(0, TILE)], col_sem.at[slot, 0]),
            local(lift_w.at[:, lanes], col.at[slot, :, pl.ds(TILE, TILE)], col_sem.at[slot, 1]),
        ]

    def down_load(j):
        slot = j % 3
        return local(down_w.at[pl.ds(pl.multiple_of(j * TILE, 128), TILE), :], down_ring.at[slot], down_sem.at[slot])

    barrier = pltpu.get_barrier_semaphore()
    for axis in range(3):
        for step in range(1, 4):
            pl.semaphore_signal(barrier, inc=1, device_id=(peer(axis, step), core), device_id_type=MESH)
    pl.semaphore_signal(barrier, inc=1, device_id=(seq, 1 - core), device_id_type=MESH)

    block = jnp.int32(0)
    for i in range(64):
        block = jnp.where(block_slots[i] == seq, i, block)
    before = block_slots[jnp.maximum(block - 1, 0)]
    after = block_slots[jnp.minimum(block + 1, 63)]
    has_after = (block < 63).astype(F32)
    rows = lax.broadcasted_iota(jnp.int32, (BLK, 1), 0)
    positions = block * BLK + rows
    start = jnp.zeros((BLK, 1), jnp.int32)
    offset = jnp.int32(0)
    for i in range(4):
        start = jnp.where(offset <= positions, offset, start)
        offset = offset + seq_lengths[i]
    mask1 = (positions - 1 >= start).astype(F32)
    mask2 = (positions - 2 >= start).astype(F32)

    def halo_links(land, job, phase):
        out = []
        for k in range(3):
            where = [pl.ds(0, 4) if axis in ROUTES[k][:phase] else pl.ds(place[axis], 1) for axis in range(3)]
            view = land.at[k, where[0], where[1], where[2]]
            axis = ROUTES[k][phase]
            for step in range(1, 4):
                out.append(link(view, view, halo_send.at[job, phase, k, step - 1], halo_recv.at[job, phase, k, step - 1], axis, step))
        return out

    def halo_rows(land, slot):
        at = (slot // 16, (slot // 4) % 4, slot % 4)
        return jnp.concatenate([land[k, at[0], at[1], at[2]] for k in range(3)], axis=1)

    def put_halo(land, two):
        for k in range(3):
            land[k, place[0], place[1], place[2]] = two[:, 256 * k:256 * k + 256]

    tok_load.wait()
    resid = tok_v[...].astype(F32)
    scale_a = lax.rsqrt(jnp.mean(resid * resid, axis=1, keepdims=True) + EPS)
    n1 = (resid * scale_a * mixgain[...]).astype(BF16)
    n1_v[...] = n1
    in_loads[0].wait()
    b_v[...] = dot_nn(n1_v[...], col[0])
    in_loads[2].wait()
    x_v[...] = dot_nn(n1_v[...], col[2])
    v_v[...] = (b_v[...] * x_v[...]).astype(BF16).astype(F32)
    put_halo(tails, v_v[BLK - 2:BLK, :])
    pl.semaphore_wait(barrier, 10)
    halo = started(halo_links(tails, 0, 0))
    started([cot_load, out_load])
    started(pair_loads(0))
    for j in range(3):
        down_load(j).start()
    in_loads[1].wait()
    c_v[...] = dot_nn(n1_v[...], col[1])
    for j in range(1, 4):
        started(pair_loads(j))
    waited(halo)
    halo = started(halo_links(tails, 0, 1))
    m_src[0] = n1_v[...].T
    cot_load.wait()
    s_src[1] = cot_v[...].T
    waited(halo)
    halo = started(halo_links(tails, 0, 2))

    half = pl.ds(pl.multiple_of(core * HALF, HALF), HALF)

    def left_link(job, k, src, step):
        left = (s_left, m_left)[job]
        return link(src.at[half, :], left.at[k, half, pl.ds(128 * step, 128)],
                    l_send.at[job, k, step - 1], l_recv.at[job, k, step - 1], k, step)

    def send_left_s(k):
        src = s_src.at[1 if k == 2 else 0]
        local(src, s_left.at[k, :, pl.ds(0, 128)], own_sem.at[0, k, 0]).start()
        for step in range(1, 4):
            left_link(0, k, src, step).start()

    def send_left_m(k, which):
        for step in range(1, 4):
            @pl.when(((place[k] + step) % 4 == 3) == (which == 1))
            def _():
                left_link(1, k, m_src.at[which], step).start()

    send_left_s(2)
    for k in range(3):
        send_left_m(k, 0)

    waited(halo)
    carried = halo_rows(tails, before)
    row_is0, row_is1 = rows == 0, rows == 1
    tap0, tap1, tap2 = taps[0:1, :], taps[1:2, :], taps[2:3, :]

    def shifted():
        v = v_v[...]
        one = jnp.where(row_is0, carried[1:2], pltpu.roll(v, 1, 0)) * mask1
        two = jnp.where(row_is0, carried[0:1], jnp.where(row_is1, carried[1:2], pltpu.roll(v, 2, 0))) * mask2
        return v, one, two

    v0, v1, v2 = shifted()
    u_v[...] = tap0 * v0 + tap1 * v1 + tap2 * v2
    y_v[...] = (c_v[...] * u_v[...]).astype(BF16)
    out_load.wait()
    dn2_v[...] = dot_nn(y_v[...], out_v[...])
    swap = cross(dn2_v, h2_v, x_send.at[0], x_recv.at[0])
    swap.start()
    swap.wait()
    h2_v[...] = tok_v[...].astype(F32) + (dn2_v[...] + h2_v[...])
    h2 = h2_v[...]
    scale_b = lax.rsqrt(jnp.mean(h2 * h2, axis=1, keepdims=True) + EPS)
    n2_v[...] = (h2 * scale_b * glugain[...]).astype(BF16)
    s_src[0] = n2_v[...].T
    send_left_s(0)
    send_left_s(1)

    glu_v[...] = jnp.zeros_like(glu_v)
    dn2_v[...] = jnp.zeros_like(dn2_v)

    def tile(j, carry):
        slot = (j + 3) % 4
        lanes = pl.ds(pl.multiple_of(j * TILE, 128), TILE)
        waited(pair_loads(j))
        both = dot_nn(n2_v[...], col[slot])
        gate_pre, lift_pre = both[:, :TILE], both[:, TILE:]
        down_load(j).wait()
        hidden_grad = dot_nt(cot_v[...], down_ring[j % 3])
        sig = jax.nn.sigmoid(gate_pre)
        silu = gate_pre * sig
        hidden = (silu * lift_pre).astype(BF16)
        d_lift = (hidden_grad * silu).astype(BF16)
        d_gate = (hidden_grad * lift_pre * sig * (1.0 + gate_pre * (1.0 - sig))).astype(BF16)
        act[0, :, lanes] = d_gate
        act[1, :, lanes] = d_lift
        act[2, :, lanes] = hidden
        glu_v[...] += dot_nn(hidden, down_ring[j % 3])
        dn2_v[...] += dot_nt(jnp.concatenate([d_gate, d_lift], axis=1), col[slot])

        @pl.when(j + 4 < TILES)
        def _():
            started(pair_loads(j + 4))

        @pl.when(j + 3 < TILES)
        def _():
            down_load(j + 3).start()

        return carry

    def right_link(job, k, src, step):
        right = (s_right, m_right)[job]
        return link(src, right.at[k, pl.ds(pl.multiple_of(128 * step, 128), 128), :],
                    r_send.at[job, k, step - 1], r_recv.at[job, k, step - 1], k, step)

    def s_piece(k, i):
        return act.at[k, :, pl.ds(slice_start(i), WS)]

    for i, (first, end) in enumerate(READY):
        lax.fori_loop(first, end, tile, 0)
        for k in range(3):
            step = (i - place[k] + 4) % 4

            @pl.when(step != 0)
            def _():
                right_link(0, k, s_piece(k, i), step).start()

    own = {}
    for k in range(3):
        own[0, k] = local(s_piece(k, place[k]), s_right.at[k, pl.ds(0, 128), :], own_sem.at[0, k, 1])
        own[0, k].start()
    started(in_loads)

    xh_send[0] = dn2_v[...].astype(BF16)
    swap_dn2 = cross(xh_send.at[0], xh_recv.at[0], x_send.at[1], x_recv.at[1])
    swap_dn2.start()
    xh_send[1] = glu_v[...].astype(BF16)
    swap_glu = cross(xh_send.at[1], xh_recv.at[1], x_send.at[2], x_recv.at[2])
    swap_glu.start()
    swap_dn2.wait()
    h2 = h2_v[...]
    z2 = h2 * scale_b
    dn2 = xh_send[0].astype(F32) + xh_recv[0].astype(F32)
    glu_term = jnp.sum(dn2 * z2, axis=0, keepdims=True)
    scaled = dn2 * glugain[...]
    glu_v[...] = cot_v[...].astype(F32) + scale_b * (scaled - z2 * jnp.mean(scaled * z2, axis=1, keepdims=True))
    n2_v[...] = glu_v[...].astype(BF16)
    m_src[1] = n2_v[...].T
    for k in range(3):
        send_left_m(k, 1)
        local(m_src.at[jnp.where(place[k] == 3, 1, 0)], m_left.at[k, :, pl.ds(0, 128)], own_sem.at[1, k, 0]).start()
    dy = dot_nt(n2_v[...], out_v[...])
    d_c = (dy * u_v[...]).astype(BF16)
    du = dy * c_v[...]
    v0, v1, v2 = shifted()
    tap_terms = [jnp.sum(du * v, axis=0, keepdims=True) for v in (v0, v1, v2)]
    w1, w2 = tap1 * (du * mask1), tap2 * (du * mask2)
    put_halo(heads, jnp.concatenate([w2[0:1], w1[0:1] + w2[1:2]], axis=0))
    halo = started(halo_links(heads, 1, 0))
    dv = tap0 * du + jnp.where(rows < 127, pltpu.roll(w1, 127, 0), 0.0) + jnp.where(rows < 126, pltpu.roll(w2, 126, 0), 0.0)
    u_v[...] = dv
    y_out = y_v[...]
    for k in range(3):
        mixed_r[k, :, HALF:] = y_out[:, 256 * k:256 * k + 256]
    mixed_r[1, :, :HALF] = d_c
    swap_glu.wait()
    o_layer[...] = (h2_v[...] + (xh_send[1].astype(F32) + xh_recv[1].astype(F32))).astype(BF16)

    lefts, rights, dsends, dlands = (s_left, m_left), (s_right, m_right), (s_dsend, m_dsend), (s_dland, m_dland)

    def b_out(job, k, j, row=0, count=384):
        if job == 0:
            return s_bsend.at[k, j, pl.ds(row, count), :]
        return col.at[3, pl.ds(pl.multiple_of(384 * j + row, 96), count), pl.ds(WM * k, WM)]

    def b_in(job, k, i, row=0, count=384):
        if job == 0:
            return s_bland.at[k, i, pl.ds(row, count), :]
        return down_ring.at[i, pl.ds(row, count), pl.ds(WM * k, WM)]

    def c_out(job, k, j, row=0, count=96):
        return rights[job].at[k, pl.ds(pl.multiple_of(96 * j + row, 48), count), :]

    def c_in(job, k, i):
        if job == 0:
            return s_cland.at[k, i]
        return down_ring.at[i, pl.ds(0, 96), pl.ds(HALF + WM * k, WM)]

    def forward_left(job, k):
        left = lefts[job]
        out = []
        for step in range(1, 4):
            left_link(job, k, m_src.at[0], step).wait()
            view = left.at[k, half, pl.ds(128 * step, 128)]
            out.append(cross(view, view, f_send.at[job, k, step - 1], f_recv.at[job, k, step - 1]))
            out[-1].start()
        return out

    def finish_a(job, k, forwarded):
        local(m_src.at[0], lefts[job].at[k, :, pl.ds(0, 128)], own_sem.at[job, k, 0]).wait()
        own[job, k].wait()
        for step in range(1, 4):
            src = s_piece(k, 0) if job == 0 else mixed_r.at[k, :, pl.ds(0, WM)]
            right_link(job, k, src, step).wait()
        waited(forwarded)

    def start_b(job, k):
        left, right = lefts[job], rights[job]

        def slab(x, carry):
            acc = dot_nn(left[k, pl.ds(pl.multiple_of(x * 384, 384), 384), :], right[k])
            for j in range(4):
                if k == 0:
                    b_out(job, k, j, 96 * x, 96)[...] = acc[96 * j:96 * j + 96].astype(BF16)
                elif k == 1:
                    parts = [acc[96 * y + 24 * j:96 * y + 24 * j + 24] for y in range(4)]
                    b_out(job, k, j, 96 * x, 96)[...] = jnp.concatenate(parts, axis=0).astype(BF16)
                else:
                    b_out(job, k, x, 96 * j, 96)[...] = acc[96 * j:96 * j + 96].astype(BF16)
            return carry

        lax.fori_loop(0, 4, slab, 0)
        axis = (k + 1) % 3
        return started([
            link(b_out(job, k, (place[axis] + step) % 4), b_in(job, k, step - 1),
                 b_send.at[job, k, step - 1], b_recv.at[job, k, step - 1], axis, step)
            for step in range(1, 4)])

    def start_c(job, k, copies):
        waited(copies)
        me = place[(k + 1) % 3]

        def summed(q):
            total = b_out(job, k, me, 96 * q, 96)[...].astype(F32)
            for i in range(3):
                total = total + b_in(job, k, i, 96 * q, 96)[...].astype(F32)
            return total

        if k == 0:
            for p in range(2):
                a, b = summed(2 * p), summed(2 * p + 1)
                for j in range(4):
                    both = jnp.concatenate([a[24 * j:24 * j + 24], b[24 * j:24 * j + 24]], axis=0)
                    c_out(job, k, j, 48 * p, 48)[...] = both.astype(BF16)
        else:
            for q in range(4):
                c_out(job, k, q)[...] = summed(q).astype(BF16)
        axis = (k + 2) % 3
        return started([
            link(c_out(job, k, (place[axis] + step) % 4), c_in(job, k, step - 1),
                 c_send.at[job, k, step - 1], c_recv.at[job, k, step - 1], axis, step)
            for step in range(1, 4)])

    def start_d(job, k, copies):
        dsend, dland = dsends[job], dlands[job]
        waited(copies)
        total = c_out(job, k, place[(k + 2) % 3])[...].astype(F32)
        for i in range(3):
            total = total + c_in(job, k, i)[...].astype(F32)
        pad = jnp.zeros((8, total.shape[1]), F32)
        for j in range(4):
            dsend[k, j] = jnp.concatenate([total[24 * j:24 * j + 24], pad], axis=0).astype(BF16)
        dland[k, 0] = dsend[k, place[k]]
        return started([
            link(dsend.at[k, (place[k] + step) % 4], dland.at[k, step],
                 d_send.at[job, k, step - 1], d_recv.at[job, k, step - 1], k, step)
            for step in range(1, 4)])

    def finish(job, k, copies):
        dland = dlands[job]
        waited(copies)
        for i in range(4):
            piece = dland[k, (place[k] - i + 4) % 4].astype(F32)[:24]
            if job == 0:
                out = (o_gate, o_lift, o_down)[k]
                if i < 3:
                    out[:, WS * i:WS * i + WS] = piece
                else:
                    out[:, WS * 3:FF] = piece[:, 4 * WS - FF:]
            elif i < 3:
                o_in[k, :, WM * i:WM * i + WM] = piece
            else:
                o_out[:, WM * k:WM * k + WM] = piece

    def gain_links(axis):
        view = gain_land.at[axis, place[axis]]
        return [link(view, view, gain_send.at[axis, step - 1], gain_recv.at[axis, step - 1], axis, step) for step in range(1, 4)]

    def gain_sum(axis):
        return (gain_land[axis, 0] + gain_land[axis, 1]) + (gain_land[axis, 2] + gain_land[axis, 3])

    b, c, d = {}, {}, {}
    fwd = [forward_left(0, k) for k in range(3)]
    waited(halo)
    halo = started(halo_links(heads, 1, 1))
    finish_a(0, 0, fwd[0])
    b[0, 0] = start_b(0, 0)
    waited(halo)
    halo = started(halo_links(heads, 1, 2))
    finish_a(0, 1, fwd[1])
    b[0, 1] = start_b(0, 1)
    finish_a(0, 2, fwd[2])
    b[0, 2] = start_b(0, 2)

    waited(halo)
    incoming = halo_rows(heads, after) * has_after
    dv = u_v[...] + jnp.where(rows == 126, incoming[0:1], jnp.where(rows == 127, incoming[1:2], 0.0))
    mixed_r[0, :, :HALF] = (dv * x_v[...]).astype(BF16)
    mixed_r[2, :, :HALF] = (dv * b_v[...]).astype(BF16)

    def m_piece(k, i):
        return mixed_r.at[k, :, pl.ds(pl.multiple_of(i * WM, WM), WM)]

    for k in range(3):
        for step in range(1, 4):
            right_link(1, k, m_piece(k, (place[k] + step) % 4), step).start()
        own[1, k] = local(m_piece(k, place[k]), m_right.at[k, pl.ds(0, 128), :], own_sem.at[1, k, 1])
        own[1, k].start()
    waited(in_loads)
    for k in range(3):
        part = dot_nt(mixed_r[k, :, :HALF], col[k])
        if k == 0:
            dn2_v[...] = part
        else:
            dn2_v[...] += part
    xh_send[2] = dn2_v[...].astype(BF16)
    swap = cross(xh_send.at[2], xh_recv.at[2], x_send.at[3], x_recv.at[3])
    swap.start()
    fwd = [forward_left(1, k) for k in range(3)]
    swap.wait()
    dn1 = xh_send[2].astype(F32) + xh_recv[2].astype(F32)
    z1 = tok_v[...].astype(F32) * scale_a
    mix_term = jnp.sum(dn1 * z1, axis=0, keepdims=True)
    scaled = dn1 * mixgain[...]
    o_input[...] = (glu_v[...] + scale_a * (scaled - z1 * jnp.mean(scaled * z1, axis=1, keepdims=True))).astype(BF16)

    def my_half(row):
        return jnp.where(core == 0, row[:, :HALF], row[:, HALF:])

    gain_land[0, place[0]] = jnp.concatenate(
        [my_half(mix_term), my_half(glu_term), *tap_terms, jnp.zeros((3, HALF), F32)], axis=0)
    gains = started(gain_links(0))
    for k in range(3):
        finish_a(1, k, fwd[k])
        b[1, k] = start_b(1, k)
    waited(gains)
    gain_land[1, place[1]] = gain_sum(0)
    gains = started(gain_links(1))
    for k in range(3):
        c[0, k] = start_c(0, k, b[0, k])
    waited(gains)
    gain_land[2, place[2]] = gain_sum(1)
    gains = started(gain_links(2))
    for k in range(3):
        c[1, k] = start_c(1, k, b[1, k])
    waited(gains)
    o_gains[...] = gain_sum(2)
    for job in range(2):
        for k in range(3):
            d[job, k] = start_d(job, k, c[job, k])
    for job in range(2):
        for k in range(3):
            finish(job, k, d[job, k])


def run_layer(seq_lengths, block_slots, mixgain, glugain, taps, tokens, cotangent, inproj, outproj, gate_w, lift_w, down_w):
    vm = pl.BlockSpec(memory_space=pltpu.VMEM)
    sm = pl.BlockSpec(memory_space=pltpu.SMEM)
    hbm = pl.BlockSpec(memory_space=pl.ANY)
    dma = pltpu.SemaphoreType.DMA
    shape = jax.ShapeDtypeStruct
    full16, full32, half32 = pltpu.VMEM((BLK, D), BF16), pltpu.VMEM((BLK, D), F32), pltpu.VMEM((BLK, HALF), F32)
    return pl.pallas_call(
        layer_kernel,
        out_shape=[shape((BLK, D), BF16), shape((BLK, D), BF16), shape((8, HALF), F32)]
        + [shape(s, F32) for s in ((24, FF), (24, FF), (24, FF), (3, 24, HALF), (24, HALF))],
        in_specs=[sm, sm, vm, vm, vm] + [hbm] * 7,
        out_specs=[vm] * 8,
        scratch_shapes=[
            full16, full16, full16,
            half32, half32, half32, half32, half32, pltpu.VMEM((BLK, HALF), BF16),
            full32, full16, full32, full32,
            pltpu.VMEM((4, D, HALF), BF16), pltpu.VMEM((3, TILE, D), BF16), pltpu.VMEM((HALF, D), BF16),
            pltpu.VMEM((3, BLK, FF), BF16), pltpu.VMEM((3, BLK, 4 * WM), BF16),
            pltpu.VMEM((2, D, BLK), BF16), pltpu.VMEM((2, D, BLK), BF16),
            pltpu.VMEM((3, BLK, D), BF16), pltpu.VMEM((3, BLK, D), BF16),
            pltpu.VMEM((3, 4, 4, 4, 2, 256), F32), pltpu.VMEM((3, 4, 4, 4, 2, 256), F32),
            pltpu.VMEM((3, 4, 8, HALF), F32),
            pltpu.VMEM((3, D, 512), BF16), pltpu.VMEM((3, 512, WS), BF16), pltpu.VMEM((3, 4, 384, WS), BF16),
            pltpu.VMEM((3, 3, 384, WS), BF16), pltpu.VMEM((3, 3, 96, WS), BF16),
            pltpu.VMEM((3, 4, 32, WS), BF16), pltpu.VMEM((3, 4, 32, WS), BF16),
            pltpu.VMEM((3, D, 512), BF16), pltpu.VMEM((3, 512, WM), BF16),
            pltpu.VMEM((3, 4, 32, WM), BF16), pltpu.VMEM((3, 4, 32, WM), BF16),
        ]
        + [dma((3,)), dma((4, 2)), dma((3,)), dma((4,)), dma((4,)),
           dma((2, 3, 3, 3)), dma((2, 3, 3, 3)), dma((3, 3)), dma((3, 3))]
        + [dma((2, 3, 3))] * 12 + [dma((2, 3, 2))],
        compiler_params=pltpu.CompilerParams(collective_id=1, has_side_effects=True, vmem_limit_bytes=LIMIT),
        name="layer",
    )(seq_lengths, block_slots, mixgain, glugain, taps, tokens, cotangent, inproj, outproj, gate_w, lift_w, down_w)


LIMIT = 64 * 1024 * 1024 - 256 * 1024


def on_device(
    tokens, cotangent, seq_lengths, block_slots, mixgain, inproj, conv_taps, outproj, glugain, gate_weight, lift_weight, down_weight
):
    layer_out, input_grad, gains, gate_grad, lift_grad, down_rows, inproj_grad, out_rows = run_layer(
        seq_lengths, block_slots, mixgain[None, :], glugain[None, :], conv_taps,
        tokens, cotangent, inproj, outproj, gate_weight, lift_weight, down_weight,
    )
    return (
        layer_out, input_grad, gains[0], inproj_grad, gains[2:5], out_rows.T, gains[1], gate_grad, lift_grad, down_rows.T,
    )


def solution(mesh):
    in_specs = (
        P("seq", None), P("seq", None), P(), P(), P(), P(None, None, "ch"), P(None, "ch"), P("ch", None),
        P(), P(None, "ch"), P(None, "ch"), P("ch", None),
    )
    out_specs = (
        P("seq", None), P("seq", None), P("ch"), P(None, "seq", "ch"), P(None, "ch"), P("ch", "seq"),
        P("ch"), P("seq", "ch"), P("seq", "ch"), P("ch", "seq"),
    )
    return jax.shard_map(on_device, mesh=mesh, in_specs=in_specs, out_specs=out_specs, check_vma=False)
```

```python
import jax
import jax.numpy as jnp
from jax import lax
from jax.experimental import pallas as pl
from jax.experimental.pallas import tpu as pltpu
from jax.sharding import PartitionSpec as P

MESH = pl.DeviceIdType.MESH
F32, BF16 = jnp.float32, jnp.bfloat16
BLK, D, HALF, FF = 128, 1536, 768, 3456
WS, WM = 896, 256
STEPS, SPAN = 7, 512
EPS = 1e-05
LIMIT = 64 * 1024 * 1024 - 256 * 1024
ROUTES = ((2, 1, 0), (0, 2, 1), (1, 0, 2))
GROUPS = ((0, 256), (256, 256), (512, 256), (768, 128))


def dot_nt(a, b):
    return lax.dot_general(a, b, (((1,), (1,)), ((), ())), preferred_element_type=F32)


def dot_nn(a, b):
    return jnp.dot(a, b, preferred_element_type=F32)


def block_of(i, s):
    return min(7 * i, 20) + s


def layer_kernel(
    seq_lengths, block_slots, mixgain_1d, glugain_1d, taps,
    tokens, cotangent, inproj, outproj, gate_w, lift_w, down_w,
    o_layer, o_input, o_gains, o_gate, o_lift, o_down, o_in, o_out,
    mixgain, glugain, tok_v, cot_v, n_v, b_v, c_v, x_v, v_v, u_v, y_v, h2_v, glu_v, dn2_v,
    col, down_ring, out_v, act, mixed_r, s_src, m_src, xh_send, xh_recv, tails, heads, gain_land,
    s_left, s_right, s_bsend, s_bland, s_cland, s_dsend, s_dland, m_left, m_right, m_dsend, m_dland,
    load_sem, col_sem, down_sem, store_sem, x_send, x_recv, halo_send, halo_recv, gain_send, gain_recv,
    l_send, l_recv, f_send, f_recv, r_send, r_recv,
    b_send, b_recv, c_send, c_recv, d_send, d_recv, own_left, own_right,
):
    seq, core = lax.axis_index("seq"), lax.axis_index("ch")
    place = (seq // 16, (seq // 4) % 4, seq % 4)

    def peer(axis, step):
        at = [(place[i] + step) % 4 if i == axis else place[i] for i in range(3)]
        return at[0] * 16 + at[1] * 4 + at[2]

    def local(src, dst, sem):
        return pltpu.make_async_copy(src, dst, sem)

    def link(src, dst, send, recv, axis, step):
        return pltpu.make_async_remote_copy(
            src_ref=src, dst_ref=dst, send_sem=send, recv_sem=recv,
            device_id=(peer(axis, step), core), device_id_type=MESH)

    def cross(src, dst, send, recv):
        return pltpu.make_async_remote_copy(
            src_ref=src, dst_ref=dst, send_sem=send, recv_sem=recv,
            device_id=(seq, 1 - core), device_id_type=MESH)

    def started(copies):
        for c in copies:
            c.start()
        return copies

    def waited(copies):
        for c in copies:
            c.wait()

    tok_load = local(tokens, tok_v, load_sem.at[0])
    cot_load = local(cotangent, cot_v, load_sem.at[1])
    out_load = local(outproj, out_v, load_sem.at[2])
    gain_loads = [local(mixgain_1d, mixgain.at[0], load_sem.at[3]), local(glugain_1d, glugain.at[0], load_sem.at[4])]
    in_loads = [local(inproj.at[k], col.at[k, :, pl.ds(0, HALF)], col_sem.at[k, 0]) for k in range(3)]
    tok_load.start()
    started(gain_loads)
    in_loads[0].start()
    in_loads[2].start()
    in_loads[1].start()

    def pair_loads(s):
        slot = (s + 1) % 3
        out = []
        for m, w in enumerate((gate_w, lift_w)):
            for i in range(4):
                lanes = pl.ds(128 * block_of(i, s), 128)
                out.append(local(w.at[:, lanes], col.at[slot, :, pl.ds(SPAN * m + 128 * i, 128)], col_sem.at[slot, 4 * m + i]))
        return out

    def down_loads(s):
        slot = s % 3
        return [
            local(down_w.at[pl.ds(128 * block_of(i, s), 128), :], down_ring.at[slot, pl.ds(128 * i, 128), :], down_sem.at[slot, i])
            for i in range(4)]

    barrier = pltpu.get_barrier_semaphore()
    for axis in range(3):
        for step in range(1, 4):
            pl.semaphore_signal(barrier, inc=1, device_id=(peer(axis, step), core), device_id_type=MESH)
    pl.semaphore_signal(barrier, inc=1, device_id=(seq, 1 - core), device_id_type=MESH)

    block = jnp.int32(0)
    for i in range(64):
        block = jnp.where(block_slots[i] == seq, i, block)
    before = block_slots[jnp.maximum(block - 1, 0)]
    after = block_slots[jnp.minimum(block + 1, 63)]
    has_after = (block < 63).astype(F32)
    rows = lax.broadcasted_iota(jnp.int32, (BLK, 1), 0)
    positions = block * BLK + rows
    start = jnp.zeros((BLK, 1), jnp.int32)
    offset = jnp.int32(0)
    for i in range(4):
        start = jnp.where(offset <= positions, offset, start)
        offset = offset + seq_lengths[i]
    mask1 = (positions - 1 >= start).astype(F32)
    mask2 = (positions - 2 >= start).astype(F32)

    def halo_links(land, job, phase):
        out = []
        for k in range(3):
            where = [pl.ds(0, 4) if axis in ROUTES[k][:phase] else pl.ds(place[axis], 1) for axis in range(3)]
            view = land.at[k, where[0], where[1], where[2]]
            axis = ROUTES[k][phase]
            for step in range(1, 4):
                out.append(link(view, view, halo_send.at[job, phase, k, step - 1], halo_recv.at[job, phase, k, step - 1], axis, step))
        return out

    def halo_rows(land, slot):
        at = (slot // 16, (slot // 4) % 4, slot % 4)
        return jnp.concatenate([land[k, at[0], at[1], at[2]] for k in range(3)], axis=1)

    def put_halo(land, two):
        width = two.shape[1] // 3
        for k in range(3):
            land[k, place[0], place[1], place[2]] = two[:, width * k:width * k + width]

    def first_norm(values):
        scale = lax.rsqrt(jnp.mean(values * values, axis=1, keepdims=True) + EPS)
        return scale, values * scale * mixgain[...]

    tok_load.wait()
    put_halo(tails, tok_v[BLK - 16:BLK, :].astype(F32)[14:16])
    pl.semaphore_wait(barrier, 10)
    halo = started(halo_links(tails, 0, 0))
    waited(gain_loads)
    scale_a, n1 = first_norm(tok_v[...].astype(F32))
    n_v[...] = n1.astype(BF16)
    in_loads[0].wait()
    b_v[...] = dot_nn(n_v[...], col[0, :, :HALF])
    waited(halo)
    halo = started(halo_links(tails, 0, 1))
    started([cot_load, out_load])
    for s in range(3):
        started(down_loads(s))
    in_loads[2].wait()
    x_v[...] = dot_nn(n_v[...], col[2, :, :HALF])
    v_v[...] = (b_v[...] * x_v[...]).astype(BF16).astype(F32)
    in_loads[1].wait()
    c_v[...] = dot_nn(n_v[...], col[1, :, :HALF])
    started(pair_loads(0))
    waited(halo)
    halo = started(halo_links(tails, 0, 2))
    m_src[0] = n_v[...].T
    cot_load.wait()
    s_src[1] = cot_v[...].T

    half = pl.ds(pl.multiple_of(core * HALF, HALF), HALF)

    def left_link(job, k, src, step):
        left = (s_left, m_left)[job]
        return link(src.at[half, :], left.at[k, half, pl.ds(128 * step, 128)],
                    l_send.at[job, k, step - 1], l_recv.at[job, k, step - 1], k, step)

    def send_left_s(k):
        src = s_src.at[1 if k == 2 else 0]
        local(src, s_left.at[k, :, pl.ds(0, 128)], own_left.at[0, k]).start()
        for step in range(1, 4):
            left_link(0, k, src, step).start()

    def send_left_m(k, which):
        for step in range(1, 4):
            @pl.when(((place[k] + step) % 4 == 3) == (which == 1))
            def _():
                left_link(1, k, m_src.at[which], step).start()

    def forward_left(job, k):
        left = (s_left, m_left)[job]
        out = []
        for step in range(1, 4):
            left_link(job, k, m_src.at[0], step).wait()
            view = left.at[k, half, pl.ds(128 * step, 128)]
            out.append(cross(view, view, f_send.at[job, k, step - 1], f_recv.at[job, k, step - 1]))
            out[-1].start()
        return out

    send_left_s(2)
    for k in range(3):
        send_left_m(k, 0)

    waited(halo)
    last_two = jnp.concatenate([halo_rows(tails, before), jnp.zeros((14, D), F32)], axis=0)
    edge = first_norm(last_two)[1].astype(BF16)
    carried = (dot_nn(edge, col[0, :, :HALF]) * dot_nn(edge, col[2, :, :HALF])).astype(BF16).astype(F32)
    for s in range(1, 3):
        started(pair_loads(s))
    row_is0, row_is1 = rows == 0, rows == 1
    tap0, tap1, tap2 = taps[0:1, :], taps[1:2, :], taps[2:3, :]

    def shifted():
        v = v_v[...]
        one = jnp.where(row_is0, carried[1:2], pltpu.roll(v, 1, 0)) * mask1
        two = jnp.where(row_is0, carried[0:1], jnp.where(row_is1, carried[1:2], pltpu.roll(v, 2, 0))) * mask2
        return v, one, two

    v0, v1, v2 = shifted()
    u_v[...] = tap0 * v0 + tap1 * v1 + tap2 * v2
    y_v[...] = (c_v[...] * u_v[...]).astype(BF16)
    out_load.wait()
    dn2_v[...] = dot_nn(y_v[...], out_v[...])
    swap = cross(dn2_v, h2_v, x_send.at[0], x_recv.at[0])
    swap.start()
    swap.wait()
    h2_v[...] = tok_v[...].astype(F32) + (dn2_v[...] + h2_v[...])
    h2 = h2_v[...]
    scale_b = lax.rsqrt(jnp.mean(h2 * h2, axis=1, keepdims=True) + EPS)
    n_v[...] = (h2 * scale_b * glugain[...]).astype(BF16)
    s_src[0] = n_v[...].T
    send_left_s(0)
    send_left_s(1)

    lefts, rights, dsends, dlands = (s_left, m_left), (s_right, m_right), (s_dsend, m_dsend), (s_dland, m_dland)

    def right_piece(job, k, i, g):
        if job == 0:
            return act.at[k, i, :, pl.ds(*GROUPS[g])]
        return mixed_r.at[k, :, pl.ds(pl.multiple_of(i * WM, WM), WM)]

    def right_links(job, k, g):
        lanes = pl.ds(*GROUPS[g])
        return [
            link(right_piece(job, k, (place[k] + step) % 4, g), rights[job].at[k, pl.ds(128 * step, 128), lanes],
                 r_send.at[job, k, g, step - 1], r_recv.at[job, k, g, step - 1], k, step)
            for step in range(1, 4)]

    def right_own(job, k, g):
        return local(right_piece(job, k, place[k], g), rights[job].at[k, pl.ds(0, 128), pl.ds(*GROUPS[g])], own_right.at[job, k, g])

    def send_right(job, g):
        for k in range(3):
            right_own(job, k, g).start()
            started(right_links(job, k, g))

    def b_out(job, k, j, g, row=0, count=384):
        lanes = pl.ds(*GROUPS[g])
        if job == 0:
            return s_bsend.at[k, j, pl.ds(row, count), lanes]
        return col.at[0, pl.ds(pl.multiple_of(384 * j + row, 96), count), pl.ds(WM * k, WM)]

    def b_in(job, k, i, g, row=0, count=384):
        if job == 0:
            return s_bland.at[k, i, pl.ds(row, count), pl.ds(*GROUPS[g])]
        return down_ring.at[i, pl.ds(row, count), pl.ds(WM * k, WM)]

    def c_out(job, k, j, g, row=0, count=96):
        return rights[job].at[k, pl.ds(pl.multiple_of(96 * j + row, 48), count), pl.ds(*GROUPS[g])]

    def c_in(job, k, i, g):
        if job == 0:
            return s_cland.at[k, i, :, pl.ds(*GROUPS[g])]
        return down_ring.at[i, pl.ds(0, 96), pl.ds(HALF + WM * k, WM)]

    def b_links(job, k, g):
        axis = (k + 1) % 3
        return [
            link(b_out(job, k, (place[axis] + step) % 4, g), b_in(job, k, step - 1, g),
                 b_send.at[job, k, g, step - 1], b_recv.at[job, k, g, step - 1], axis, step)
            for step in range(1, 4)]

    def c_links(job, k, g):
        axis = (k + 2) % 3
        return [
            link(c_out(job, k, (place[axis] + step) % 4, g), c_in(job, k, step - 1, g),
                 c_send.at[job, k, g, step - 1], c_recv.at[job, k, g, step - 1], axis, step)
            for step in range(1, 4)]

    def start_b(job, k, g):
        right_own(job, k, g).wait()
        waited(right_links(job, k, g))
        lanes = pl.ds(*GROUPS[g])

        def slab(x, carry):
            acc = dot_nn(lefts[job][k, pl.ds(pl.multiple_of(x * 384, 384), 384), :], rights[job][k, :, lanes])
            for j in range(4):
                if k == 0:
                    b_out(job, k, j, g, 96 * x, 96)[...] = acc[96 * j:96 * j + 96].astype(BF16)
                elif k == 1:
                    parts = [acc[96 * y + 24 * j:96 * y + 24 * j + 24] for y in range(4)]
                    b_out(job, k, j, g, 96 * x, 96)[...] = jnp.concatenate(parts, axis=0).astype(BF16)
                else:
                    b_out(job, k, x, g, 96 * j, 96)[...] = acc[96 * j:96 * j + 96].astype(BF16)
            return carry

        lax.fori_loop(0, 4, slab, 0)
        started(b_links(job, k, g))

    def start_c(job, k, g):
        waited(b_links(job, k, g))
        me = place[(k + 1) % 3]

        def summed(q):
            total = b_out(job, k, me, g, 96 * q, 96)[...].astype(F32)
            for i in range(3):
                total = total + b_in(job, k, i, g, 96 * q, 96)[...].astype(F32)
            return total

        if k == 0:
            for p in range(2):
                a, b = summed(2 * p), summed(2 * p + 1)
                for j in range(4):
                    both = jnp.concatenate([a[24 * j:24 * j + 24], b[24 * j:24 * j + 24]], axis=0)
                    c_out(job, k, j, g, 48 * p, 48)[...] = both.astype(BF16)
        else:
            for q in range(4):
                c_out(job, k, q, g)[...] = summed(q).astype(BF16)
        started(c_links(job, k, g))

    def d_links(job, k):
        return [
            link(dsends[job].at[k, (place[k] + step) % 4], dlands[job].at[k, step],
                 d_send.at[job, k, step - 1], d_recv.at[job, k, step - 1], k, step)
            for step in range(1, 4)]

    def start_d(job, k):
        dsend, dland = dsends[job], dlands[job]
        for g in range(4 if job == 0 else 1):
            first, width = GROUPS[g]
            waited(c_links(job, k, g))
            total = c_out(job, k, place[(k + 2) % 3], g)[...].astype(F32)
            for i in range(3):
                total = total + c_in(job, k, i, g)[...].astype(F32)
            pad = jnp.zeros((8, width), F32)
            for j in range(4):
                dsend[k, j, :, first:first + width] = jnp.concatenate([total[24 * j:24 * j + 24], pad], axis=0).astype(BF16)
        dland[k, 0] = dsend[k, place[k]]
        started(d_links(job, k))

    def finish(job, k):
        waited(d_links(job, k))
        stage = (h2_v, glu_v, dn2_v)[k]
        out = []
        for i in range(4):
            piece = dlands[job][k, (place[k] - i + 4) % 4].astype(F32)[:24]
            at = pl.ds(32 * i, 24)
            if job == 0:
                stage[32 * i:32 * i + 24, :WS] = piece
                skip = 0 if i < 3 else 4 * WS - FF
                src = stage.at[at, pl.ds(skip, WS - skip)]
                dst = (o_gate, o_lift, o_down)[k].at[:, pl.ds(WS * i, WS - skip)]
            else:
                stage[32 * i:32 * i + 24, 1024:1024 + WM] = piece
                src = stage.at[at, pl.ds(1024, WM)]
                dst = o_in.at[k, :, pl.ds(WM * i, WM)] if i < 3 else o_out.at[:, pl.ds(WM * k, WM)]
            out.append(local(src, dst, store_sem.at[job, k, i]))
        return started(out)

    glu_v[...] = jnp.zeros_like(glu_v)
    dn2_v[...] = jnp.zeros_like(dn2_v)

    def swiglu_step(s):
        slot = (s + 1) % 3
        waited(pair_loads(s))
        both = dot_nn(n_v[...], col[slot])
        gate_pre, lift_pre = both[:, :SPAN], both[:, SPAN:]
        waited(down_loads(s))
        hidden_grad = dot_nt(cot_v[...], down_ring[s % 3])
        sig = jax.nn.sigmoid(gate_pre)
        silu = gate_pre * sig
        hidden = (silu * lift_pre).astype(BF16)
        d_lift = (hidden_grad * silu).astype(BF16)
        d_gate = (hidden_grad * lift_pre * sig * (1.0 + gate_pre * (1.0 - sig))).astype(BF16)
        for i in range(4):
            for k, values in enumerate((d_gate, d_lift, hidden)):
                act[k, i, :, 128 * s:128 * s + 128] = values[:, 128 * i:128 * i + 128]

        def once(values):
            if s < STEPS - 1:
                return values
            return jnp.concatenate([values[:, :256], jnp.zeros((BLK, 128), BF16), values[:, 384:]], axis=1)

        glu_v[...] += dot_nn(once(hidden), down_ring[s % 3])
        dn2_v[...] += dot_nt(jnp.concatenate([once(d_gate), once(d_lift)], axis=1), col[slot])
        if s + 3 < STEPS:
            started(pair_loads(s + 3))
            started(down_loads(s + 3))

    def left_ready(job, fwd):
        for k in range(3):
            local(m_src.at[0], lefts[job].at[k, :, pl.ds(0, 128)], own_left.at[job, k]).wait()
            waited(fwd[k])

    for s in range(2):
        swiglu_step(s)
    send_right(0, 0)
    swiglu_step(2)
    fwd = [forward_left(0, k) for k in range(3)]
    swiglu_step(3)
    send_right(0, 1)
    left_ready(0, fwd)
    for k in range(3):
        start_b(0, k, 0)
    swiglu_step(4)
    swiglu_step(5)
    send_right(0, 2)
    for k in range(3):
        start_b(0, k, 1)
    swiglu_step(6)
    send_right(0, 3)
    started(in_loads)

    xh_send[0] = dn2_v[...].astype(BF16)
    swap_dn2 = cross(xh_send.at[0], xh_recv.at[0], x_send.at[1], x_recv.at[1])
    swap_dn2.start()
    xh_send[1] = glu_v[...].astype(BF16)
    swap_glu = cross(xh_send.at[1], xh_recv.at[1], x_send.at[2], x_recv.at[2])
    swap_glu.start()
    swap_dn2.wait()
    h2 = h2_v[...]
    z2 = h2 * scale_b
    dn2 = xh_send[0].astype(F32) + xh_recv[0].astype(F32)
    glu_term = jnp.sum(dn2 * z2, axis=0, keepdims=True)
    scaled = dn2 * glugain[...]
    glu_v[...] = cot_v[...].astype(F32) + scale_b * (scaled - z2 * jnp.mean(scaled * z2, axis=1, keepdims=True))
    n_v[...] = glu_v[...].astype(BF16)
    dy = dot_nt(n_v[...], out_v[...])
    d_c = (dy * u_v[...]).astype(BF16)
    du = dy * c_v[...]
    v0, v1, v2 = shifted()
    tap_terms = [jnp.sum(du * v, axis=0, keepdims=True) for v in (v0, v1, v2)]
    w1, w2 = tap1 * (du * mask1), tap2 * (du * mask2)
    put_halo(heads, jnp.concatenate([w2[0:1], w1[0:1] + w2[1:2]], axis=0))
    halo = started(halo_links(heads, 1, 0))
    u_v[...] = (tap0 * du + jnp.where(rows < 127, pltpu.roll(w1, 127, 0), 0.0)
                + jnp.where(rows < 126, pltpu.roll(w2, 126, 0), 0.0))
    m_src[1] = n_v[...].T
    for k in range(3):
        send_left_m(k, 1)
        local(m_src.at[jnp.where(place[k] == 3, 1, 0)], m_left.at[k, :, pl.ds(0, 128)], own_left.at[1, k]).start()
    y_out = y_v[...]
    for k in range(3):
        mixed_r[k, :, HALF:] = y_out[:, 256 * k:256 * k + 256]
    mixed_r[1, :, :HALF] = d_c
    swap_glu.wait()
    xh_send[1] = (h2_v[...] + (xh_send[1].astype(F32) + xh_recv[1].astype(F32))).astype(BF16)
    stores = started([local(xh_send.at[1], o_layer, load_sem.at[5])])
    start_b(0, 0, 2)
    waited(halo)
    halo = started(halo_links(heads, 1, 1))
    start_b(0, 1, 2)
    start_b(0, 2, 2)
    waited(halo)
    halo = started(halo_links(heads, 1, 2))
    for k in range(3):
        start_b(0, k, 3)

    waited(halo)
    incoming = halo_rows(heads, after) * has_after
    dv = u_v[...] + jnp.where(rows == 126, incoming[0:1], jnp.where(rows == 127, incoming[1:2], 0.0))
    mixed_r[0, :, :HALF] = (dv * x_v[...]).astype(BF16)
    mixed_r[2, :, :HALF] = (dv * b_v[...]).astype(BF16)
    send_right(1, 0)
    waited(in_loads)
    for k in range(3):
        part = dot_nt(mixed_r[k, :, :HALF], col[k, :, :HALF])
        if k == 0:
            dn2_v[...] = part
        else:
            dn2_v[...] += part
    xh_send[2] = dn2_v[...].astype(BF16)
    swap = cross(xh_send.at[2], xh_recv.at[2], x_send.at[3], x_recv.at[3])
    swap.start()
    fwd = [forward_left(1, k) for k in range(3)]
    swap.wait()
    dn1 = xh_send[2].astype(F32) + xh_recv[2].astype(F32)
    z1 = tok_v[...].astype(F32) * scale_a
    mix_term = jnp.sum(dn1 * z1, axis=0, keepdims=True)
    scaled = dn1 * mixgain[...]
    xh_send[2] = (glu_v[...] + scale_a * (scaled - z1 * jnp.mean(scaled * z1, axis=1, keepdims=True))).astype(BF16)
    stores += started([local(xh_send.at[2], o_input, load_sem.at[6])])

    def my_half(row):
        return jnp.where(core == 0, row[:, :HALF], row[:, HALF:])

    def gain_links(axis):
        view = gain_land.at[axis, place[axis]]
        return [link(view, view, gain_send.at[axis, step - 1], gain_recv.at[axis, step - 1], axis, step) for step in range(1, 4)]

    def gain_sum(axis):
        return (gain_land[axis, 0] + gain_land[axis, 1]) + (gain_land[axis, 2] + gain_land[axis, 3])

    gain_land[0, place[0]] = jnp.concatenate(
        [my_half(mix_term), my_half(glu_term), *tap_terms, jnp.zeros((3, HALF), F32)], axis=0)
    gains = started(gain_links(0))
    left_ready(1, fwd)
    for k in range(3):
        start_b(1, k, 0)
    for g in range(2):
        for k in range(3):
            start_c(0, k, g)
    waited(gains)
    gain_land[1, place[1]] = gain_sum(0)
    gains = started(gain_links(1))
    for g in range(2, 4):
        for k in range(3):
            start_c(0, k, g)
    waited(gains)
    gain_land[2, place[2]] = gain_sum(1)
    gains = started(gain_links(2))
    for k in range(3):
        start_c(1, k, 0)
    waited(gains)
    v_v[0:8, :] = gain_sum(2)
    stores += started([local(v_v.at[pl.ds(0, 8), :], o_gains, load_sem.at[7])])
    for job in range(2):
        for k in range(3):
            start_d(job, k)
    for job in range(2):
        for k in range(3):
            stores += finish(job, k)
    waited(stores)


def run_layer(seq_lengths, block_slots, mixgain, glugain, taps, tokens, cotangent, inproj, outproj, gate_w, lift_w, down_w):
    vm = pl.BlockSpec(memory_space=pltpu.VMEM)
    sm = pl.BlockSpec(memory_space=pltpu.SMEM)
    hbm = pl.BlockSpec(memory_space=pl.ANY)
    dma = pltpu.SemaphoreType.DMA
    shape = jax.ShapeDtypeStruct
    row, full16, full32, half32 = (
        pltpu.VMEM((1, D), F32), pltpu.VMEM((BLK, D), BF16), pltpu.VMEM((BLK, D), F32), pltpu.VMEM((BLK, HALF), F32))
    return pl.pallas_call(
        layer_kernel,
        out_shape=[shape((BLK, D), BF16), shape((BLK, D), BF16), shape((8, HALF), F32)]
        + [shape(s, F32) for s in ((24, FF), (24, FF), (24, FF), (3, 24, HALF), (24, HALF))],
        in_specs=[sm, sm, hbm, hbm, vm] + [hbm] * 7,
        out_specs=[hbm] * 8,
        scratch_shapes=[
            row, row, full16, full16, full16,
            half32, half32, half32, half32, half32, pltpu.VMEM((BLK, HALF), BF16),
            full32, full32, full32,
            pltpu.VMEM((3, D, 2 * SPAN), BF16), pltpu.VMEM((3, SPAN, D), BF16), pltpu.VMEM((HALF, D), BF16),
            pltpu.VMEM((3, 4, BLK, WS), BF16), pltpu.VMEM((3, BLK, 4 * WM), BF16),
            pltpu.VMEM((2, D, BLK), BF16), pltpu.VMEM((2, D, BLK), BF16),
            pltpu.VMEM((3, BLK, D), BF16), pltpu.VMEM((3, BLK, D), BF16),
            pltpu.VMEM((3, 4, 4, 4, 2, 512), F32), pltpu.VMEM((3, 4, 4, 4, 2, 256), F32),
            pltpu.VMEM((3, 4, 8, HALF), F32),
            pltpu.VMEM((3, D, 512), BF16), pltpu.VMEM((3, 512, WS), BF16), pltpu.VMEM((3, 4, 384, WS), BF16),
            pltpu.VMEM((3, 3, 384, WS), BF16), pltpu.VMEM((3, 3, 96, WS), BF16),
            pltpu.VMEM((3, 4, 32, WS), BF16), pltpu.VMEM((3, 4, 32, WS), BF16),
            pltpu.VMEM((3, D, 512), BF16), pltpu.VMEM((3, 512, WM), BF16),
            pltpu.VMEM((3, 4, 32, WM), BF16), pltpu.VMEM((3, 4, 32, WM), BF16),
            dma((8,)), dma((3, 8)), dma((3, 4)), dma((2, 3, 4)), dma((4,)), dma((4,)),
            dma((2, 3, 3, 3)), dma((2, 3, 3, 3)), dma((3, 3)), dma((3, 3)),
        ]
        + [dma((2, 3, 3))] * 4 + [dma((2, 3, 4, 3))] * 6 + [dma((2, 3, 3))] * 2 + [dma((2, 3)), dma((2, 3, 4))],
        compiler_params=pltpu.CompilerParams(collective_id=1, has_side_effects=True, vmem_limit_bytes=LIMIT),
        name="layer",
    )(seq_lengths, block_slots, mixgain, glugain, taps, tokens, cotangent, inproj, outproj, gate_w, lift_w, down_w)


def place_kernel(*refs):
    ins, outs, held, in_sems, out_sems = refs[:8], refs[8:18], refs[18:26], refs[26], refs[27]
    loads = [pltpu.make_async_copy(a, b, in_sems.at[i]) for i, (a, b) in enumerate(zip(ins, held))]
    for c in loads:
        c.start()
    gains = held[2]
    parts = [held[0], held[1], gains.at[0], gains.at[1], gains.at[pl.ds(2, 3)], *held[3:]]
    stores = []
    for i, (a, b) in enumerate(zip(parts, outs)):
        if i not in (3, 4):
            loads[i if i < 3 else i - 2].wait()
        stores.append(pltpu.make_async_copy(a, b, out_sems.at[i]))
        stores[-1].start()
    for c in stores:
        c.wait()


def place_outputs(results):
    hbm = pl.BlockSpec(memory_space=pl.ANY)
    shape = jax.ShapeDtypeStruct
    return pl.pallas_call(
        place_kernel,
        out_shape=[shape((BLK, D), BF16), shape((BLK, D), BF16), shape((HALF,), F32), shape((HALF,), F32), shape((3, HALF), F32)]
        + [shape(s, F32) for s in ((24, FF), (24, FF), (24, FF), (3, 24, HALF), (24, HALF))],
        in_specs=[hbm] * 8,
        out_specs=[hbm] * 10,
        scratch_shapes=[pltpu.VMEM(r.shape, r.dtype) for r in results] + [pltpu.SemaphoreType.DMA((8,)), pltpu.SemaphoreType.DMA((10,))],
        name="place",
    )(*results)


def on_device(
    tokens, cotangent, seq_lengths, block_slots, mixgain, inproj, conv_taps, outproj, glugain, gate_weight, lift_weight, down_weight
):
    results = run_layer(
        seq_lengths, block_slots, mixgain, glugain, conv_taps,
        tokens, cotangent, inproj, outproj, gate_weight, lift_weight, down_weight,
    )
    layer_out, input_grad, mixgain_grad, glugain_grad, taps_grad, gate_grad, lift_grad, down_rows, inproj_grad, out_rows = place_outputs(results)
    return (
        layer_out, input_grad, mixgain_grad, inproj_grad, taps_grad, out_rows.T, glugain_grad, gate_grad, lift_grad, down_rows.T,
    )


def solution(mesh):
    in_specs = (
        P("seq", None), P("seq", None), P(), P(), P(), P(None, None, "ch"), P(None, "ch"), P("ch", None),
        P(), P(None, "ch"), P(None, "ch"), P("ch", None),
    )
    out_specs = (
        P("seq", None), P("seq", None), P("ch"), P(None, "seq", "ch"), P(None, "ch"), P("ch", "seq"),
        P("ch"), P("seq", "ch"), P("seq", "ch"), P("ch", "seq"),
    )
    return jax.shard_map(on_device, mesh=mesh, in_specs=in_specs, out_specs=out_specs, check_vma=False)
```

```python
import jax
import jax.numpy as jnp
from jax import lax
from jax.experimental import pallas as pl
from jax.experimental.pallas import tpu as pltpu
from jax.sharding import PartitionSpec as P

MESH = pl.DeviceIdType.MESH
F32, BF16 = jnp.float32, jnp.bfloat16
BLK, D, HALF, FF = 128, 1536, 768, 3456
WS, WM = 896, 256
STEPS, SPAN = 7, 512
EPS = 1e-05
LIMIT = 64 * 1024 * 1024 - 256 * 1024
ROUTES = ((2, 1, 0), (0, 2, 1), (1, 0, 2))
GROUPS = ((0, 256), (256, 256), (512, 256), (768, 128))


def dot_nt(a, b):
    return lax.dot_general(a, b, (((1,), (1,)), ((), ())), preferred_element_type=F32)


def outer(a, b):
    return lax.dot_general(a, b, (((0,), (0,)), ((), ())), preferred_element_type=F32)


def dot_nn(a, b):
    return jnp.dot(a, b, preferred_element_type=F32)


def block_of(i, s):
    return min(7 * i, 20) + s


def layer_kernel(
    seq_lengths, block_slots, mixgain_1d, glugain_1d, taps,
    tokens, cotangent, inproj, outproj, gate_w, lift_w, down_w,
    o_layer, o_input, o_gains, o_gate, o_lift, o_down, o_in, o_out,
    mixgain, glugain, tok_v, cot_v, n_v, b_v, c_v, x_v, v_v, u_v, y_v, h2_v, glu_v, dn2_v,
    col, down_ring, out_v, da_v, act, mixed_r, s_src, m_src, e_src, eb_v, ex_v, er_src, e_left, e_right, xh_send, xh_recv, tails, heads, gain_land,
    s_left, s_right, s_bsend, s_bland, s_cland, s_dsend, s_dland, m_left, m_right, m_dsend, m_dland,
    load_sem, col_sem, down_sem, store_sem, x_send, x_recv, halo_send, halo_recv, gain_send, gain_recv,
    l_send, l_recv, f_send, f_recv, r_send, r_recv,
    b_send, b_recv, c_send, c_recv, d_send, d_recv, own_left, own_right, e_send, e_recv, own_edge,
):
    seq, core = lax.axis_index("seq"), lax.axis_index("ch")
    place = (seq // 16, (seq // 4) % 4, seq % 4)

    def peer(axis, step):
        at = [(place[i] + step) % 4 if i == axis else place[i] for i in range(3)]
        return at[0] * 16 + at[1] * 4 + at[2]

    def local(src, dst, sem):
        return pltpu.make_async_copy(src, dst, sem)

    def link(src, dst, send, recv, axis, step):
        return pltpu.make_async_remote_copy(
            src_ref=src, dst_ref=dst, send_sem=send, recv_sem=recv,
            device_id=(peer(axis, step), core), device_id_type=MESH)

    def cross(src, dst, send, recv):
        return pltpu.make_async_remote_copy(
            src_ref=src, dst_ref=dst, send_sem=send, recv_sem=recv,
            device_id=(seq, 1 - core), device_id_type=MESH)

    def started(copies):
        for c in copies:
            c.start()
        return copies

    def waited(copies):
        for c in copies:
            c.wait()

    tok_load = local(tokens, tok_v, load_sem.at[0])
    cot_load = local(cotangent, cot_v, load_sem.at[1])
    out_load = local(outproj, out_v, load_sem.at[2])
    gain_loads = [local(mixgain_1d, mixgain.at[0], load_sem.at[3]), local(glugain_1d, glugain.at[0], load_sem.at[4])]
    in_loads = [local(inproj.at[k], col.at[k, :, pl.ds(0, HALF)], col_sem.at[k, 0]) for k in range(3)]
    tok_load.start()
    started(gain_loads)
    in_loads[0].start()
    in_loads[2].start()
    in_loads[1].start()

    def pair_loads(s):
        slot = (s + 1) % 3
        out = []
        for m, w in enumerate((gate_w, lift_w)):
            for i in range(4):
                lanes = pl.ds(128 * block_of(i, s), 128)
                out.append(local(w.at[:, lanes], col.at[slot, :, pl.ds(SPAN * m + 128 * i, 128)], col_sem.at[slot, 4 * m + i]))
        return out

    def down_loads(t):
        s, slot = t % STEPS, t % 3
        return [
            local(down_w.at[pl.ds(128 * block_of(i, s), 128), :], down_ring.at[slot, pl.ds(128 * i, 128), :], down_sem.at[slot, i])
            for i in range(4)]

    barrier = pltpu.get_barrier_semaphore()
    for axis in range(3):
        for step in range(1, 4):
            pl.semaphore_signal(barrier, inc=1, device_id=(peer(axis, step), core), device_id_type=MESH)
    pl.semaphore_signal(barrier, inc=1, device_id=(seq, 1 - core), device_id_type=MESH)

    block = jnp.int32(0)
    for i in range(64):
        block = jnp.where(block_slots[i] == seq, i, block)
    before = block_slots[jnp.maximum(block - 1, 0)]
    after = block_slots[jnp.minimum(block + 1, 63)]
    has_after = (block < 63).astype(F32)
    rows = lax.broadcasted_iota(jnp.int32, (BLK, 1), 0)
    positions = block * BLK + rows
    start = jnp.zeros((BLK, 1), jnp.int32)
    offset = jnp.int32(0)
    for i in range(4):
        start = jnp.where(offset <= positions, offset, start)
        offset = offset + seq_lengths[i]
    mask1 = (positions - 1 >= start).astype(F32)
    mask2 = (positions - 2 >= start).astype(F32)

    def halo_links(land, job, phase):
        out = []
        for k in range(3):
            where = [pl.ds(0, 4) if axis in ROUTES[k][:phase] else pl.ds(place[axis], 1) for axis in range(3)]
            view = land.at[k, where[0], where[1], where[2]]
            axis = ROUTES[k][phase]
            for step in range(1, 4):
                out.append(link(view, view, halo_send.at[job, phase, k, step - 1], halo_recv.at[job, phase, k, step - 1], axis, step))
        return out

    def halo_rows(land, slot):
        at = (slot // 16, (slot // 4) % 4, slot % 4)
        return jnp.concatenate([land[k, at[0], at[1], at[2]] for k in range(3)], axis=1)

    def put_halo(land, two):
        width = two.shape[1] // 3
        for k in range(3):
            land[k, place[0], place[1], place[2]] = two[:, width * k:width * k + width]

    def first_norm(values):
        scale = lax.rsqrt(jnp.mean(values * values, axis=1, keepdims=True) + EPS)
        return scale, values * scale * mixgain[...]

    tok_load.wait()
    put_halo(tails, tok_v[BLK - 16:BLK, :].astype(F32)[14:16])
    pl.semaphore_wait(barrier, 10)
    halo = started(halo_links(tails, 0, 0))
    waited(gain_loads)
    scale_a, n1 = first_norm(tok_v[...].astype(F32))
    n_v[...] = n1.astype(BF16)
    in_loads[0].wait()
    b_v[...] = dot_nn(n_v[...], col[0, :, :HALF])
    started([cot_load])
    for s in range(3):
        started(down_loads(s))
    waited(halo)
    halo = started(halo_links(tails, 0, 1))
    in_loads[2].wait()
    x_v[...] = dot_nn(n_v[...], col[2, :, :HALF])
    v_v[...] = (b_v[...] * x_v[...]).astype(BF16).astype(F32)
    in_loads[1].wait()
    c_v[...] = dot_nn(n_v[...], col[1, :, :HALF])
    started(pair_loads(0))
    cot_load.wait()

    def hidden_grads(first, end):
        for s in range(first, end):
            waited(down_loads(s))
            da_v[s] = dot_nt(cot_v[...], down_ring[s % 3])
            started(down_loads(s + 3))

    waited(halo)
    halo = started(halo_links(tails, 0, 2))
    s_src[1] = cot_v[...].T
    m_src[0] = n_v[...].T

    half = pl.ds(pl.multiple_of(core * HALF, HALF), HALF)

    def left_link(job, k, src, step):
        left = (s_left, m_left)[job]
        return link(src.at[half, :], left.at[k, half, pl.ds(128 * step, 128)],
                    l_send.at[job, k, step - 1], l_recv.at[job, k, step - 1], k, step)

    def send_left_s(k):
        src = s_src.at[1 if k == 2 else 0]
        local(src, s_left.at[k, :, pl.ds(0, 128)], own_left.at[0, k]).start()
        for step in range(1, 4):
            left_link(0, k, src, step).start()

    def send_left_m(k, which):
        for step in range(1, 4):
            @pl.when(((place[k] + step) % 4 == 3) == (which == 1))
            def _():
                left_link(1, k, m_src.at[which], step).start()

    def forward_left(job, k):
        left = (s_left, m_left)[job]
        out = []
        for step in range(1, 4):
            left_link(job, k, m_src.at[0], step).wait()
            view = left.at[k, half, pl.ds(128 * step, 128)]
            out.append(cross(view, view, f_send.at[job, k, step - 1], f_recv.at[job, k, step - 1]))
            out[-1].start()
        return out

    send_left_s(2)
    for k in range(3):
        send_left_m(k, 0)
    started([out_load])
    hidden_grads(0, STEPS)

    waited(halo)
    last_two = jnp.concatenate([halo_rows(tails, before), jnp.zeros((14, D), F32)], axis=0)
    edge = first_norm(last_two)[1].astype(BF16)
    edge_b, edge_x = dot_nn(edge, col[0, :, :HALF]), dot_nn(edge, col[2, :, :HALF])
    carried = (edge_b * edge_x).astype(BF16).astype(F32)
    e_src[...] = edge
    eb_v[...] = edge_b
    ex_v[...] = edge_x

    def edge_left_links(n):
        return [
            link(e_src, e_left.at[n, pl.ds(16 * step, 16), :], e_send.at[0, n, step - 1], e_recv.at[0, n, step - 1], 2 * n, step)
            for step in range(1, 4)]

    def edge_piece(n, i):
        return er_src.at[n, :, pl.ds(pl.multiple_of(i * WM, WM), WM)]

    def edge_right_links(n):
        return [
            link(edge_piece(n, (place[2 * n] + step) % 4), e_right.at[n, pl.ds(16 * step, 16), :],
                 e_send.at[1, n, step - 1], e_recv.at[1, n, step - 1], 2 * n, step)
            for step in range(1, 4)]

    def edge_own(n):
        return [
            local(e_src, e_left.at[n, pl.ds(0, 16), :], own_edge.at[0, n]),
            local(edge_piece(n, place[2 * n]), e_right.at[n, pl.ds(0, 16), :], own_edge.at[1, n])]
    for s in range(1, 3):
        started(pair_loads(s))
    row_is0, row_is1 = rows == 0, rows == 1
    tap0, tap1, tap2 = taps[0:1, :], taps[1:2, :], taps[2:3, :]

    def shifted():
        v = v_v[...]
        one = jnp.where(row_is0, carried[1:2], pltpu.roll(v, 1, 0)) * mask1
        two = jnp.where(row_is0, carried[0:1], jnp.where(row_is1, carried[1:2], pltpu.roll(v, 2, 0))) * mask2
        return v, one, two

    v0, v1, v2 = shifted()
    u_v[...] = tap0 * v0 + tap1 * v1 + tap2 * v2
    y_v[...] = (c_v[...] * u_v[...]).astype(BF16)
    out_load.wait()
    dn2_v[...] = dot_nn(y_v[...], out_v[...])
    swap = cross(dn2_v, h2_v, x_send.at[0], x_recv.at[0])
    swap.start()
    swap.wait()
    h2_v[...] = tok_v[...].astype(F32) + (dn2_v[...] + h2_v[...])
    h2 = h2_v[...]
    scale_b = lax.rsqrt(jnp.mean(h2 * h2, axis=1, keepdims=True) + EPS)
    n_v[...] = (h2 * scale_b * glugain[...]).astype(BF16)
    s_src[0] = n_v[...].T
    send_left_s(0)
    send_left_s(1)

    lefts, rights, dsends, dlands = (s_left, m_left), (s_right, m_right), (s_dsend, m_dsend), (s_dland, m_dland)

    def right_piece(job, k, i, g):
        if job == 0:
            return act.at[k, i, :, pl.ds(*GROUPS[g])]
        return mixed_r.at[k, :, pl.ds(pl.multiple_of(i * WM, WM), WM)]

    def right_links(job, k, g):
        lanes = pl.ds(*GROUPS[g])
        return [
            link(right_piece(job, k, (place[k] + step) % 4, g), rights[job].at[k, pl.ds(128 * step, 128), lanes],
                 r_send.at[job, k, g, step - 1], r_recv.at[job, k, g, step - 1], k, step)
            for step in range(1, 4)]

    def right_own(job, k, g):
        return local(right_piece(job, k, place[k], g), rights[job].at[k, pl.ds(0, 128), pl.ds(*GROUPS[g])], own_right.at[job, k, g])

    def send_right(job, g):
        for k in range(3):
            right_own(job, k, g).start()
            started(right_links(job, k, g))

    def b_out(job, k, j, g, row=0, count=384):
        lanes = pl.ds(*GROUPS[g])
        if job == 0:
            return s_bsend.at[k, j, pl.ds(row, count), lanes]
        return col.at[1, pl.ds(pl.multiple_of(384 * j + row, 96), count), pl.ds(WM * k, WM)]

    def b_in(job, k, i, g, row=0, count=384):
        if job == 0:
            return s_bland.at[k, i, pl.ds(row, count), pl.ds(*GROUPS[g])]
        return down_ring.at[i, pl.ds(row, count), pl.ds(WM * k, WM)]

    def c_out(job, k, j, g, row=0, count=96):
        return rights[job].at[k, pl.ds(pl.multiple_of(96 * j + row, 48), count), pl.ds(*GROUPS[g])]

    def c_in(job, k, i, g):
        if job == 0:
            return s_cland.at[k, i, :, pl.ds(*GROUPS[g])]
        return down_ring.at[i, pl.ds(0, 96), pl.ds(HALF + WM * k, WM)]

    LOW, HIGH = 0, 192

    def b_links(job, k, g, which):
        axis = (k + 1) % 3
        me = place[axis]
        opposite, ahead, behind = (me + 2) % 4, (me + 1) % 4, (me + 3) % 4
        table = (
            (opposite, LOW, 2, 1), (ahead, HIGH, 0, 1), (opposite, HIGH, 2, 3),
            (behind, LOW, 1, 3), (ahead, LOW, 0, 1), (behind, HIGH, 1, 3))
        out = []
        for n in which:
            part, row, land, step = table[n]
            out.append(link(b_out(job, k, part, g, row, 192), b_in(job, k, land, g, row, 192),
                            b_send.at[job, k, g, n], b_recv.at[job, k, g, n], axis, step))
        return out

    def c_links(job, k, g):
        axis = (k + 2) % 3
        return [
            link(c_out(job, k, (place[axis] + step) % 4, g), c_in(job, k, step - 1, g),
                 c_send.at[job, k, g, step - 1], c_recv.at[job, k, g, step - 1], axis, step)
            for step in range(1, 4)]

    def start_b(job, k, g):
        right_own(job, k, g).wait()
        waited(right_links(job, k, g))
        lanes = pl.ds(*GROUPS[g])
        edges = job == 1 and k != 1
        if edges:
            for c in edge_own(k // 2):
                c.wait()
            waited(edge_left_links(k // 2))
            waited(edge_right_links(k // 2))

        def slab(x, carry):
            at = pl.ds(pl.multiple_of(x * HALF, HALF), HALF)
            acc = dot_nn(lefts[job][k, at, :], rights[job][k, :, lanes])
            if edges:
                acc = acc + outer(e_left[k // 2, :, at], e_right[k // 2])
            for h in range(2):
                row = pl.multiple_of(192 * x + 96 * h, 96)
                for j in range(4):
                    base = 384 * h + 96 * j
                    if k == 0:
                        b_out(job, k, j, g, row, 96)[...] = acc[base:base + 96].astype(BF16)
                    elif k == 1:
                        parts = [acc[384 * h + 96 * y + 24 * j:384 * h + 96 * y + 24 * j + 24] for y in range(4)]
                        b_out(job, k, j, g, row, 96)[...] = jnp.concatenate(parts, axis=0).astype(BF16)
                    else:
                        b_out(job, k, 2 * x + h, g, 96 * j, 96)[...] = acc[base:base + 96].astype(BF16)
            return carry

        lax.fori_loop(0, 2, slab, 0)
        started(b_links(job, k, g, range(4)))

    def pass_on(job, k, g):
        waited(b_links(job, k, g, (0, 2)))
        me = place[(k + 1) % 3]
        for step, row in ((1, LOW), (3, HIGH)):
            own, via = b_out(job, k, (me + step) % 4, g, row, 192), b_in(job, k, 2, g, row, 192)
            own[...] = (own[...].astype(F32) + via[...].astype(F32)).astype(BF16)
        started(b_links(job, k, g, (4, 5)))

    def start_c(job, k, g):
        waited(b_links(job, k, g, (1, 3, 4, 5)))
        me = place[(k + 1) % 3]

        def summed(q):
            total = b_out(job, k, me, g, 96 * q, 96)[...].astype(F32)
            for i in range(2):
                total = total + b_in(job, k, i, g, 96 * q, 96)[...].astype(F32)
            return total

        if k == 0:
            for p in range(2):
                a, b = summed(2 * p), summed(2 * p + 1)
                for j in range(4):
                    both = jnp.concatenate([a[24 * j:24 * j + 24], b[24 * j:24 * j + 24]], axis=0)
                    c_out(job, k, j, g, 48 * p, 48)[...] = both.astype(BF16)
        else:
            for q in range(4):
                c_out(job, k, q, g)[...] = summed(q).astype(BF16)
        started(c_links(job, k, g))

    def d_links(job, k):
        return [
            link(dsends[job].at[k, (place[k] + step) % 4], dlands[job].at[k, step],
                 d_send.at[job, k, step - 1], d_recv.at[job, k, step - 1], k, step)
            for step in range(1, 4)]

    def start_d(job, k):
        dsend, dland = dsends[job], dlands[job]
        for g in range(4 if job == 0 else 1):
            first, width = GROUPS[g]
            waited(c_links(job, k, g))
            total = c_out(job, k, place[(k + 2) % 3], g)[...].astype(F32)
            for i in range(3):
                total = total + c_in(job, k, i, g)[...].astype(F32)
            pad = jnp.zeros((8, width), F32)
            for j in range(4):
                dsend[k, j, :, first:first + width] = jnp.concatenate([total[24 * j:24 * j + 24], pad], axis=0).astype(BF16)
        dland[k, 0] = dsend[k, place[k]]
        started(d_links(job, k))

    def finish(job, k):
        waited(d_links(job, k))
        stage = (h2_v, glu_v, dn2_v)[k]
        out = []
        for i in range(4):
            piece = dlands[job][k, (place[k] - i + 4) % 4].astype(F32)[:24]
            at = pl.ds(32 * i, 24)
            if job == 0:
                stage[32 * i:32 * i + 24, :WS] = piece
                skip = 0 if i < 3 else 4 * WS - FF
                src = stage.at[at, pl.ds(skip, WS - skip)]
                dst = (o_gate, o_lift, o_down)[k].at[:, pl.ds(WS * i, WS - skip)]
            else:
                stage[32 * i:32 * i + 24, 1024:1024 + WM] = piece
                src = stage.at[at, pl.ds(1024, WM)]
                dst = o_in.at[k, :, pl.ds(WM * i, WM)] if i < 3 else o_out.at[:, pl.ds(WM * k, WM)]
            out.append(local(src, dst, store_sem.at[job, k, i]))
        return started(out)

    glu_v[...] = jnp.zeros_like(glu_v)
    dn2_v[...] = jnp.zeros_like(dn2_v)

    def swiglu_step(s):
        slot = (s + 1) % 3
        waited(pair_loads(s))
        both = dot_nn(n_v[...], col[slot])
        gate_pre, lift_pre = both[:, :SPAN], both[:, SPAN:]
        hidden_grad = da_v[s]
        sig = jax.nn.sigmoid(gate_pre)
        silu = gate_pre * sig
        hidden = (silu * lift_pre).astype(BF16)
        d_lift = (hidden_grad * silu).astype(BF16)
        d_gate = (hidden_grad * lift_pre * sig * (1.0 + gate_pre * (1.0 - sig))).astype(BF16)
        for i in range(4):
            for k, values in enumerate((d_gate, d_lift, hidden)):
                act[k, i, :, 128 * s:128 * s + 128] = values[:, 128 * i:128 * i + 128]

        def once(values):
            if s < STEPS - 1:
                return values
            return jnp.concatenate([values[:, :256], jnp.zeros((BLK, 128), BF16), values[:, 384:]], axis=1)

        waited(down_loads(STEPS + s))
        glu_v[...] += dot_nn(once(hidden), down_ring[(STEPS + s) % 3])
        dn2_v[...] += dot_nt(jnp.concatenate([once(d_gate), once(d_lift)], axis=1), col[slot])
        if s + 3 < STEPS:
            started(pair_loads(s + 3))
            started(down_loads(STEPS + s + 3))

    def left_ready(job, fwd):
        for k in range(3):
            local(m_src.at[0], lefts[job].at[k, :, pl.ds(0, 128)], own_left.at[job, k]).wait()
            waited(fwd[k])

    for s in range(2):
        swiglu_step(s)
    send_right(0, 0)
    swiglu_step(2)
    fwd = [forward_left(0, k) for k in range(3)]
    swiglu_step(3)
    send_right(0, 1)
    left_ready(0, fwd)
    for k in range(3):
        start_b(0, k, 0)
    swiglu_step(4)
    swiglu_step(5)
    send_right(0, 2)
    for k in range(3):
        start_b(0, k, 1)
    for k in range(3):
        pass_on(0, k, 0)
    swiglu_step(6)
    send_right(0, 3)
    started(in_loads)

    xh_send[0] = dn2_v[...].astype(BF16)
    swap_dn2 = cross(xh_send.at[0], xh_recv.at[0], x_send.at[1], x_recv.at[1])
    swap_dn2.start()
    xh_send[1] = glu_v[...].astype(BF16)
    swap_glu = cross(xh_send.at[1], xh_recv.at[1], x_send.at[2], x_recv.at[2])
    swap_glu.start()
    swap_dn2.wait()
    h2 = h2_v[...]
    z2 = h2 * scale_b
    dn2 = xh_send[0].astype(F32) + xh_recv[0].astype(F32)
    glu_term = jnp.sum(dn2 * z2, axis=0, keepdims=True)
    scaled = dn2 * glugain[...]
    glu_v[...] = cot_v[...].astype(F32) + scale_b * (scaled - z2 * jnp.mean(scaled * z2, axis=1, keepdims=True))
    n_v[...] = glu_v[...].astype(BF16)
    dy = dot_nt(n_v[...], out_v[...])
    d_c = (dy * u_v[...]).astype(BF16)
    du = dy * c_v[...]
    v0, v1, v2 = shifted()
    tap_terms = [jnp.sum(du * v, axis=0, keepdims=True) for v in (v0, v1, v2)]
    w1, w2 = tap1 * (du * mask1), tap2 * (du * mask2)
    two = jnp.concatenate([w2[0:1], w1[0:1] + w2[1:2]], axis=0)
    put_halo(heads, two)
    dv = (tap0 * du + jnp.where(rows < 127, pltpu.roll(w1, 127, 0), 0.0)
          + jnp.where(rows < 126, pltpu.roll(w2, 126, 0), 0.0))
    mixed_r[0, :, :HALF] = (dv * x_v[...]).astype(BF16)
    mixed_r[1, :, :HALF] = d_c
    mixed_r[2, :, :HALF] = (dv * b_v[...]).astype(BF16)
    y_out = y_v[...]
    for k in range(3):
        mixed_r[k, :, HALF:] = y_out[:, 256 * k:256 * k + 256]
    share = jnp.concatenate([two, jnp.zeros((14, HALF), F32)], axis=0)
    none = jnp.zeros((16, WM), BF16)
    for n, other in enumerate((ex_v, eb_v)):
        er_src[n] = jnp.concatenate([(share * other[...]).astype(BF16), none], axis=1)
    send_right(1, 0)
    for n in range(2):
        started(edge_own(n))
        started(edge_left_links(n))
        started(edge_right_links(n))
    m_src[1] = n_v[...].T
    for k in range(3):
        send_left_m(k, 1)
        local(m_src.at[jnp.where(place[k] == 3, 1, 0)], m_left.at[k, :, pl.ds(0, 128)], own_left.at[1, k]).start()
    halo = started(halo_links(heads, 1, 0))
    swap_glu.wait()
    xh_send[1] = (h2_v[...] + (xh_send[1].astype(F32) + xh_recv[1].astype(F32))).astype(BF16)
    stores = started([local(xh_send.at[1], o_layer, load_sem.at[5])])
    for k in range(3):
        start_b(0, k, 2)
    for k in range(3):
        pass_on(0, k, 1)
    waited(halo)
    halo = started(halo_links(heads, 1, 1))
    for k in range(3):
        start_b(0, k, 3)
    for k in range(3):
        pass_on(0, k, 2)

    waited(in_loads)
    for k in range(3):
        part = dot_nt(mixed_r[k, :, :HALF], col[k, :, :HALF])
        if k == 0:
            dn2_v[...] = part
        else:
            dn2_v[...] += part
    waited(halo)
    halo = started(halo_links(heads, 1, 2))
    fwd = [forward_left(1, k) for k in range(3)]
    left_ready(1, fwd)
    for k in range(3):
        start_b(1, k, 0)
    for k in range(3):
        pass_on(0, k, 3)
    for k in range(3):
        start_c(0, k, 0)
    waited(halo)
    incoming = jnp.concatenate([jnp.zeros((14, HALF), F32), halo_rows(heads, after) * has_after], axis=0)
    extra = dot_nt((incoming * x_v[BLK - 16:, :]).astype(BF16), col[0, :, :HALF])
    extra += dot_nt((incoming * b_v[BLK - 16:, :]).astype(BF16), col[2, :, :HALF])
    dn2_v[BLK - 16:, :] += extra
    xh_send[0] = dn2_v[...].astype(BF16)
    swap = cross(xh_send.at[0], xh_recv.at[0], x_send.at[3], x_recv.at[3])
    swap.start()
    for k in range(3):
        pass_on(1, k, 0)
    for k in range(3):
        start_c(0, k, 1)
    swap.wait()
    dn1 = xh_send[0].astype(F32) + xh_recv[0].astype(F32)
    z1 = tok_v[...].astype(F32) * scale_a
    mix_term = jnp.sum(dn1 * z1, axis=0, keepdims=True)
    scaled = dn1 * mixgain[...]
    xh_send[0] = (glu_v[...] + scale_a * (scaled - z1 * jnp.mean(scaled * z1, axis=1, keepdims=True))).astype(BF16)
    stores += started([local(xh_send.at[0], o_input, load_sem.at[6])])

    def my_half(row):
        return jnp.where(core == 0, row[:, :HALF], row[:, HALF:])

    def gain_links(axis):
        view = gain_land.at[axis, place[axis]]
        return [link(view, view, gain_send.at[axis, step - 1], gain_recv.at[axis, step - 1], axis, step) for step in range(1, 4)]

    def gain_sum(axis):
        return (gain_land[axis, 0] + gain_land[axis, 1]) + (gain_land[axis, 2] + gain_land[axis, 3])

    gain_land[0, place[0]] = jnp.concatenate(
        [my_half(mix_term), my_half(glu_term), *tap_terms, jnp.zeros((3, HALF), F32)], axis=0)
    gains = started(gain_links(0))
    for k in range(3):
        start_c(0, k, 2)
    waited(gains)
    gain_land[1, place[1]] = gain_sum(0)
    gains = started(gain_links(1))
    for k in range(3):
        start_c(0, k, 3)
    for k in range(3):
        start_c(1, k, 0)
    waited(gains)
    gain_land[2, place[2]] = gain_sum(1)
    gains = started(gain_links(2))
    for k in range(3):
        start_d(0, k)
    waited(gains)
    v_v[0:8, :] = gain_sum(2)
    stores += started([local(v_v.at[pl.ds(0, 8), :], o_gains, load_sem.at[7])])
    for k in range(3):
        start_d(1, k)
    for job in range(2):
        for k in range(3):
            stores += finish(job, k)
    waited(stores)


def run_layer(seq_lengths, block_slots, mixgain, glugain, taps, tokens, cotangent, inproj, outproj, gate_w, lift_w, down_w):
    vm = pl.BlockSpec(memory_space=pltpu.VMEM)
    sm = pl.BlockSpec(memory_space=pltpu.SMEM)
    hbm = pl.BlockSpec(memory_space=pl.ANY)
    dma = pltpu.SemaphoreType.DMA
    shape = jax.ShapeDtypeStruct
    row, full16, full32, half32 = (
        pltpu.VMEM((1, D), F32), pltpu.VMEM((BLK, D), BF16), pltpu.VMEM((BLK, D), F32), pltpu.VMEM((BLK, HALF), F32))
    return pl.pallas_call(
        layer_kernel,
        out_shape=[shape((BLK, D), BF16), shape((BLK, D), BF16), shape((8, HALF), F32)]
        + [shape(s, F32) for s in ((24, FF), (24, FF), (24, FF), (3, 24, HALF), (24, HALF))],
        in_specs=[sm, sm, hbm, hbm, vm] + [hbm] * 7,
        out_specs=[hbm] * 8,
        scratch_shapes=[
            row, row, full16, full16, full16,
            half32, half32, half32, half32, half32, pltpu.VMEM((BLK, HALF), BF16),
            full32, full32, full32,
            pltpu.VMEM((3, D, 2 * SPAN), BF16), pltpu.VMEM((3, SPAN, D), BF16), pltpu.VMEM((HALF, D), BF16),
            pltpu.VMEM((STEPS, BLK, SPAN), F32), pltpu.VMEM((3, 4, BLK, WS), BF16), pltpu.VMEM((3, BLK, 4 * WM), BF16),
            pltpu.VMEM((2, D, BLK), BF16), pltpu.VMEM((2, D, BLK), BF16),
            pltpu.VMEM((16, D), BF16), pltpu.VMEM((16, HALF), F32), pltpu.VMEM((16, HALF), F32),
            pltpu.VMEM((2, 16, 4 * WM), BF16), pltpu.VMEM((2, 64, D), BF16), pltpu.VMEM((2, 64, WM), BF16),
            pltpu.VMEM((2, BLK, D), BF16), pltpu.VMEM((2, BLK, D), BF16),
            pltpu.VMEM((3, 4, 4, 4, 2, 512), F32), pltpu.VMEM((3, 4, 4, 4, 2, 256), F32),
            pltpu.VMEM((3, 4, 8, HALF), F32),
            pltpu.VMEM((3, D, 512), BF16), pltpu.VMEM((3, 512, WS), BF16), pltpu.VMEM((3, 4, 384, WS), BF16),
            pltpu.VMEM((3, 3, 384, WS), BF16), pltpu.VMEM((3, 3, 96, WS), BF16),
            pltpu.VMEM((3, 4, 32, WS), BF16), pltpu.VMEM((3, 4, 32, WS), BF16),
            pltpu.VMEM((3, D, 512), BF16), pltpu.VMEM((3, 512, WM), BF16),
            pltpu.VMEM((3, 4, 32, WM), BF16), pltpu.VMEM((3, 4, 32, WM), BF16),
            dma((8,)), dma((3, 8)), dma((3, 4)), dma((2, 3, 4)), dma((4,)), dma((4,)),
            dma((2, 3, 3, 3)), dma((2, 3, 3, 3)), dma((3, 3)), dma((3, 3)),
        ]
        + [dma((2, 3, 3))] * 4 + [dma((2, 3, 4, 3))] * 2 + [dma((2, 3, 4, 6))] * 2 + [dma((2, 3, 4, 3))] * 2 + [dma((2, 3, 3))] * 2
        + [dma((2, 3)), dma((2, 3, 4)), dma((2, 2, 3)), dma((2, 2, 3)), dma((2, 2))],
        compiler_params=pltpu.CompilerParams(collective_id=1, has_side_effects=True, vmem_limit_bytes=LIMIT),
        name="layer",
    )(seq_lengths, block_slots, mixgain, glugain, taps, tokens, cotangent, inproj, outproj, gate_w, lift_w, down_w)


def place_kernel(*refs):
    ins, outs, held, in_sems, out_sems = refs[:8], refs[8:18], refs[18:26], refs[26], refs[27]
    loads = [pltpu.make_async_copy(a, b, in_sems.at[i]) for i, (a, b) in enumerate(zip(ins, held))]
    for c in loads:
        c.start()
    gains = held[2]
    parts = [held[0], held[1], gains.at[0], gains.at[1], gains.at[pl.ds(2, 3)], *held[3:]]
    stores = []
    for i, (a, b) in enumerate(zip(parts, outs)):
        if i not in (3, 4):
            loads[i if i < 3 else i - 2].wait()
        stores.append(pltpu.make_async_copy(a, b, out_sems.at[i]))
        stores[-1].start()
    for c in stores:
        c.wait()


def place_outputs(results):
    hbm = pl.BlockSpec(memory_space=pl.ANY)
    shape = jax.ShapeDtypeStruct
    return pl.pallas_call(
        place_kernel,
        out_shape=[shape((BLK, D), BF16), shape((BLK, D), BF16), shape((HALF,), F32), shape((HALF,), F32), shape((3, HALF), F32)]
        + [shape(s, F32) for s in ((24, FF), (24, FF), (24, FF), (3, 24, HALF), (24, HALF))],
        in_specs=[hbm] * 8,
        out_specs=[hbm] * 10,
        scratch_shapes=[pltpu.VMEM(r.shape, r.dtype) for r in results] + [pltpu.SemaphoreType.DMA((8,)), pltpu.SemaphoreType.DMA((10,))],
        name="place",
    )(*results)


def on_device(
    tokens, cotangent, seq_lengths, block_slots, mixgain, inproj, conv_taps, outproj, glugain, gate_weight, lift_weight, down_weight
):
    results = run_layer(
        seq_lengths, block_slots, mixgain, glugain, conv_taps,
        tokens, cotangent, inproj, outproj, gate_weight, lift_weight, down_weight,
    )
    layer_out, input_grad, mixgain_grad, glugain_grad, taps_grad, gate_grad, lift_grad, down_rows, inproj_grad, out_rows = place_outputs(results)
    return (
        layer_out, input_grad, mixgain_grad, inproj_grad, taps_grad, out_rows.T, glugain_grad, gate_grad, lift_grad, down_rows.T,
    )


def solution(mesh):
    in_specs = (
        P("seq", None), P("seq", None), P(), P(), P(), P(None, None, "ch"), P(None, "ch"), P("ch", None),
        P(), P(None, "ch"), P(None, "ch"), P("ch", None),
    )
    out_specs = (
        P("seq", None), P("seq", None), P("ch"), P(None, "seq", "ch"), P(None, "ch"), P("ch", "seq"),
        P("ch"), P("seq", "ch"), P("seq", "ch"), P("ch", "seq"),
    )
    return jax.shard_map(on_device, mesh=mesh, in_specs=in_specs, out_specs=out_specs, check_vma=False)
```

```python
import jax
import jax.numpy as jnp
from jax import lax
from jax.experimental import pallas as pl
from jax.experimental.pallas import tpu as pltpu
from jax.sharding import PartitionSpec as P

MESH = pl.DeviceIdType.MESH
F32, BF16 = jnp.float32, jnp.bfloat16
BLK, D, HALF, FF = 128, 1536, 768, 3456
WS, WM = 896, 256
STEPS, SPAN = 7, 512
EPS = 1e-05
LIMIT = 64 * 1024 * 1024 - 256 * 1024
ROUTES = ((2, 1, 0), (0, 2, 1), (1, 0, 2))
GROUPS = ((0, 256), (256, 256), (512, 256), (768, 128))


def dot_nt(a, b):
    return lax.dot_general(a, b, (((1,), (1,)), ((), ())), preferred_element_type=F32)


def outer(a, b):
    return lax.dot_general(a, b, (((0,), (0,)), ((), ())), preferred_element_type=F32)


def dot_nn(a, b):
    return jnp.dot(a, b, preferred_element_type=F32)


def block_of(i, s):
    return min(7 * i, 20) + s


def layer_kernel(
    seq_lengths, block_slots, mixgain_1d, glugain_1d, taps,
    tokens, cotangent, inproj, outproj, gate_w, lift_w, down_w,
    o_layer, o_input, o_gains, o_gate, o_lift, o_down, o_in, o_out,
    mixgain, glugain, tok_v, cot_v, n_v, b_v, c_v, x_v, v_v, u_v, y_v, h2_v, glu_v, dn2_v,
    col, down_ring, out_v, da_v, act, mixed_r, s_src, m_src, e_src, eb_v, ex_v, er_src, e_left, e_right, xh_send, xh_recv, tails, heads, gain_land,
    s_left, s_right, s_bsend, s_bland, s_cland, s_dsend, s_dland, m_left, m_right, m_dsend, m_dland,
    load_sem, col_sem, down_sem, store_sem, x_send, x_recv, halo_send, halo_recv, gain_send, gain_recv,
    l_send, l_recv, f_send, f_recv, r_send, r_recv,
    b_send, b_recv, c_send, c_recv, d_send, d_recv, own_left, own_right, e_send, e_recv, own_edge,
):
    seq, core = lax.axis_index("seq"), lax.axis_index("ch")
    place = (seq // 16, (seq // 4) % 4, seq % 4)

    def peer(axis, step):
        at = [(place[i] + step) % 4 if i == axis else place[i] for i in range(3)]
        return at[0] * 16 + at[1] * 4 + at[2]

    def local(src, dst, sem):
        return pltpu.make_async_copy(src, dst, sem)

    def link(src, dst, send, recv, axis, step):
        return pltpu.make_async_remote_copy(
            src_ref=src, dst_ref=dst, send_sem=send, recv_sem=recv,
            device_id=(peer(axis, step), core), device_id_type=MESH)

    def cross(src, dst, send, recv):
        return pltpu.make_async_remote_copy(
            src_ref=src, dst_ref=dst, send_sem=send, recv_sem=recv,
            device_id=(seq, 1 - core), device_id_type=MESH)

    def started(copies):
        for c in copies:
            c.start()
        return copies

    def waited(copies):
        for c in copies:
            c.wait()

    def all_of(view, sem):
        local(view, view, sem).wait()

    def all_links(view, send, recv):
        link(view, view, send, recv, 0, 1).wait()

    tok_load = local(tokens, tok_v, load_sem.at[0])
    cot_load = local(cotangent, cot_v, load_sem.at[1])
    out_load = local(outproj, out_v, load_sem.at[2])
    gain_loads = [local(mixgain_1d, mixgain.at[0], load_sem.at[3]), local(glugain_1d, glugain.at[0], load_sem.at[4])]
    in_loads = [local(inproj.at[k], col.at[k, :, pl.ds(0, HALF)], col_sem.at[3 + k]) for k in range(3)]
    tok_load.start()
    started(gain_loads)
    in_loads[0].start()
    in_loads[2].start()
    in_loads[1].start()

    def pair_loads(s):
        slot = (s + 1) % 3
        out = []
        for m, w in enumerate((gate_w, lift_w)):
            for i in range(4):
                lanes = pl.ds(128 * block_of(i, s), 128)
                out.append(local(w.at[:, lanes], col.at[slot, :, pl.ds(SPAN * m + 128 * i, 128)], col_sem.at[slot]))
        return out

    def down_loads(t):
        s, slot = t % STEPS, t % 3
        return [
            local(down_w.at[pl.ds(128 * block_of(i, s), 128), :], down_ring.at[slot, pl.ds(128 * i, 128), :], down_sem.at[slot])
            for i in range(4)]

    def pair_ready(s):
        all_of(col.at[(s + 1) % 3], col_sem.at[(s + 1) % 3])

    def down_ready(t):
        all_of(down_ring.at[t % 3], down_sem.at[t % 3])

    barrier = pltpu.get_barrier_semaphore()
    for axis in range(3):
        for step in range(1, 4):
            pl.semaphore_signal(barrier, inc=1, device_id=(peer(axis, step), core), device_id_type=MESH)
    pl.semaphore_signal(barrier, inc=1, device_id=(seq, 1 - core), device_id_type=MESH)

    block = jnp.int32(0)
    for i in range(64):
        block = jnp.where(block_slots[i] == seq, i, block)
    before = block_slots[jnp.maximum(block - 1, 0)]
    after = block_slots[jnp.minimum(block + 1, 63)]
    has_after = (block < 63).astype(F32)
    rows = lax.broadcasted_iota(jnp.int32, (BLK, 1), 0)
    positions = block * BLK + rows
    start = jnp.zeros((BLK, 1), jnp.int32)
    offset = jnp.int32(0)
    for i in range(4):
        start = jnp.where(offset <= positions, offset, start)
        offset = offset + seq_lengths[i]
    mask1 = (positions - 1 >= start).astype(F32)
    mask2 = (positions - 2 >= start).astype(F32)

    def halo_links(land, job, phase):
        out = []
        for k in range(3):
            where = [pl.ds(0, 4) if axis in ROUTES[k][:phase] else pl.ds(place[axis], 1) for axis in range(3)]
            view = land.at[k, where[0], where[1], where[2]]
            axis = ROUTES[k][phase]
            for step in range(1, 4):
                out.append(link(view, view, halo_send.at[job, phase], halo_recv.at[job, phase], axis, step))
        return out

    def halo_ready(land, job, phase):
        view = (land.at[:, pl.ds(0, 3), 0, 0], land.at[:, pl.ds(0, 3), :, 0], land.at[:, pl.ds(0, 3)])[phase]
        all_links(view, halo_send.at[job, phase], halo_recv.at[job, phase])

    def halo_rows(land, slot):
        at = (slot // 16, (slot // 4) % 4, slot % 4)
        return jnp.concatenate([land[k, at[0], at[1], at[2]] for k in range(3)], axis=1)

    def put_halo(land, two):
        width = two.shape[1] // 3
        for k in range(3):
            land[k, place[0], place[1], place[2]] = two[:, width * k:width * k + width]

    def first_norm(values):
        scale = lax.rsqrt(jnp.mean(values * values, axis=1, keepdims=True) + EPS)
        return scale, values * scale * mixgain[...]

    tok_load.wait()
    put_halo(tails, tok_v[BLK - 16:BLK, :].astype(F32)[14:16])
    pl.semaphore_wait(barrier, 10)
    started(halo_links(tails, 0, 0))
    waited(gain_loads)
    scale_a, n1 = first_norm(tok_v[...].astype(F32))
    n_v[...] = n1.astype(BF16)
    in_loads[0].wait()
    b_v[...] = dot_nn(n_v[...], col[0, :, :HALF])
    started([cot_load])
    for s in range(3):
        started(down_loads(s))
    halo_ready(tails, 0, 0)
    started(halo_links(tails, 0, 1))
    in_loads[2].wait()
    x_v[...] = dot_nn(n_v[...], col[2, :, :HALF])
    v_v[...] = (b_v[...] * x_v[...]).astype(BF16).astype(F32)
    in_loads[1].wait()
    c_v[...] = dot_nn(n_v[...], col[1, :, :HALF])
    started(pair_loads(0))
    cot_load.wait()

    def hidden_grads(first, end):
        for s in range(first, end):
            down_ready(s)
            da_v[s] = dot_nt(cot_v[...], down_ring[s % 3])
            started(down_loads(s + 3))

    halo_ready(tails, 0, 1)
    started(halo_links(tails, 0, 2))
    s_src[1] = cot_v[...].T
    m_src[0] = n_v[...].T

    half = pl.ds(pl.multiple_of(core * HALF, HALF), HALF)

    def left_link(job, k, src, step):
        left = (s_left, m_left)[job]
        return link(src.at[half, :], left.at[k, half, pl.ds(128 * step, 128)],
                    l_send.at[job], l_recv.at[job], k, step)

    def send_left_s(k):
        src = s_src.at[1 if k == 2 else 0]
        local(src, s_left.at[k, :, pl.ds(0, 128)], own_left.at[0]).start()
        for step in range(1, 4):
            left_link(0, k, src, step).start()

    def send_left_m(k, which):
        for step in range(1, 4):
            @pl.when(((place[k] + step) % 4 == 3) == (which == 1))
            def _():
                left_link(1, k, m_src.at[which], step).start()

    def others(job):
        return (s_left, m_left)[job].at[:, half, pl.ds(128, 384)]

    def forward_left(job):
        all_links(others(job), l_send.at[job], l_recv.at[job])
        cross(others(job), others(job), f_send.at[job], f_recv.at[job]).start()

    started([out_load])
    hidden_grads(0, STEPS)

    halo_ready(tails, 0, 2)
    send_left_s(2)
    for k in range(3):
        send_left_m(k, 0)
    last_two = jnp.concatenate([halo_rows(tails, before), jnp.zeros((14, D), F32)], axis=0)
    edge = first_norm(last_two)[1].astype(BF16)
    edge_b, edge_x = dot_nn(edge, col[0, :, :HALF]), dot_nn(edge, col[2, :, :HALF])
    carried = (edge_b * edge_x).astype(BF16).astype(F32)
    e_src[...] = edge
    eb_v[...] = edge_b
    ex_v[...] = edge_x

    def edge_left_links(n):
        return [
            link(e_src, e_left.at[n, pl.ds(16 * step, 16), :], e_send.at[0], e_recv.at[0], 2 * n, step)
            for step in range(1, 4)]

    def edge_piece(n, i):
        return er_src.at[n, :, pl.ds(pl.multiple_of(i * WM, WM), WM)]

    def edge_right_links(n):
        return [
            link(edge_piece(n, (place[2 * n] + step) % 4), e_right.at[n, pl.ds(16 * step, 16), :],
                 e_send.at[1], e_recv.at[1], 2 * n, step)
            for step in range(1, 4)]

    def edge_own(n):
        return [
            local(e_src, e_left.at[n, pl.ds(0, 16), :], own_edge.at[0]),
            local(edge_piece(n, place[2 * n]), e_right.at[n, pl.ds(0, 16), :], own_edge.at[1])]
    for s in range(1, 3):
        started(pair_loads(s))
    row_is0, row_is1 = rows == 0, rows == 1
    tap0, tap1, tap2 = taps[0:1, :], taps[1:2, :], taps[2:3, :]

    def shifted():
        v = v_v[...]
        one = jnp.where(row_is0, carried[1:2], pltpu.roll(v, 1, 0)) * mask1
        two = jnp.where(row_is0, carried[0:1], jnp.where(row_is1, carried[1:2], pltpu.roll(v, 2, 0))) * mask2
        return v, one, two

    v0, v1, v2 = shifted()
    u_v[...] = tap0 * v0 + tap1 * v1 + tap2 * v2
    y_v[...] = (c_v[...] * u_v[...]).astype(BF16)
    out_load.wait()
    dn2_v[...] = dot_nn(y_v[...], out_v[...])
    swap = cross(dn2_v, h2_v, x_send.at[0], x_recv.at[0])
    swap.start()
    swap.wait()
    h2_v[...] = tok_v[...].astype(F32) + (dn2_v[...] + h2_v[...])
    h2 = h2_v[...]
    scale_b = lax.rsqrt(jnp.mean(h2 * h2, axis=1, keepdims=True) + EPS)
    n_v[...] = (h2 * scale_b * glugain[...]).astype(BF16)
    s_src[0] = n_v[...].T
    send_left_s(0)
    send_left_s(1)

    lefts, rights, dsends, dlands = (s_left, m_left), (s_right, m_right), (s_dsend, m_dsend), (s_dland, m_dland)

    def right_piece(job, k, i, g):
        if job == 0:
            return act.at[k, i, :, pl.ds(*GROUPS[g])]
        return mixed_r.at[k, :, pl.ds(pl.multiple_of(i * WM, WM), WM)]

    def right_links(job, k, g):
        lanes = pl.ds(*GROUPS[g])
        return [
            link(right_piece(job, k, (place[k] + step) % 4, g), rights[job].at[k, pl.ds(128 * step, 128), lanes],
                 r_send.at[4 * job + g], r_recv.at[4 * job + g], k, step)
            for step in range(1, 4)]

    def right_own(job, k, g):
        return local(right_piece(job, k, place[k], g), rights[job].at[k, pl.ds(0, 128), pl.ds(*GROUPS[g])], own_right.at[4 * job + g])

    def send_right(job, g):
        for k in range(3):
            right_own(job, k, g).start()
            started(right_links(job, k, g))

    def b_out(job, k, j, g, row=0, count=384):
        lanes = pl.ds(*GROUPS[g])
        if job == 0:
            return s_bsend.at[k, j, pl.ds(row, count), lanes]
        return col.at[1, pl.ds(pl.multiple_of(384 * j + row, 96), count), pl.ds(WM * k, WM)]

    def b_in(job, k, i, g, row=0, count=384):
        if job == 0:
            return s_bland.at[k, i, pl.ds(row, count), pl.ds(*GROUPS[g])]
        return down_ring.at[i, pl.ds(row, count), pl.ds(WM * k, WM)]

    def c_out(job, k, j, g, row=0, count=96):
        return rights[job].at[k, pl.ds(pl.multiple_of(96 * j + row, 48), count), pl.ds(*GROUPS[g])]

    def c_in(job, k, i, g):
        if job == 0:
            return s_cland.at[k, i, :, pl.ds(*GROUPS[g])]
        return down_ring.at[i, pl.ds(0, 96), pl.ds(HALF + WM * k, WM)]

    LOW, HIGH = 0, 192

    def b_links(job, k, g, which):
        axis = (k + 1) % 3
        me = place[axis]
        opposite, ahead, behind = (me + 2) % 4, (me + 1) % 4, (me + 3) % 4
        table = (
            (opposite, LOW, 2, 1), (ahead, HIGH, 0, 1), (opposite, HIGH, 2, 3),
            (behind, LOW, 1, 3), (ahead, LOW, 0, 1), (behind, HIGH, 1, 3))
        out = []
        for n in which:
            part, row, land, step = table[n]
            sem = 2 * (4 * job + g) + (land != 2)
            out.append(link(b_out(job, k, part, g, row, 192), b_in(job, k, land, g, row, 192),
                            b_send.at[sem], b_recv.at[sem], axis, step))
        return out

    def c_links(job, k, g):
        axis = (k + 2) % 3
        return [
            link(c_out(job, k, (place[axis] + step) % 4, g), c_in(job, k, step - 1, g),
                 c_send.at[4 * job + g], c_recv.at[4 * job + g], axis, step)
            for step in range(1, 4)]

    def right_ready(job, g):
        lanes, n = pl.ds(*GROUPS[g]), 4 * job + g
        all_of(rights[job].at[:, pl.ds(0, 128), lanes], own_right.at[n])
        all_links(rights[job].at[:, pl.ds(128, 384), lanes], r_send.at[n], r_recv.at[n])

    def edges_ready():
        all_of(e_left.at[:, pl.ds(0, 16), :], own_edge.at[0])
        all_of(e_right.at[:, pl.ds(0, 16), :], own_edge.at[1])
        all_links(e_left.at[:, pl.ds(16, 48), :], e_send.at[0], e_recv.at[0])
        all_links(e_right.at[:, pl.ds(16, 48), :], e_send.at[1], e_recv.at[1])

    def start_b(job, k, g):
        lanes = pl.ds(*GROUPS[g])
        edges = job == 1 and k != 1

        def slab(x, carry):
            at = pl.ds(pl.multiple_of(x * HALF, HALF), HALF)
            acc = dot_nn(lefts[job][k, at, :], rights[job][k, :, lanes])
            if edges:
                acc = acc + outer(e_left[k // 2, :, at], e_right[k // 2])
            for h in range(2):
                row = pl.multiple_of(192 * x + 96 * h, 96)
                for j in range(4):
                    base = 384 * h + 96 * j
                    if k == 0:
                        b_out(job, k, j, g, row, 96)[...] = acc[base:base + 96].astype(BF16)
                    elif k == 1:
                        parts = [acc[384 * h + 96 * y + 24 * j:384 * h + 96 * y + 24 * j + 24] for y in range(4)]
                        b_out(job, k, j, g, row, 96)[...] = jnp.concatenate(parts, axis=0).astype(BF16)
                    else:
                        b_out(job, k, 2 * x + h, g, 96 * j, 96)[...] = acc[base:base + 96].astype(BF16)
            return carry

        lax.fori_loop(0, 2, slab, 0)
        started(b_links(job, k, g, range(4)))

    def b_ready(job, g, last):
        sem = 2 * (4 * job + g) + last
        if job == 0:
            view = s_bland.at[:, pl.ds(0, 2) if last else pl.ds(2, 1), :, pl.ds(*GROUPS[g])]
        else:
            view = down_ring.at[pl.ds(0, 2) if last else pl.ds(2, 1), pl.ds(0, 384), pl.ds(0, HALF)]
        all_links(view, b_send.at[sem], b_recv.at[sem])

    def pass_on(job, k, g):
        me = place[(k + 1) % 3]
        for step, row in ((1, LOW), (3, HIGH)):
            own, via = b_out(job, k, (me + step) % 4, g, row, 192), b_in(job, k, 2, g, row, 192)
            own[...] = (own[...].astype(F32) + via[...].astype(F32)).astype(BF16)
        started(b_links(job, k, g, (4, 5)))

    def c_ready(job, g):
        if job == 0:
            view = s_cland.at[:, :, :, pl.ds(*GROUPS[g])]
        else:
            view = down_ring.at[:, pl.ds(0, 96), pl.ds(HALF, HALF)]
        all_links(view, c_send.at[4 * job + g], c_recv.at[4 * job + g])

    def start_c(job, k, g):
        me = place[(k + 1) % 3]

        def summed(q):
            total = b_out(job, k, me, g, 96 * q, 96)[...].astype(F32)
            for i in range(2):
                total = total + b_in(job, k, i, g, 96 * q, 96)[...].astype(F32)
            return total

        if k == 0:
            for p in range(2):
                a, b = summed(2 * p), summed(2 * p + 1)
                for j in range(4):
                    both = jnp.concatenate([a[24 * j:24 * j + 24], b[24 * j:24 * j + 24]], axis=0)
                    c_out(job, k, j, g, 48 * p, 48)[...] = both.astype(BF16)
        else:
            for q in range(4):
                c_out(job, k, q, g)[...] = summed(q).astype(BF16)
        started(c_links(job, k, g))

    def d_links(job, k):
        return [
            link(dsends[job].at[k, (place[k] + step) % 4], dlands[job].at[k, step],
                 d_send.at[job], d_recv.at[job], k, step)
            for step in range(1, 4)]

    def start_d(job, k):
        dsend, dland = dsends[job], dlands[job]
        for g in range(4 if job == 0 else 1):
            first, width = GROUPS[g]
            total = c_out(job, k, place[(k + 2) % 3], g)[...].astype(F32)
            for i in range(3):
                total = total + c_in(job, k, i, g)[...].astype(F32)
            pad = jnp.zeros((8, width), F32)
            for j in range(4):
                dsend[k, j, :, first:first + width] = jnp.concatenate([total[24 * j:24 * j + 24], pad], axis=0).astype(BF16)
        dland[k, 0] = dsend[k, place[k]]
        started(d_links(job, k))

    def finish(job, k):
        stage = (h2_v, glu_v, dn2_v)[k]
        for i in range(4):
            piece = dlands[job][k, (place[k] - i + 4) % 4].astype(F32)[:24]
            at = pl.ds(32 * i, 24)
            if job == 0:
                stage[32 * i:32 * i + 24, :WS] = piece
                skip = 0 if i < 3 else 4 * WS - FF
                src = stage.at[at, pl.ds(skip, WS - skip)]
                dst = (o_gate, o_lift, o_down)[k].at[:, pl.ds(WS * i, WS - skip)]
            else:
                stage[32 * i:32 * i + 24, 1024:1024 + WM] = piece
                src = stage.at[at, pl.ds(1024, WM)]
                dst = o_in.at[k, :, pl.ds(WM * i, WM)] if i < 3 else o_out.at[:, pl.ds(WM * k, WM)]
            local(src, dst, store_sem.at[k if job == 0 else 3 + (i == 3)]).start()

    glu_v[...] = jnp.zeros_like(glu_v)
    dn2_v[...] = jnp.zeros_like(dn2_v)

    def swiglu_step(s):
        slot = (s + 1) % 3
        pair_ready(s)
        both = dot_nn(n_v[...], col[slot])
        gate_pre, lift_pre = both[:, :SPAN], both[:, SPAN:]
        hidden_grad = da_v[s]
        sig = jax.nn.sigmoid(gate_pre)
        silu = gate_pre * sig
        hidden = (silu * lift_pre).astype(BF16)
        d_lift = (hidden_grad * silu).astype(BF16)
        d_gate = (hidden_grad * lift_pre * sig * (1.0 + gate_pre * (1.0 - sig))).astype(BF16)
        for i in range(4):
            for k, values in enumerate((d_gate, d_lift, hidden)):
                act[k, i, :, 128 * s:128 * s + 128] = values[:, 128 * i:128 * i + 128]

        def once(values):
            if s < STEPS - 1:
                return values
            return jnp.concatenate([values[:, :256], jnp.zeros((BLK, 128), BF16), values[:, 384:]], axis=1)

        down_ready(STEPS + s)
        glu_v[...] += dot_nn(once(hidden), down_ring[(STEPS + s) % 3])
        dn2_v[...] += dot_nt(jnp.concatenate([once(d_gate), once(d_lift)], axis=1), col[slot])
        if s + 3 < STEPS:
            started(pair_loads(s + 3))
            started(down_loads(STEPS + s + 3))

    def left_ready(job):
        all_of(lefts[job].at[:, :, pl.ds(0, 128)], own_left.at[job])
        cross(others(job), others(job), f_send.at[job], f_recv.at[job]).wait()

    for s in range(2):
        swiglu_step(s)
    send_right(0, 0)
    swiglu_step(2)
    forward_left(0)
    swiglu_step(3)
    send_right(0, 1)
    left_ready(0)
    right_ready(0, 0)
    for k in range(3):
        start_b(0, k, 0)
    swiglu_step(4)
    swiglu_step(5)
    send_right(0, 2)
    right_ready(0, 1)
    for k in range(3):
        start_b(0, k, 1)
    b_ready(0, 0, 0)
    for k in range(3):
        pass_on(0, k, 0)
    swiglu_step(6)
    send_right(0, 3)
    started(in_loads)

    xh_send[0] = dn2_v[...].astype(BF16)
    swap_dn2 = cross(xh_send.at[0], xh_recv.at[0], x_send.at[1], x_recv.at[1])
    swap_dn2.start()
    xh_send[1] = glu_v[...].astype(BF16)
    swap_glu = cross(xh_send.at[1], xh_recv.at[1], x_send.at[2], x_recv.at[2])
    swap_glu.start()
    swap_dn2.wait()
    h2 = h2_v[...]
    z2 = h2 * scale_b
    dn2 = xh_send[0].astype(F32) + xh_recv[0].astype(F32)
    glu_term = jnp.sum(dn2 * z2, axis=0, keepdims=True)
    scaled = dn2 * glugain[...]
    glu_v[...] = cot_v[...].astype(F32) + scale_b * (scaled - z2 * jnp.mean(scaled * z2, axis=1, keepdims=True))
    n_v[...] = glu_v[...].astype(BF16)
    dy = dot_nt(n_v[...], out_v[...])
    d_c = (dy * u_v[...]).astype(BF16)
    du = dy * c_v[...]
    v0, v1, v2 = shifted()
    tap_terms = [jnp.sum(du * v, axis=0, keepdims=True) for v in (v0, v1, v2)]
    w1, w2 = tap1 * (du * mask1), tap2 * (du * mask2)
    two = jnp.concatenate([w2[0:1], w1[0:1] + w2[1:2]], axis=0)
    put_halo(heads, two)
    dv = (tap0 * du + jnp.where(rows < 127, pltpu.roll(w1, 127, 0), 0.0)
          + jnp.where(rows < 126, pltpu.roll(w2, 126, 0), 0.0))
    mixed_r[0, :, :HALF] = (dv * x_v[...]).astype(BF16)
    mixed_r[1, :, :HALF] = d_c
    mixed_r[2, :, :HALF] = (dv * b_v[...]).astype(BF16)
    y_out = y_v[...]
    for k in range(3):
        mixed_r[k, :, HALF:] = y_out[:, 256 * k:256 * k + 256]
    share = jnp.concatenate([two, jnp.zeros((14, HALF), F32)], axis=0)
    none = jnp.zeros((16, WM), BF16)
    for n, other in enumerate((ex_v, eb_v)):
        er_src[n] = jnp.concatenate([(share * other[...]).astype(BF16), none], axis=1)
    send_right(1, 0)
    for n in range(2):
        started(edge_own(n))
        started(edge_left_links(n))
        started(edge_right_links(n))
    m_src[1] = n_v[...].T
    for k in range(3):
        send_left_m(k, 1)
        local(m_src.at[jnp.where(place[k] == 3, 1, 0)], m_left.at[k, :, pl.ds(0, 128)], own_left.at[1]).start()
    started(halo_links(heads, 1, 0))
    swap_glu.wait()
    xh_send[1] = (h2_v[...] + (xh_send[1].astype(F32) + xh_recv[1].astype(F32))).astype(BF16)
    stores = started([local(xh_send.at[1], o_layer, load_sem.at[5])])
    right_ready(0, 2)
    for k in range(3):
        start_b(0, k, 2)
    b_ready(0, 1, 0)
    for k in range(3):
        pass_on(0, k, 1)
    halo_ready(heads, 1, 0)
    started(halo_links(heads, 1, 1))
    right_ready(0, 3)
    for k in range(3):
        start_b(0, k, 3)
    b_ready(0, 2, 0)
    for k in range(3):
        pass_on(0, k, 2)

    waited(in_loads)
    for k in range(3):
        part = dot_nt(mixed_r[k, :, :HALF], col[k, :, :HALF])
        if k == 0:
            dn2_v[...] = part
        else:
            dn2_v[...] += part
    halo_ready(heads, 1, 1)
    started(halo_links(heads, 1, 2))
    forward_left(1)
    left_ready(1)
    right_ready(1, 0)
    edges_ready()
    for k in range(3):
        start_b(1, k, 0)
    b_ready(0, 3, 0)
    for k in range(3):
        pass_on(0, k, 3)
    b_ready(0, 0, 1)
    for k in range(3):
        start_c(0, k, 0)
    halo_ready(heads, 1, 2)
    incoming = jnp.concatenate([jnp.zeros((14, HALF), F32), halo_rows(heads, after) * has_after], axis=0)
    extra = dot_nt((incoming * x_v[BLK - 16:, :]).astype(BF16), col[0, :, :HALF])
    extra += dot_nt((incoming * b_v[BLK - 16:, :]).astype(BF16), col[2, :, :HALF])
    dn2_v[BLK - 16:, :] += extra
    xh_send[0] = dn2_v[...].astype(BF16)
    swap = cross(xh_send.at[0], xh_recv.at[0], x_send.at[3], x_recv.at[3])
    swap.start()
    b_ready(1, 0, 0)
    for k in range(3):
        pass_on(1, k, 0)
    b_ready(0, 1, 1)
    for k in range(3):
        start_c(0, k, 1)
    swap.wait()
    dn1 = xh_send[0].astype(F32) + xh_recv[0].astype(F32)
    z1 = tok_v[...].astype(F32) * scale_a
    mix_term = jnp.sum(dn1 * z1, axis=0, keepdims=True)
    scaled = dn1 * mixgain[...]
    xh_send[0] = (glu_v[...] + scale_a * (scaled - z1 * jnp.mean(scaled * z1, axis=1, keepdims=True))).astype(BF16)
    stores += started([local(xh_send.at[0], o_input, load_sem.at[6])])

    def my_half(row):
        return jnp.where(core == 0, row[:, :HALF], row[:, HALF:])

    def gain_links(axis):
        view = gain_land.at[axis, place[axis]]
        return [link(view, view, gain_send.at[axis], gain_recv.at[axis], axis, step) for step in range(1, 4)]

    def gain_sum(axis):
        all_links(gain_land.at[axis, pl.ds(0, 3)], gain_send.at[axis], gain_recv.at[axis])
        return (gain_land[axis, 0] + gain_land[axis, 1]) + (gain_land[axis, 2] + gain_land[axis, 3])

    gain_land[0, place[0]] = jnp.concatenate(
        [my_half(mix_term), my_half(glu_term), *tap_terms, jnp.zeros((3, HALF), F32)], axis=0)
    started(gain_links(0))
    b_ready(0, 2, 1)
    for k in range(3):
        start_c(0, k, 2)
    gain_land[1, place[1]] = gain_sum(0)
    started(gain_links(1))
    b_ready(0, 3, 1)
    for k in range(3):
        start_c(0, k, 3)
    b_ready(1, 0, 1)
    for k in range(3):
        start_c(1, k, 0)
    gain_land[2, place[2]] = gain_sum(1)
    started(gain_links(2))
    for g in range(4):
        c_ready(0, g)
    for k in range(3):
        start_d(0, k)
    v_v[0:8, :] = gain_sum(2)
    stores += started([local(v_v.at[pl.ds(0, 8), :], o_gains, load_sem.at[7])])
    c_ready(1, 0)
    for k in range(3):
        start_d(1, k)
    for job in range(2):
        all_links(dlands[job].at[:, pl.ds(1, 3)], d_send.at[job], d_recv.at[job])
        for k in range(3):
            finish(job, k)
    for n, out in enumerate((o_gate, o_lift, o_down, o_in, o_out)):
        all_of(out, store_sem.at[n])
    waited(stores)


def run_layer(seq_lengths, block_slots, mixgain, glugain, taps, tokens, cotangent, inproj, outproj, gate_w, lift_w, down_w):
    vm = pl.BlockSpec(memory_space=pltpu.VMEM)
    sm = pl.BlockSpec(memory_space=pltpu.SMEM)
    hbm = pl.BlockSpec(memory_space=pl.ANY)
    dma = pltpu.SemaphoreType.DMA
    shape = jax.ShapeDtypeStruct
    row, full16, full32, half32 = (
        pltpu.VMEM((1, D), F32), pltpu.VMEM((BLK, D), BF16), pltpu.VMEM((BLK, D), F32), pltpu.VMEM((BLK, HALF), F32))
    return pl.pallas_call(
        layer_kernel,
        out_shape=[shape((BLK, D), BF16), shape((BLK, D), BF16), shape((8, HALF), F32)]
        + [shape(s, F32) for s in ((24, FF), (24, FF), (24, FF), (3, 24, HALF), (24, HALF))],
        in_specs=[sm, sm, hbm, hbm, vm] + [hbm] * 7,
        out_specs=[hbm] * 8,
        scratch_shapes=[
            row, row, full16, full16, full16,
            half32, half32, half32, half32, half32, pltpu.VMEM((BLK, HALF), BF16),
            full32, full32, full32,
            pltpu.VMEM((3, D, 2 * SPAN), BF16), pltpu.VMEM((3, SPAN, D), BF16), pltpu.VMEM((HALF, D), BF16),
            pltpu.VMEM((STEPS, BLK, SPAN), F32), pltpu.VMEM((3, 4, BLK, WS), BF16), pltpu.VMEM((3, BLK, 4 * WM), BF16),
            pltpu.VMEM((2, D, BLK), BF16), pltpu.VMEM((2, D, BLK), BF16),
            pltpu.VMEM((16, D), BF16), pltpu.VMEM((16, HALF), F32), pltpu.VMEM((16, HALF), F32),
            pltpu.VMEM((2, 16, 4 * WM), BF16), pltpu.VMEM((2, 64, D), BF16), pltpu.VMEM((2, 64, WM), BF16),
            pltpu.VMEM((2, BLK, D), BF16), pltpu.VMEM((2, BLK, D), BF16),
            pltpu.VMEM((3, 4, 4, 4, 2, 512), F32), pltpu.VMEM((3, 4, 4, 4, 2, 256), F32),
            pltpu.VMEM((3, 4, 8, HALF), F32),
            pltpu.VMEM((3, D, 512), BF16), pltpu.VMEM((3, 512, WS), BF16), pltpu.VMEM((3, 4, 384, WS), BF16),
            pltpu.VMEM((3, 3, 384, WS), BF16), pltpu.VMEM((3, 3, 96, WS), BF16),
            pltpu.VMEM((3, 4, 32, WS), BF16), pltpu.VMEM((3, 4, 32, WS), BF16),
            pltpu.VMEM((3, D, 512), BF16), pltpu.VMEM((3, 512, WM), BF16),
            pltpu.VMEM((3, 4, 32, WM), BF16), pltpu.VMEM((3, 4, 32, WM), BF16),
            dma((8,)), dma((6,)), dma((3,)), dma((5,)), dma((4,)), dma((4,)),
            dma((2, 3)), dma((2, 3)), dma((3,)), dma((3,)),
            dma((2,)), dma((2,)), dma((2,)), dma((2,)), dma((5,)), dma((5,)),
            dma((10,)), dma((10,)), dma((5,)), dma((5,)), dma((2,)), dma((2,)),
            dma((2,)), dma((5,)), dma((2,)), dma((2,)), dma((2,)),
        ],
        compiler_params=pltpu.CompilerParams(collective_id=1, has_side_effects=True, vmem_limit_bytes=LIMIT),
        name="layer",
    )(seq_lengths, block_slots, mixgain, glugain, taps, tokens, cotangent, inproj, outproj, gate_w, lift_w, down_w)


def place_kernel(*refs):
    ins, outs, held, in_sems, out_sems = refs[:8], refs[8:18], refs[18:26], refs[26], refs[27]
    loads = [pltpu.make_async_copy(a, b, in_sems.at[i]) for i, (a, b) in enumerate(zip(ins, held))]
    for c in loads:
        c.start()
    gains = held[2]
    parts = [held[0], held[1], gains.at[0], gains.at[1], gains.at[pl.ds(2, 3)], *held[3:]]
    stores = []
    for i, (a, b) in enumerate(zip(parts, outs)):
        if i not in (3, 4):
            loads[i if i < 3 else i - 2].wait()
        stores.append(pltpu.make_async_copy(a, b, out_sems.at[i]))
        stores[-1].start()
    for c in stores:
        c.wait()


def place_outputs(results):
    hbm = pl.BlockSpec(memory_space=pl.ANY)
    shape = jax.ShapeDtypeStruct
    return pl.pallas_call(
        place_kernel,
        out_shape=[shape((BLK, D), BF16), shape((BLK, D), BF16), shape((HALF,), F32), shape((HALF,), F32), shape((3, HALF), F32)]
        + [shape(s, F32) for s in ((24, FF), (24, FF), (24, FF), (3, 24, HALF), (24, HALF))],
        in_specs=[hbm] * 8,
        out_specs=[hbm] * 10,
        scratch_shapes=[pltpu.VMEM(r.shape, r.dtype) for r in results] + [pltpu.SemaphoreType.DMA((8,)), pltpu.SemaphoreType.DMA((10,))],
        name="place",
    )(*results)


def on_device(
    tokens, cotangent, seq_lengths, block_slots, mixgain, inproj, conv_taps, outproj, glugain, gate_weight, lift_weight, down_weight
):
    results = run_layer(
        seq_lengths, block_slots, mixgain, glugain, conv_taps,
        tokens, cotangent, inproj, outproj, gate_weight, lift_weight, down_weight,
    )
    layer_out, input_grad, mixgain_grad, glugain_grad, taps_grad, gate_grad, lift_grad, down_rows, inproj_grad, out_rows = place_outputs(results)
    return (
        layer_out, input_grad, mixgain_grad, inproj_grad, taps_grad, out_rows.T, glugain_grad, gate_grad, lift_grad, down_rows.T,
    )


def solution(mesh):
    in_specs = (
        P("seq", None), P("seq", None), P(), P(), P(), P(None, None, "ch"), P(None, "ch"), P("ch", None),
        P(), P(None, "ch"), P(None, "ch"), P("ch", None),
    )
    out_specs = (
        P("seq", None), P("seq", None), P("ch"), P(None, "seq", "ch"), P(None, "ch"), P("ch", "seq"),
        P("ch"), P("seq", "ch"), P("seq", "ch"), P("ch", "seq"),
    )
    return jax.shard_map(on_device, mesh=mesh, in_specs=in_specs, out_specs=out_specs, check_vma=False)
```

```python
import jax
import jax.numpy as jnp
from jax import lax
from jax.experimental import pallas as pl
from jax.experimental.pallas import tpu as pltpu
from jax.sharding import PartitionSpec as P

MESH = pl.DeviceIdType.MESH
F32, BF16 = jnp.float32, jnp.bfloat16
BLK, D, HALF, FF = 128, 1536, 768, 3456
WS, WM = 896, 256
STEPS, SPAN = 7, 512
EPS = 1e-05
LIMIT = 64 * 1024 * 1024 - 256 * 1024
ROUTES = ((2, 1, 0), (0, 2, 1), (1, 0, 2))
GROUPS = (((0, 256), (256, 256), (512, 256), (768, 128)), ((0, 256),))


def dot_nt(a, b):
    return lax.dot_general(a, b, (((1,), (1,)), ((), ())), preferred_element_type=F32)


def outer(a, b):
    return lax.dot_general(a, b, (((0,), (0,)), ((), ())), preferred_element_type=F32)


def dot_nn(a, b):
    return jnp.dot(a, b, preferred_element_type=F32)


def span(s):
    return min(SPAN, FF - SPAN * s)


def layer_kernel(
    seq_lengths, block_slots, mixgain_1d, glugain_1d, taps,
    tokens, cotangent, inproj, outproj, gate_w, lift_w, down_w,
    o_layer, o_input, o_gains, o_gate, o_lift, o_down, o_in, o_out,
    mixgain, glugain, tok_v, cot_v, n_v, b_v, c_v, x_v, v_v, u_v, y_v, h2_v, glu_v, dn2_v,
    col, down_ring, out_v, da_v, act, mixed_r, s_src, m_src, e_src, eb_v, ex_v, er_src, e_left, e_right, xh_send, xh_recv, xs_send, tails, heads, gain_land,
    s_left, s_right, s_bsend, s_bland, s_cland, s_dsend, s_dland, m_left, m_right, m_dsend, m_dland,
    load_sem, col_sem, down_sem, store_sem, x_send, x_recv, halo_send, halo_recv, gain_send, gain_recv,
    l_send, l_recv, f_send, f_recv, r_send, r_recv,
    b_send, b_recv, c_send, c_recv, d_send, d_recv, e_send, e_recv, own_edge,
):
    seq, core = lax.axis_index("seq"), lax.axis_index("ch")
    place = (seq // 16, (seq // 4) % 4, seq % 4)

    def peer(axis, step):
        at = [(place[i] + step) % 4 if i == axis else place[i] for i in range(3)]
        return at[0] * 16 + at[1] * 4 + at[2]

    def local(src, dst, sem):
        return pltpu.make_async_copy(src, dst, sem)

    def link(src, dst, send, recv, axis, step):
        return pltpu.make_async_remote_copy(
            src_ref=src, dst_ref=dst, send_sem=send, recv_sem=recv,
            device_id=(peer(axis, step), core), device_id_type=MESH)

    def cross(src, dst, send, recv):
        return pltpu.make_async_remote_copy(
            src_ref=src, dst_ref=dst, send_sem=send, recv_sem=recv,
            device_id=(seq, 1 - core), device_id_type=MESH)

    def started(copies):
        for c in copies:
            c.start()
        return copies

    def waited(copies):
        for c in copies:
            c.wait()

    def all_of(view, sem):
        local(view, view, sem).wait()

    def all_links(view, send, recv):
        link(view, view, send, recv, 0, 1).wait()

    tok_load = local(tokens, tok_v, load_sem.at[0])
    cot_load = local(cotangent, cot_v, load_sem.at[1])
    out_load = local(outproj, out_v, load_sem.at[2])
    gain_loads = [local(mixgain_1d, mixgain.at[0], load_sem.at[3]), local(glugain_1d, glugain.at[0], load_sem.at[4])]
    in_loads = [local(inproj.at[k], col.at[k, :, pl.ds(0, HALF)], col_sem.at[3 + k]) for k in range(3)]
    tok_load.start()
    started(gain_loads)
    in_loads[0].start()
    in_loads[2].start()
    in_loads[1].start()

    def pair_loads(s):
        slot, w = (s + 1) % 3, span(s)
        return [
            local(weight.at[:, pl.ds(SPAN * s, w)], col.at[slot, :, pl.ds(w * m, w)], col_sem.at[slot])
            for m, weight in enumerate((gate_w, lift_w))]

    def down_loads(t):
        s, slot = t % STEPS, t % 3
        return [local(down_w.at[pl.ds(SPAN * s, span(s)), :], down_ring.at[slot, pl.ds(0, span(s)), :], down_sem.at[slot])]

    def pair_ready(s):
        all_of(col.at[(s + 1) % 3, :, pl.ds(0, 2 * span(s))], col_sem.at[(s + 1) % 3])

    def down_ready(t):
        all_of(down_ring.at[t % 3, pl.ds(0, span(t % STEPS)), :], down_sem.at[t % 3])

    barrier = pltpu.get_barrier_semaphore()
    for axis in range(3):
        for step in range(1, 4):
            pl.semaphore_signal(barrier, inc=1, device_id=(peer(axis, step), core), device_id_type=MESH)
    pl.semaphore_signal(barrier, inc=1, device_id=(seq, 1 - core), device_id_type=MESH)

    block = jnp.int32(0)
    for i in range(64):
        block = jnp.where(block_slots[i] == seq, i, block)
    before = block_slots[jnp.maximum(block - 1, 0)]
    after = block_slots[jnp.minimum(block + 1, 63)]
    has_after = (block < 63).astype(F32)
    rows = lax.broadcasted_iota(jnp.int32, (BLK, 1), 0)
    positions = block * BLK + rows
    start = jnp.zeros((BLK, 1), jnp.int32)
    offset = jnp.int32(0)
    for i in range(4):
        start = jnp.where(offset <= positions, offset, start)
        offset = offset + seq_lengths[i]
    mask1 = (positions - 1 >= start).astype(F32)
    mask2 = (positions - 2 >= start).astype(F32)

    def halo_links(land, job, phase):
        out = []
        for k in range(3):
            where = [pl.ds(0, 4) if axis in ROUTES[k][:phase] else pl.ds(place[axis], 1) for axis in range(3)]
            view = land.at[k, where[0], where[1], where[2]]
            axis = ROUTES[k][phase]
            for step in range(1, 4):
                out.append(link(view, view, halo_send.at[job, phase], halo_recv.at[job, phase], axis, step))
        return out

    def halo_ready(land, job, phase):
        view = (land.at[:, pl.ds(0, 3), 0, 0], land.at[:, pl.ds(0, 3), :, 0], land.at[:, pl.ds(0, 3)])[phase]
        all_links(view, halo_send.at[job, phase], halo_recv.at[job, phase])

    def halo_rows(land, slot):
        at = (slot // 16, (slot // 4) % 4, slot % 4)
        return jnp.concatenate([land[k, at[0], at[1], at[2]] for k in range(3)], axis=1)

    def put_halo(land, two):
        width = two.shape[1] // 3
        for k in range(3):
            land[k, place[0], place[1], place[2]] = two[:, width * k:width * k + width]

    def first_norm(values):
        scale = lax.rsqrt(jnp.mean(values * values, axis=1, keepdims=True) + EPS)
        return scale, values * scale * mixgain[...]

    tok_load.wait()
    put_halo(tails, tok_v[BLK - 16:BLK, :].astype(F32)[14:16])
    pl.semaphore_wait(barrier, 10)
    started(halo_links(tails, 0, 0))
    waited(gain_loads)
    scale_a, n1 = first_norm(tok_v[...].astype(F32))
    n_v[...] = n1.astype(BF16)
    in_loads[0].wait()
    b_v[...] = dot_nn(n_v[...], col[0, :, :HALF])
    started([cot_load])
    for s in range(3):
        started(down_loads(s))
    halo_ready(tails, 0, 0)
    started(halo_links(tails, 0, 1))
    in_loads[2].wait()
    x_v[...] = dot_nn(n_v[...], col[2, :, :HALF])
    v_v[...] = (b_v[...] * x_v[...]).astype(BF16).astype(F32)
    in_loads[1].wait()
    c_v[...] = dot_nn(n_v[...], col[1, :, :HALF])
    started(pair_loads(0))
    cot_load.wait()

    def hidden_grads(first, end):
        for s in range(first, end):
            down_ready(s)
            da_v[:, SPAN * s:SPAN * s + span(s)] = dot_nt(cot_v[...], down_ring[s % 3, :span(s), :])
            started(down_loads(s + 3))

    halo_ready(tails, 0, 1)
    started(halo_links(tails, 0, 2))
    s_src[1] = cot_v[...].T
    m_src[0] = n_v[...].T

    half = pl.ds(pl.multiple_of(core * HALF, HALF), HALF)

    def left_link(job, k, src, step):
        left = (s_left, m_left)[job]
        return link(src.at[half, :], left.at[k, half, pl.ds(128 * step, 128)],
                    l_send.at[job], l_recv.at[job], k, step)

    def send_left_s(k):
        src = s_src.at[1 if k == 2 else 0]
        s_left[k, :, :128] = src[...]
        for step in range(1, 4):
            left_link(0, k, src, step).start()

    def send_left_m(k, which):
        for step in range(1, 4):
            @pl.when(((place[k] + step) % 4 == 3) == (which == 1))
            def _():
                left_link(1, k, m_src.at[which], step).start()

    def others(job):
        return (s_left, m_left)[job].at[:, half, pl.ds(128, 384)]

    def forward_left(job):
        all_links(others(job), l_send.at[job], l_recv.at[job])
        cross(others(job), others(job), f_send.at[job], f_recv.at[job]).start()

    started([out_load])
    hidden_grads(0, 4)

    halo_ready(tails, 0, 2)
    send_left_s(2)
    for k in range(3):
        send_left_m(k, 0)
    last_two = jnp.concatenate([halo_rows(tails, before), jnp.zeros((14, D), F32)], axis=0)
    edge_scale, edge = first_norm(last_two)
    xs_send[1] = last_two * edge_scale
    edge = edge.astype(BF16)
    edge_b, edge_x = dot_nn(edge, col[0, :, :HALF]), dot_nn(edge, col[2, :, :HALF])
    carried = (edge_b * edge_x).astype(BF16).astype(F32)
    e_src[...] = edge
    eb_v[...] = edge_b
    ex_v[...] = edge_x

    def edge_left_links(n):
        return [
            link(e_src, e_left.at[n, pl.ds(16 * step, 16), :], e_send.at[0], e_recv.at[0], 2 * n, step)
            for step in range(1, 4)]

    def edge_piece(n, i):
        return er_src.at[n, :, pl.ds(pl.multiple_of(i * WM, WM), WM)]

    def edge_right_links(n):
        return [
            link(edge_piece(n, (place[2 * n] + step) % 4), e_right.at[n, pl.ds(16 * step, 16), :],
                 e_send.at[1], e_recv.at[1], 2 * n, step)
            for step in range(1, 4)]

    def edge_own(n):
        return [
            local(e_src, e_left.at[n, pl.ds(0, 16), :], own_edge.at[0]),
            local(edge_piece(n, place[2 * n]), e_right.at[n, pl.ds(0, 16), :], own_edge.at[1])]
    for s in range(1, 3):
        started(pair_loads(s))
    row_is0, row_is1 = rows == 0, rows == 1
    tap0, tap1, tap2 = taps[0:1, :], taps[1:2, :], taps[2:3, :]

    def shifted():
        v = v_v[...]
        one = jnp.where(row_is0, carried[1:2], pltpu.roll(v, 1, 0)) * mask1
        two = jnp.where(row_is0, carried[0:1], jnp.where(row_is1, carried[1:2], pltpu.roll(v, 2, 0))) * mask2
        return v, one, two

    v0, v1, v2 = shifted()
    u_v[...] = tap0 * v0 + tap1 * v1 + tap2 * v2
    y_v[...] = (c_v[...] * u_v[...]).astype(BF16)
    out_load.wait()
    dn2_v[...] = dot_nn(y_v[...], out_v[...])
    swap = cross(dn2_v, h2_v, x_send.at[0], x_recv.at[0])
    swap.start()
    hidden_grads(4, 6)
    swap.wait()
    h2_v[...] = tok_v[...].astype(F32) + (dn2_v[...] + h2_v[...])
    h2 = h2_v[...]
    scale_b = lax.rsqrt(jnp.mean(h2 * h2, axis=1, keepdims=True) + EPS)
    n_v[...] = (h2 * scale_b * glugain[...]).astype(BF16)
    s_src[0] = n_v[...].T
    send_left_s(0)
    send_left_s(1)

    lefts, rights, dsends, dlands = (s_left, m_left), (s_right, m_right), (s_dsend, m_dsend), (s_dland, m_dland)

    def right_piece(job, k, i, g):
        if job == 0:
            return act.at[k, i, :, pl.ds(*GROUPS[0][g])]
        return mixed_r.at[k, :, pl.ds(pl.multiple_of(i * WM, WM), WM)]

    def right_links(job, k, g):
        lanes = pl.ds(*GROUPS[job][g])
        return [
            link(right_piece(job, k, (place[k] + step) % 4, g), rights[job].at[k, pl.ds(128 * step, 128), lanes],
                 r_send.at[4 * job + g], r_recv.at[4 * job + g], k, step)
            for step in range(1, 4)]

    def send_right(job, g):
        for k in range(3):
            started(right_links(job, k, g))
        first, width = GROUPS[job][g]
        for k in range(3):
            rights[job][k, :128, first:first + width] = right_piece(job, k, place[k], g)[...]

    def b_out(job, k, j, g, row=0, count=384):
        lanes = pl.ds(*GROUPS[job][g])
        if job == 0:
            return s_bsend.at[k, j, pl.ds(row, count), lanes]
        return col.at[1, pl.ds(pl.multiple_of(384 * j + row, 96), count), pl.ds(WM * k, WM)]

    def b_in(job, k, i, g, row=0, count=384):
        if job == 0:
            return s_bland.at[k, i, pl.ds(row, count), pl.ds(*GROUPS[job][g])]
        return down_ring.at[i, pl.ds(row, count), pl.ds(WM * k, WM)]

    def c_out(job, k, j, g, row=0, count=96):
        return rights[job].at[k, pl.ds(pl.multiple_of(96 * j + row, 48), count), pl.ds(*GROUPS[job][g])]

    def c_in(job, k, i, g):
        if job == 0:
            return s_cland.at[k, i, :, pl.ds(*GROUPS[job][g])]
        return down_ring.at[i, pl.ds(0, 96), pl.ds(HALF + WM * k, WM)]

    LOW, HIGH = 0, 192

    def b_links(job, k, g, which):
        axis = (k + 1) % 3
        me = place[axis]
        opposite, ahead, behind = (me + 2) % 4, (me + 1) % 4, (me + 3) % 4
        table = (
            (opposite, LOW, 2, 1), (ahead, HIGH, 0, 1), (opposite, HIGH, 2, 3),
            (behind, LOW, 1, 3), (ahead, LOW, 0, 1), (behind, HIGH, 1, 3))
        out = []
        for n in which:
            part, row, land, step = table[n]
            sem = 2 * (4 * job + g) + (land != 2)
            out.append(link(b_out(job, k, part, g, row, 192), b_in(job, k, land, g, row, 192),
                            b_send.at[sem], b_recv.at[sem], axis, step))
        return out

    def c_links(job, k, g):
        axis = (k + 2) % 3
        return [
            link(c_out(job, k, (place[axis] + step) % 4, g), c_in(job, k, step - 1, g),
                 c_send.at[4 * job + g], c_recv.at[4 * job + g], axis, step)
            for step in range(1, 4)]

    def right_ready(job, g):
        lanes, n = pl.ds(*GROUPS[job][g]), 4 * job + g
        all_links(rights[job].at[:, pl.ds(128, 384), lanes], r_send.at[n], r_recv.at[n])

    def edges_ready():
        all_of(e_left.at[:, pl.ds(0, 16), :], own_edge.at[0])
        all_of(e_right.at[:, pl.ds(0, 16), :], own_edge.at[1])
        all_links(e_left.at[:, pl.ds(16, 48), :], e_send.at[0], e_recv.at[0])
        all_links(e_right.at[:, pl.ds(16, 48), :], e_send.at[1], e_recv.at[1])

    def start_b(job, k, g):
        lanes = pl.ds(*GROUPS[job][g])
        edges = job == 1 and k != 1

        def slab(x, carry):
            at = pl.ds(pl.multiple_of(x * 384, 384), 384)
            acc = dot_nn(lefts[job][k, at, :], rights[job][k, :, lanes])
            if edges:
                acc = acc + outer(e_left[k // 2, :, at], e_right[k // 2])
            row = pl.multiple_of(96 * x, 96)
            for j in range(4):
                if k == 0:
                    b_out(job, k, j, g, row, 96)[...] = acc[96 * j:96 * j + 96].astype(BF16)
                elif k == 1:
                    parts = [acc[96 * y + 24 * j:96 * y + 24 * j + 24] for y in range(4)]
                    b_out(job, k, j, g, row, 96)[...] = jnp.concatenate(parts, axis=0).astype(BF16)
                else:
                    b_out(job, k, x, g, 96 * j, 96)[...] = acc[96 * j:96 * j + 96].astype(BF16)
            return carry

        lax.fori_loop(0, 4, slab, 0)
        started(b_links(job, k, g, range(4)))

    def b_ready(job, g, last):
        sem = 2 * (4 * job + g) + last
        if job == 0:
            view = s_bland.at[:, pl.ds(0, 2) if last else pl.ds(2, 1), :, pl.ds(*GROUPS[job][g])]
        else:
            view = down_ring.at[pl.ds(0, 2) if last else pl.ds(2, 1), pl.ds(0, 384), pl.ds(0, HALF)]
        all_links(view, b_send.at[sem], b_recv.at[sem])

    def pass_on(job, k, g):
        me = place[(k + 1) % 3]
        for step, row in ((1, LOW), (3, HIGH)):
            own, via = b_out(job, k, (me + step) % 4, g, row, 192), b_in(job, k, 2, g, row, 192)
            own[...] = (own[...].astype(F32) + via[...].astype(F32)).astype(BF16)
        started(b_links(job, k, g, (4, 5)))

    def c_ready(job, g):
        if job == 0:
            view = s_cland.at[:, :, :, pl.ds(*GROUPS[job][g])]
        else:
            view = down_ring.at[:, pl.ds(0, 96), pl.ds(HALF, HALF)]
        all_links(view, c_send.at[4 * job + g], c_recv.at[4 * job + g])

    def start_c(job, k, g):
        me = place[(k + 1) % 3]

        def summed(q):
            total = b_out(job, k, me, g, 96 * q, 96)[...].astype(F32)
            for i in range(2):
                total = total + b_in(job, k, i, g, 96 * q, 96)[...].astype(F32)
            return total

        if k == 0:
            for p in range(2):
                a, b = summed(2 * p), summed(2 * p + 1)
                for j in range(4):
                    both = jnp.concatenate([a[24 * j:24 * j + 24], b[24 * j:24 * j + 24]], axis=0)
                    c_out(job, k, j, g, 48 * p, 48)[...] = both.astype(BF16)
        else:
            for q in range(4):
                c_out(job, k, q, g)[...] = summed(q).astype(BF16)
        started(c_links(job, k, g))

    def d_links(job, k):
        return [
            link(dsends[job].at[k, (place[k] + step) % 4], dlands[job].at[k, step],
                 d_send.at[job], d_recv.at[job], k, step)
            for step in range(1, 4)]

    def start_d(job, k):
        dsend, dland = dsends[job], dlands[job]
        for g, (first, width) in enumerate(GROUPS[job]):
            total = c_out(job, k, place[(k + 2) % 3], g)[...].astype(F32)
            for i in range(3):
                total = total + c_in(job, k, i, g)[...].astype(F32)
            pad = jnp.zeros((8, width), F32)
            for j in range(4):
                dsend[k, j, :, first:first + width] = jnp.concatenate([total[24 * j:24 * j + 24], pad], axis=0).astype(BF16)
        dland[k, 0] = dsend[k, place[k]]
        started(d_links(job, k))

    def finish(job, k):
        pieces = [dlands[job][k, (place[k] - i + 4) % 4].astype(F32)[:24] for i in range(4)]
        if job == 0:
            for i in range(4):
                for s in range(STEPS):
                    if SPAN * s + 128 * i < FF:
                        da_v[32 * k:32 * k + 24, SPAN * s + 128 * i:SPAN * s + 128 * i + 128] = pieces[i][:, 128 * s:128 * s + 128]
            local(da_v.at[pl.ds(32 * k, 24), :], (o_gate, o_lift, o_down)[k], store_sem.at[k]).start()
        else:
            stage = (h2_v, glu_v, dn2_v)[k]
            for i in range(4):
                stage[:24, WM * i:WM * i + WM] = pieces[i]
            local(stage.at[pl.ds(0, 24), pl.ds(0, HALF)], o_in.at[k], store_sem.at[3]).start()
            local(stage.at[pl.ds(0, 24), pl.ds(HALF, WM)], o_out.at[:, pl.ds(WM * k, WM)], store_sem.at[4]).start()

    glu_v[...] = jnp.zeros_like(glu_v)
    dn2_v[...] = jnp.zeros_like(dn2_v)

    def swiglu_step(s):
        slot = (s + 1) % 3
        pair_ready(s)
        w = span(s)
        both = dot_nn(n_v[...], col[slot, :, :2 * w])
        gate_pre, lift_pre = both[:, :w], both[:, w:]
        hidden_grad = da_v[:, SPAN * s:SPAN * s + w]
        sig = jax.nn.sigmoid(gate_pre)
        silu = gate_pre * sig
        hidden = (silu * lift_pre).astype(BF16)
        d_lift = (hidden_grad * silu).astype(BF16)
        d_gate = (hidden_grad * lift_pre * sig * (1.0 + gate_pre * (1.0 - sig))).astype(BF16)
        for k, values in enumerate((d_gate, d_lift, hidden)):
            for i in range(4):
                part = values[:, 128 * i:128 * i + 128] if 128 * i < w else jnp.zeros((BLK, 128), BF16)
                act[k, i, :, 128 * s:128 * s + 128] = part
        down_ready(STEPS + s)
        glu_v[...] += dot_nn(hidden, down_ring[(STEPS + s) % 3, :w, :])
        dn2_v[...] += dot_nt(jnp.concatenate([d_gate, d_lift], axis=1), col[slot, :, :2 * w])
        if s + 3 < STEPS:
            started(pair_loads(s + 3))
            started(down_loads(STEPS + s + 3))

    def left_ready(job):
        cross(others(job), others(job), f_send.at[job], f_recv.at[job]).wait()

    hidden_grads(6, STEPS)
    for s in range(2):
        swiglu_step(s)
    send_right(0, 0)
    for s in range(2, 4):
        swiglu_step(s)
    send_right(0, 1)
    forward_left(0)
    swiglu_step(4)
    left_ready(0)
    right_ready(0, 0)
    for k in range(3):
        start_b(0, k, 0)
    swiglu_step(5)
    send_right(0, 2)
    right_ready(0, 1)
    for k in range(3):
        start_b(0, k, 1)
    b_ready(0, 0, 0)
    for k in range(3):
        pass_on(0, k, 0)
    swiglu_step(6)
    send_right(0, 3)
    started(in_loads)

    xh_send[0] = dn2_v[...].astype(BF16)
    swap_dn2 = cross(xh_send.at[0], xh_recv.at[0], x_send.at[1], x_recv.at[1])
    swap_dn2.start()
    xh_send[1] = glu_v[...].astype(BF16)
    swap_glu = cross(xh_send.at[1], xh_recv.at[1], x_send.at[2], x_recv.at[2])
    swap_glu.start()
    swap_dn2.wait()
    h2 = h2_v[...]
    z2 = h2 * scale_b
    dn2 = xh_send[0].astype(F32) + xh_recv[0].astype(F32)
    glu_term = jnp.sum(dn2 * z2, axis=0, keepdims=True)
    scaled = dn2 * glugain[...]
    glu_v[...] = cot_v[...].astype(F32) + scale_b * (scaled - z2 * jnp.mean(scaled * z2, axis=1, keepdims=True))
    n_v[...] = glu_v[...].astype(BF16)
    dy = dot_nt(n_v[...], out_v[...])
    d_c = (dy * u_v[...]).astype(BF16)
    du = dy * c_v[...]
    v0, v1, v2 = shifted()
    tap_terms = [jnp.sum(du * v, axis=0, keepdims=True) for v in (v0, v1, v2)]
    w1, w2 = tap1 * (du * mask1), tap2 * (du * mask2)
    two = jnp.concatenate([w2[0:1], w1[0:1] + w2[1:2]], axis=0)
    put_halo(heads, two)
    started(halo_links(heads, 1, 0))
    dv = (tap0 * du + jnp.where(rows < 127, pltpu.roll(w1, 127, 0), 0.0)
          + jnp.where(rows < 126, pltpu.roll(w2, 126, 0), 0.0))
    mixed_r[0, :, :HALF] = (dv * x_v[...]).astype(BF16)
    mixed_r[1, :, :HALF] = d_c
    mixed_r[2, :, :HALF] = (dv * b_v[...]).astype(BF16)
    y_out = y_v[...]
    for k in range(3):
        mixed_r[k, :, HALF:] = y_out[:, 256 * k:256 * k + 256]
    share = jnp.concatenate([two, jnp.zeros((14, HALF), F32)], axis=0)
    none = jnp.zeros((16, WM), BF16)
    for n, other in enumerate((ex_v, eb_v)):
        er_src[n] = jnp.concatenate([(share * other[...]).astype(BF16), none], axis=1)
    send_right(1, 0)
    for n in range(2):
        started(edge_own(n))
        started(edge_left_links(n))
        started(edge_right_links(n))
    m_src[1] = n_v[...].T
    for k in range(3):
        send_left_m(k, 1)
        m_left[k, :, :128] = m_src[jnp.where(place[k] == 3, 1, 0)]
    b_ready(0, 1, 0)
    for k in range(3):
        pass_on(0, k, 1)
    right_ready(0, 2)
    for k in range(3):
        start_b(0, k, 2)
    swap_glu.wait()
    xh_send[1] = (h2_v[...] + (xh_send[1].astype(F32) + xh_recv[1].astype(F32))).astype(BF16)
    stores = started([local(xh_send.at[1], o_layer, load_sem.at[5])])
    b_ready(0, 0, 1)
    for k in range(3):
        start_c(0, k, 0)

    def my_half(row):
        return jnp.where(core == 0, row[:, :HALF], row[:, HALF:])

    def gain_links(axis):
        view = gain_land.at[axis, place[axis]]
        return [link(view, view, gain_send.at[axis], gain_recv.at[axis], axis, step) for step in range(1, 4)]

    def gain_sum(axis):
        all_links(gain_land.at[axis, pl.ds(0, 3)], gain_send.at[axis], gain_recv.at[axis])
        return (gain_land[axis, 0] + gain_land[axis, 1]) + (gain_land[axis, 2] + gain_land[axis, 3])

    def input_rows(dn1, first):
        z1 = tok_v[first:, :].astype(F32) * scale_a[first:]
        scaled = dn1 * mixgain[...]
        n_v[first:, :] = (glu_v[first:, :] + scale_a[first:] * (scaled - z1 * jnp.mean(scaled * z1, axis=1, keepdims=True))).astype(BF16)
        return z1

    waited(in_loads)
    for k in range(3):
        part = dot_nt(mixed_r[k, :, :HALF], col[k, :, :HALF])
        if k == 0:
            dn2_v[...] = part
        else:
            dn2_v[...] += part
    ahead = dot_nt(er_src[0, :, :HALF], col[0, :, :HALF]) + dot_nt(er_src[1, :, :HALF], col[2, :, :HALF])
    swap_dn1 = cross(dn2_v, da_v.at[:, pl.ds(0, D)], x_send.at[3], x_recv.at[3])
    swap_dn1.start()
    xs_send[0] = jnp.concatenate([jnp.sum(ahead * xs_send[1], axis=0, keepdims=True), jnp.zeros((15, D), F32)], axis=0)
    swap_row = cross(xs_send.at[0], da_v.at[pl.ds(0, 16), pl.ds(D, D)], x_send.at[4], x_recv.at[4])
    swap_row.start()
    right_ready(0, 3)
    for k in range(3):
        start_b(0, k, 3)
    halo_ready(heads, 1, 0)
    started(halo_links(heads, 1, 1))
    swap_dn1.wait()
    swap_row.wait()
    dn1 = dn2_v[...] + da_v[:, :D]
    z1 = input_rows(dn1, 0)
    mix_term = jnp.sum(dn1 * z1, axis=0, keepdims=True) + (xs_send[0, 0:1] + da_v[0:1, D:2 * D])
    gain_land[0, place[0]] = jnp.concatenate(
        [my_half(mix_term), my_half(glu_term), *tap_terms, jnp.zeros((3, HALF), F32)], axis=0)
    started(gain_links(0))
    forward_left(1)
    b_ready(0, 2, 0)
    for k in range(3):
        pass_on(0, k, 2)
    b_ready(0, 1, 1)
    for k in range(3):
        start_c(0, k, 1)
    b_ready(0, 3, 0)
    for k in range(3):
        pass_on(0, k, 3)
    halo_ready(heads, 1, 1)
    started(halo_links(heads, 1, 2))
    left_ready(1)
    right_ready(1, 0)
    edges_ready()
    for k in range(3):
        start_b(1, k, 0)
    gain_land[1, place[1]] = gain_sum(0)
    started(gain_links(1))
    b_ready(0, 2, 1)
    for k in range(3):
        start_c(0, k, 2)
    b_ready(1, 0, 0)
    for k in range(3):
        pass_on(1, k, 0)
    b_ready(0, 3, 1)
    for k in range(3):
        start_c(0, k, 3)
    gain_land[2, place[2]] = gain_sum(1)
    started(gain_links(2))
    halo_ready(heads, 1, 2)
    incoming = jnp.concatenate([jnp.zeros((14, HALF), F32), halo_rows(heads, after) * has_after], axis=0)
    xs_send[1] = (dot_nt((incoming * x_v[BLK - 16:, :]).astype(BF16), col[0, :, :HALF])
                  + dot_nt((incoming * b_v[BLK - 16:, :]).astype(BF16), col[2, :, :HALF]))
    swap = cross(xs_send.at[1], da_v.at[pl.ds(16, 16), pl.ds(D, D)], x_send.at[5], x_recv.at[5])
    swap.start()
    b_ready(1, 0, 1)
    for k in range(3):
        start_c(1, k, 0)
    swap.wait()
    input_rows((dn2_v[BLK - 16:, :] + da_v[BLK - 16:, :D]) + (xs_send[1] + da_v[16:32, D:2 * D]), BLK - 16)
    stores += started([local(n_v, o_input, load_sem.at[6])])
    v_v[0:8, :] = gain_sum(2)
    stores += started([local(v_v.at[pl.ds(0, 8), :], o_gains, load_sem.at[7])])
    for g in range(4):
        c_ready(0, g)
    for k in range(3):
        start_d(0, k)
    c_ready(1, 0)
    for k in range(3):
        start_d(1, k)
    for job in range(2):
        all_links(dlands[job].at[:, pl.ds(1, 3)], d_send.at[job], d_recv.at[job])
        for k in range(3):
            finish(job, k)
    for n, out in enumerate((o_gate, o_lift, o_down, o_in, o_out)):
        all_of(out, store_sem.at[n])
    waited(stores)


def run_layer(seq_lengths, block_slots, mixgain, glugain, taps, tokens, cotangent, inproj, outproj, gate_w, lift_w, down_w):
    vm = pl.BlockSpec(memory_space=pltpu.VMEM)
    sm = pl.BlockSpec(memory_space=pltpu.SMEM)
    hbm = pl.BlockSpec(memory_space=pl.ANY)
    dma = pltpu.SemaphoreType.DMA
    shape = jax.ShapeDtypeStruct
    row, full16, full32, half32 = (
        pltpu.VMEM((1, D), F32), pltpu.VMEM((BLK, D), BF16), pltpu.VMEM((BLK, D), F32), pltpu.VMEM((BLK, HALF), F32))
    return pl.pallas_call(
        layer_kernel,
        out_shape=[shape((BLK, D), BF16), shape((BLK, D), BF16), shape((8, HALF), F32)]
        + [shape(s, F32) for s in ((24, FF), (24, FF), (24, FF), (3, 24, HALF), (24, HALF))],
        in_specs=[sm, sm, hbm, hbm, vm] + [hbm] * 7,
        out_specs=[hbm] * 8,
        scratch_shapes=[
            row, row, full16, full16, full16,
            half32, half32, half32, half32, half32, pltpu.VMEM((BLK, HALF), BF16),
            full32, full32, full32,
            pltpu.VMEM((3, D, 2 * SPAN), BF16), pltpu.VMEM((3, SPAN, D), BF16), pltpu.VMEM((HALF, D), BF16),
            pltpu.VMEM((BLK, FF), F32), pltpu.VMEM((3, 4, BLK, WS), BF16), pltpu.VMEM((3, BLK, 4 * WM), BF16),
            pltpu.VMEM((2, D, BLK), BF16), pltpu.VMEM((2, D, BLK), BF16),
            pltpu.VMEM((16, D), BF16), pltpu.VMEM((16, HALF), F32), pltpu.VMEM((16, HALF), F32),
            pltpu.VMEM((2, 16, 4 * WM), BF16), pltpu.VMEM((2, 64, D), BF16), pltpu.VMEM((2, 64, WM), BF16),
            pltpu.VMEM((2, BLK, D), BF16), pltpu.VMEM((2, BLK, D), BF16), pltpu.VMEM((2, 16, D), F32),
            pltpu.VMEM((3, 4, 4, 4, 2, 512), F32), pltpu.VMEM((3, 4, 4, 4, 2, 256), F32),
            pltpu.VMEM((3, 4, 8, HALF), F32),
            pltpu.VMEM((3, D, 512), BF16), pltpu.VMEM((3, 512, WS), BF16), pltpu.VMEM((3, 4, 384, WS), BF16),
            pltpu.VMEM((3, 3, 384, WS), BF16), pltpu.VMEM((3, 3, 96, WS), BF16),
            pltpu.VMEM((3, 4, 32, WS), BF16), pltpu.VMEM((3, 4, 32, WS), BF16),
            pltpu.VMEM((3, D, 512), BF16), pltpu.VMEM((3, 512, WM), BF16),
            pltpu.VMEM((3, 4, 32, WM), BF16), pltpu.VMEM((3, 4, 32, WM), BF16),
            dma((8,)), dma((6,)), dma((3,)), dma((5,)), dma((6,)), dma((6,)),
            dma((2, 3)), dma((2, 3)), dma((3,)), dma((3,)),
            dma((2,)), dma((2,)), dma((2,)), dma((2,)), dma((5,)), dma((5,)),
            dma((10,)), dma((10,)), dma((5,)), dma((5,)), dma((2,)), dma((2,)),
            dma((2,)), dma((2,)), dma((2,)),
        ],
        compiler_params=pltpu.CompilerParams(collective_id=1, has_side_effects=True, vmem_limit_bytes=LIMIT),
        name="layer",
    )(seq_lengths, block_slots, mixgain, glugain, taps, tokens, cotangent, inproj, outproj, gate_w, lift_w, down_w)


def place_kernel(*refs):
    ins, outs, held, in_sems, out_sems = refs[:8], refs[8:18], refs[18:26], refs[26], refs[27]
    loads = [pltpu.make_async_copy(a, b, in_sems.at[i]) for i, (a, b) in enumerate(zip(ins, held))]
    for c in loads:
        c.start()
    gains = held[2]
    parts = [held[0], held[1], gains.at[0], gains.at[1], gains.at[pl.ds(2, 3)], *held[3:]]
    stores = []
    for i, (a, b) in enumerate(zip(parts, outs)):
        if i not in (3, 4):
            loads[i if i < 3 else i - 2].wait()
        stores.append(pltpu.make_async_copy(a, b, out_sems.at[i]))
        stores[-1].start()
    for c in stores:
        c.wait()


def place_outputs(results):
    hbm = pl.BlockSpec(memory_space=pl.ANY)
    shape = jax.ShapeDtypeStruct
    return pl.pallas_call(
        place_kernel,
        out_shape=[shape((BLK, D), BF16), shape((BLK, D), BF16), shape((HALF,), F32), shape((HALF,), F32), shape((3, HALF), F32)]
        + [shape(s, F32) for s in ((24, FF), (24, FF), (24, FF), (3, 24, HALF), (24, HALF))],
        in_specs=[hbm] * 8,
        out_specs=[hbm] * 10,
        scratch_shapes=[pltpu.VMEM(r.shape, r.dtype) for r in results] + [pltpu.SemaphoreType.DMA((8,)), pltpu.SemaphoreType.DMA((10,))],
        name="place",
    )(*results)


def on_device(
    tokens, cotangent, seq_lengths, block_slots, mixgain, inproj, conv_taps, outproj, glugain, gate_weight, lift_weight, down_weight
):
    results = run_layer(
        seq_lengths, block_slots, mixgain, glugain, conv_taps,
        tokens, cotangent, inproj, outproj, gate_weight, lift_weight, down_weight,
    )
    layer_out, input_grad, mixgain_grad, glugain_grad, taps_grad, gate_grad, lift_grad, down_rows, inproj_grad, out_rows = place_outputs(results)
    return (
        layer_out, input_grad, mixgain_grad, inproj_grad, taps_grad, out_rows.T, glugain_grad, gate_grad, lift_grad, down_rows.T,
    )


def solution(mesh):
    in_specs = (
        P("seq", None), P("seq", None), P(), P(), P(), P(None, None, "ch"), P(None, "ch"), P("ch", None),
        P(), P(None, "ch"), P(None, "ch"), P("ch", None),
    )
    out_specs = (
        P("seq", None), P("seq", None), P("ch"), P(None, "seq", "ch"), P(None, "ch"), P("ch", "seq"),
        P("ch"), P("seq", "ch"), P("seq", "ch"), P("ch", "seq"),
    )
    return jax.shard_map(on_device, mesh=mesh, in_specs=in_specs, out_specs=out_specs, check_vma=False)
```

```python
import jax
import jax.numpy as jnp
from jax import lax
from jax.experimental import pallas as pl
from jax.experimental.pallas import tpu as pltpu
from jax.sharding import PartitionSpec as P

MESH = pl.DeviceIdType.MESH
F32, BF16 = jnp.float32, jnp.bfloat16
BLK, D, HALF, FF = 128, 1536, 768, 3456
WS, WM = 896, 256
STEPS, SPAN = 7, 512
EPS = 1e-05
LIMIT = 64 * 1024 * 1024 - 256 * 1024
ROUTES = ((2, 1, 0), (0, 2, 1), (1, 0, 2))
GROUPS = (((0, 256), (256, 256), (512, 256), (768, 128)), ((0, 256),))


def dot_nt(a, b):
    return lax.dot_general(a, b, (((1,), (1,)), ((), ())), preferred_element_type=F32)


def outer(a, b):
    return lax.dot_general(a, b, (((0,), (0,)), ((), ())), preferred_element_type=F32)


def dot_nn(a, b):
    return jnp.dot(a, b, preferred_element_type=F32)


def span(s):
    return min(SPAN, FF - SPAN * s)


def layer_kernel(
    seq_lengths, block_slots, mixgain_1d, glugain_1d, taps,
    tokens, cotangent, inproj, outproj, gate_w, lift_w, down_w,
    o_layer, o_input, o_gains, o_gate, o_lift, o_down, o_in, o_out,
    mixgain, glugain, tok_v, cot_v, n_v, b_v, c_v, x_v, v_v, u_v, y_v, h2_v, glu_v, dn2_v,
    col, down_ring, out_v, da_v, act, mixed_r, s_src, m_src, e_src, eb_v, ex_v, er_src, er_two, e_left, e_right, xh_send, xh_recv, xs_send, tails, heads, gain_land,
    s_left, s_right, s_bsend, s_bland, s_cland, s_dsend, s_dland, m_left, m_right, m_dsend, m_dland,
    load_sem, col_sem, down_sem, store_sem, x_send, x_recv, halo_send, halo_recv, gain_send, gain_recv,
    l_send, l_recv, f_send, f_recv, r_send, r_recv,
    b_send, b_recv, c_send, c_recv, d_send, d_recv, e_send, e_recv, own_edge,
):
    seq, core = lax.axis_index("seq"), lax.axis_index("ch")
    place = (seq // 16, (seq // 4) % 4, seq % 4)

    def peer(axis, step):
        at = [(place[i] + step) % 4 if i == axis else place[i] for i in range(3)]
        return at[0] * 16 + at[1] * 4 + at[2]

    def local(src, dst, sem):
        return pltpu.make_async_copy(src, dst, sem)

    def link(src, dst, send, recv, axis, step):
        return pltpu.make_async_remote_copy(
            src_ref=src, dst_ref=dst, send_sem=send, recv_sem=recv,
            device_id=(peer(axis, step), core), device_id_type=MESH)

    def cross(src, dst, send, recv):
        return pltpu.make_async_remote_copy(
            src_ref=src, dst_ref=dst, send_sem=send, recv_sem=recv,
            device_id=(seq, 1 - core), device_id_type=MESH)

    def started(copies):
        for c in copies:
            c.start()
        return copies

    def waited(copies):
        for c in copies:
            c.wait()

    def all_of(view, sem):
        local(view, view, sem).wait()

    def all_links(view, send, recv):
        link(view, view, send, recv, 0, 1).wait()

    tok_load = local(tokens, tok_v, load_sem.at[0])
    cot_load = local(cotangent, cot_v, load_sem.at[1])
    out_load = local(outproj, out_v, load_sem.at[2])
    gain_loads = [local(mixgain_1d, mixgain.at[0], load_sem.at[3]), local(glugain_1d, glugain.at[0], load_sem.at[4])]
    in_loads = [local(inproj.at[k], col.at[k, :, pl.ds(0, HALF)], col_sem.at[3 + k]) for k in range(3)]
    tok_load.start()
    started(gain_loads)
    in_loads[0].start()
    in_loads[2].start()
    in_loads[1].start()

    def pair_loads(s):
        slot, w = (s + 1) % 3, span(s)
        return [
            local(weight.at[:, pl.ds(SPAN * s, w)], col.at[slot, :, pl.ds(w * m, w)], col_sem.at[slot])
            for m, weight in enumerate((gate_w, lift_w))]

    def down_loads(t):
        s, slot = t % STEPS, t % 3
        return [local(down_w.at[pl.ds(SPAN * s, span(s)), :], down_ring.at[slot, pl.ds(0, span(s)), :], down_sem.at[slot])]

    def pair_ready(s):
        all_of(col.at[(s + 1) % 3, :, pl.ds(0, 2 * span(s))], col_sem.at[(s + 1) % 3])

    def down_ready(t):
        all_of(down_ring.at[t % 3, pl.ds(0, span(t % STEPS)), :], down_sem.at[t % 3])

    barrier = pltpu.get_barrier_semaphore()
    for axis in range(3):
        for step in range(1, 4):
            pl.semaphore_signal(barrier, inc=1, device_id=(peer(axis, step), core), device_id_type=MESH)
    pl.semaphore_signal(barrier, inc=1, device_id=(seq, 1 - core), device_id_type=MESH)

    block = jnp.int32(0)
    for i in range(64):
        block = jnp.where(block_slots[i] == seq, i, block)
    before = block_slots[jnp.maximum(block - 1, 0)]
    after = block_slots[jnp.minimum(block + 1, 63)]
    has_after = (block < 63).astype(F32)
    rows = lax.broadcasted_iota(jnp.int32, (BLK, 1), 0)
    positions = block * BLK + rows
    start = jnp.zeros((BLK, 1), jnp.int32)
    offset = jnp.int32(0)
    for i in range(4):
        start = jnp.where(offset <= positions, offset, start)
        offset = offset + seq_lengths[i]
    mask1 = (positions - 1 >= start).astype(F32)
    mask2 = (positions - 2 >= start).astype(F32)

    def halo_links(land, job, phase):
        out = []
        for k in range(3):
            where = [pl.ds(0, 4) if axis in ROUTES[k][:phase] else pl.ds(place[axis], 1) for axis in range(3)]
            view = land.at[k, where[0], where[1], where[2]]
            axis = ROUTES[k][phase]
            for step in range(1, 4):
                out.append(link(view, view, halo_send.at[job, phase], halo_recv.at[job, phase], axis, step))
        return out

    def halo_ready(land, job, phase):
        view = (land.at[:, pl.ds(0, 3), 0, 0], land.at[:, pl.ds(0, 3), :, 0], land.at[:, pl.ds(0, 3)])[phase]
        all_links(view, halo_send.at[job, phase], halo_recv.at[job, phase])

    def halo_rows(land, slot):
        at = (slot // 16, (slot // 4) % 4, slot % 4)
        return jnp.concatenate([land[k, at[0], at[1], at[2]] for k in range(3)], axis=1)

    def put_halo(land, two):
        width = two.shape[1] // 3
        for k in range(3):
            land[k, place[0], place[1], place[2]] = two[:, width * k:width * k + width]

    def first_norm(values):
        scale = lax.rsqrt(jnp.mean(values * values, axis=1, keepdims=True) + EPS)
        return scale, values * scale * mixgain[...]

    tok_load.wait()
    put_halo(tails, tok_v[BLK - 16:BLK, :].astype(F32)[14:16])
    pl.semaphore_wait(barrier, 10)
    started(halo_links(tails, 0, 0))
    waited(gain_loads)
    scale_a, n1 = first_norm(tok_v[...].astype(F32))
    n_v[...] = n1.astype(BF16)
    in_loads[0].wait()
    b_v[...] = dot_nn(n_v[...], col[0, :, :HALF])
    started([cot_load])
    for s in range(3):
        started(down_loads(s))
    halo_ready(tails, 0, 0)
    started(halo_links(tails, 0, 1))
    in_loads[2].wait()
    x_v[...] = dot_nn(n_v[...], col[2, :, :HALF])
    v_v[...] = (b_v[...] * x_v[...]).astype(BF16).astype(F32)
    in_loads[1].wait()
    c_v[...] = dot_nn(n_v[...], col[1, :, :HALF])
    started(pair_loads(0))
    cot_load.wait()

    def hidden_grads(first, end):
        for s in range(first, end):
            down_ready(s)
            da_v[:, SPAN * s:SPAN * s + span(s)] = dot_nt(cot_v[...], down_ring[s % 3, :span(s), :])
            started(down_loads(s + 3))

    halo_ready(tails, 0, 1)
    started(halo_links(tails, 0, 2))
    s_src[1] = cot_v[...].T
    m_src[0] = n_v[...].T

    half = pl.ds(pl.multiple_of(core * HALF, HALF), HALF)

    def left_link(job, k, src, step):
        left = (s_left, m_left)[job]
        sem = 1 if job == 1 else 2 + step // 2
        return link(src.at[half, :], left.at[k, half, pl.ds(128 * step, 128)],
                    l_send.at[sem], l_recv.at[sem], k, step)

    def send_left_s(k):
        src = s_src.at[1 if k == 2 else 0]
        s_left[k, :, :128] = src[...]
        for step in (1, 3):
            left_link(0, k, src, step).start()

    def hand_on():
        for n, step in enumerate((1, 3)):
            all_links(s_left.at[:, half, pl.ds(128 * step, 128)], l_send.at[2 + n], l_recv.at[2 + n])
            part = pl.ds(pl.multiple_of(core * HALF + 384 * n, 384), 384)
            for k in range(3):
                link(s_left.at[k, part, pl.ds(128 * step, 128)], s_left.at[k, part, pl.ds(256, 128)],
                     l_send.at[0], l_recv.at[0], k, step).start()

    def send_left_m(k, which):
        for step in range(1, 4):
            @pl.when(((place[k] + step) % 4 == 3) == (which == 1))
            def _():
                left_link(1, k, m_src.at[which], step).start()

    def others(job):
        return (s_left, m_left)[job].at[:, half, pl.ds(128, 384)]

    def forward_left(job):
        if job == 0:
            all_links(s_left.at[:, half, pl.ds(256, 128)], l_send.at[0], l_recv.at[0])
        else:
            all_links(others(1), l_send.at[1], l_recv.at[1])
        cross(others(job), others(job), f_send.at[job], f_recv.at[job]).start()

    started([out_load])
    hidden_grads(0, 4)

    halo_ready(tails, 0, 2)
    send_left_s(2)
    for k in range(3):
        send_left_m(k, 0)
    last_two = jnp.concatenate([halo_rows(tails, before), jnp.zeros((14, D), F32)], axis=0)
    edge_scale, edge = first_norm(last_two)
    xs_send[1] = last_two * edge_scale
    edge = edge.astype(BF16)
    edge_b, edge_x = dot_nn(edge, col[0, :, :HALF]), dot_nn(edge, col[2, :, :HALF])
    carried = (edge_b * edge_x).astype(BF16).astype(F32)
    e_src[...] = edge.astype(F32)[0:2]
    eb_v[...] = edge_b
    ex_v[...] = edge_x

    def edge_left_links(n):
        return [
            link(e_src, e_left.at[n, step], e_send.at[0], e_recv.at[0], 2 * n, step)
            for step in range(1, 4)]

    def edge_piece(n, i):
        return er_two.at[n, :, pl.ds(pl.multiple_of(i * WM, WM), WM)]

    def edge_right_links(n):
        return [
            link(edge_piece(n, (place[2 * n] + step) % 4), e_right.at[n, step],
                 e_send.at[1], e_recv.at[1], 2 * n, step)
            for step in range(1, 4)]

    def edge_own(n):
        return [
            local(e_src, e_left.at[n, 0], own_edge.at[0]),
            local(edge_piece(n, place[2 * n]), e_right.at[n, 0], own_edge.at[1])]
    for s in range(1, 3):
        started(pair_loads(s))
    row_is0, row_is1 = rows == 0, rows == 1
    tap0, tap1, tap2 = taps[0:1, :], taps[1:2, :], taps[2:3, :]

    def shifted():
        v = v_v[...]
        one = jnp.where(row_is0, carried[1:2], pltpu.roll(v, 1, 0)) * mask1
        two = jnp.where(row_is0, carried[0:1], jnp.where(row_is1, carried[1:2], pltpu.roll(v, 2, 0))) * mask2
        return v, one, two

    v0, v1, v2 = shifted()
    u_v[...] = tap0 * v0 + tap1 * v1 + tap2 * v2
    y_v[...] = (c_v[...] * u_v[...]).astype(BF16)
    out_load.wait()
    dn2_v[...] = dot_nn(y_v[...], out_v[...])
    swap = cross(dn2_v, h2_v, x_send.at[0], x_recv.at[0])
    swap.start()
    hidden_grads(4, 6)
    swap.wait()
    h2_v[...] = tok_v[...].astype(F32) + (dn2_v[...] + h2_v[...])
    h2 = h2_v[...]
    scale_b = lax.rsqrt(jnp.mean(h2 * h2, axis=1, keepdims=True) + EPS)
    n_v[...] = (h2 * scale_b * glugain[...]).astype(BF16)
    s_src[0] = n_v[...].T
    send_left_s(0)
    send_left_s(1)

    lefts, rights, dsends, dlands = (s_left, m_left), (s_right, m_right), (s_dsend, m_dsend), (s_dland, m_dland)

    def right_piece(job, k, i, g):
        if job == 0:
            return act.at[k, i, :, pl.ds(*GROUPS[0][g])]
        return mixed_r.at[k, :, pl.ds(pl.multiple_of(i * WM, WM), WM)]

    def right_links(job, k, g):
        lanes = pl.ds(*GROUPS[job][g])
        return [
            link(right_piece(job, k, (place[k] + step) % 4, g), rights[job].at[k, pl.ds(128 * step, 128), lanes],
                 r_send.at[4 * job + g], r_recv.at[4 * job + g], k, step)
            for step in range(1, 4)]

    def send_right(job, g):
        for k in range(3):
            started(right_links(job, k, g))
        first, width = GROUPS[job][g]
        for k in range(3):
            rights[job][k, :128, first:first + width] = right_piece(job, k, place[k], g)[...]

    def b_out(job, k, j, g, row=0, count=384):
        lanes = pl.ds(*GROUPS[job][g])
        if job == 0:
            return s_bsend.at[k, j, pl.ds(row, count), lanes]
        return col.at[1, pl.ds(pl.multiple_of(384 * j + row, 96), count), pl.ds(WM * k, WM)]

    def b_in(job, k, i, g, row=0, count=384):
        if job == 0:
            return s_bland.at[k, i, pl.ds(row, count), pl.ds(*GROUPS[job][g])]
        return down_ring.at[i, pl.ds(row, count), pl.ds(WM * k, WM)]

    def c_out(job, k, j, g, row=0, count=96):
        return rights[job].at[k, pl.ds(pl.multiple_of(96 * j + row, 48), count), pl.ds(*GROUPS[job][g])]

    def c_in(job, k, i, g):
        if job == 0:
            return s_cland.at[k, i, :, pl.ds(*GROUPS[job][g])]
        return down_ring.at[i, pl.ds(0, 96), pl.ds(HALF + WM * k, WM)]

    LOW, HIGH = 0, 192

    def b_links(job, k, g, which):
        axis = (k + 1) % 3
        me = place[axis]
        opposite, ahead, behind = (me + 2) % 4, (me + 1) % 4, (me + 3) % 4
        table = (
            (opposite, LOW, 2, 1), (ahead, HIGH, 0, 1), (opposite, HIGH, 2, 3),
            (behind, LOW, 1, 3), (ahead, LOW, 0, 1), (behind, HIGH, 1, 3))
        out = []
        for n in which:
            part, row, land, step = table[n]
            sem = 2 * (4 * job + g) + (land != 2)
            out.append(link(b_out(job, k, part, g, row, 192), b_in(job, k, land, g, row, 192),
                            b_send.at[sem], b_recv.at[sem], axis, step))
        return out

    def c_links(job, k, g):
        axis = (k + 2) % 3
        return [
            link(c_out(job, k, (place[axis] + step) % 4, g), c_in(job, k, step - 1, g),
                 c_send.at[4 * job + g], c_recv.at[4 * job + g], axis, step)
            for step in range(1, 4)]

    def right_ready(job, g):
        lanes, n = pl.ds(*GROUPS[job][g]), 4 * job + g
        all_links(rights[job].at[:, pl.ds(128, 384), lanes], r_send.at[n], r_recv.at[n])

    def edges_ready():
        all_of(e_left.at[:, 0], own_edge.at[0])
        all_of(e_right.at[:, 0], own_edge.at[1])
        all_links(e_left.at[:, pl.ds(1, 3)], e_send.at[0], e_recv.at[0])
        all_links(e_right.at[:, pl.ds(1, 3)], e_send.at[1], e_recv.at[1])

    def edge_tile(parts):
        return jnp.concatenate([*parts, jnp.zeros((8, parts[0].shape[1]), F32)], axis=0).astype(BF16)

    def start_b(job, k, g):
        lanes = pl.ds(*GROUPS[job][g])
        edges = job == 1 and k != 1

        def slab(x, carry):
            at = pl.ds(pl.multiple_of(x * 384, 384), 384)
            acc = dot_nn(lefts[job][k, at, :], rights[job][k, :, lanes])
            if edges:
                acc = acc + outer(edge_tile([e_left[k // 2, i, :, at] for i in range(4)]), edge_tile([e_right[k // 2, i] for i in range(4)]))
            row = pl.multiple_of(96 * x, 96)
            for j in range(4):
                if k == 0:
                    b_out(job, k, j, g, row, 96)[...] = acc[96 * j:96 * j + 96].astype(BF16)
                elif k == 1:
                    parts = [acc[96 * y + 24 * j:96 * y + 24 * j + 24] for y in range(4)]
                    b_out(job, k, j, g, row, 96)[...] = jnp.concatenate(parts, axis=0).astype(BF16)
                else:
                    b_out(job, k, x, g, 96 * j, 96)[...] = acc[96 * j:96 * j + 96].astype(BF16)
            return carry

        lax.fori_loop(0, 4, slab, 0)
        started(b_links(job, k, g, range(4)))

    def b_ready(job, g, last):
        sem = 2 * (4 * job + g) + last
        if job == 0:
            view = s_bland.at[:, pl.ds(0, 2) if last else pl.ds(2, 1), :, pl.ds(*GROUPS[job][g])]
        else:
            view = down_ring.at[pl.ds(0, 2) if last else pl.ds(2, 1), pl.ds(0, 384), pl.ds(0, HALF)]
        all_links(view, b_send.at[sem], b_recv.at[sem])

    def pass_on(job, k, g):
        me = place[(k + 1) % 3]
        for step, row in ((1, LOW), (3, HIGH)):
            own, via = b_out(job, k, (me + step) % 4, g, row, 192), b_in(job, k, 2, g, row, 192)
            own[...] = (own[...].astype(F32) + via[...].astype(F32)).astype(BF16)
        started(b_links(job, k, g, (4, 5)))

    def c_ready(job, g):
        if job == 0:
            view = s_cland.at[:, :, :, pl.ds(*GROUPS[job][g])]
        else:
            view = down_ring.at[:, pl.ds(0, 96), pl.ds(HALF, HALF)]
        all_links(view, c_send.at[4 * job + g], c_recv.at[4 * job + g])

    def start_c(job, k, g):
        me = place[(k + 1) % 3]

        def summed(q):
            total = b_out(job, k, me, g, 96 * q, 96)[...].astype(F32)
            for i in range(2):
                total = total + b_in(job, k, i, g, 96 * q, 96)[...].astype(F32)
            return total

        if k == 0:
            for p in range(2):
                a, b = summed(2 * p), summed(2 * p + 1)
                for j in range(4):
                    both = jnp.concatenate([a[24 * j:24 * j + 24], b[24 * j:24 * j + 24]], axis=0)
                    c_out(job, k, j, g, 48 * p, 48)[...] = both.astype(BF16)
        else:
            for q in range(4):
                c_out(job, k, q, g)[...] = summed(q).astype(BF16)
        started(c_links(job, k, g))

    def d_links(job, k):
        return [
            link(dsends[job].at[k, (place[k] + step) % 4], dlands[job].at[k, step],
                 d_send.at[job], d_recv.at[job], k, step)
            for step in range(1, 4)]

    def start_d(job, k):
        dsend, dland = dsends[job], dlands[job]
        for g, (first, width) in enumerate(GROUPS[job]):
            total = c_out(job, k, place[(k + 2) % 3], g)[...].astype(F32)
            for i in range(3):
                total = total + c_in(job, k, i, g)[...].astype(F32)
            pad = jnp.zeros((8, width), F32)
            for j in range(4):
                dsend[k, j, :, first:first + width] = jnp.concatenate([total[24 * j:24 * j + 24], pad], axis=0).astype(BF16)
        dland[k, 0] = dsend[k, place[k]]
        started(d_links(job, k))

    def finish(job, k):
        pieces = [dlands[job][k, (place[k] - i + 4) % 4].astype(F32)[:24] for i in range(4)]
        if job == 0:
            for i in range(4):
                for s in range(STEPS):
                    if SPAN * s + 128 * i < FF:
                        da_v[32 * k:32 * k + 24, SPAN * s + 128 * i:SPAN * s + 128 * i + 128] = pieces[i][:, 128 * s:128 * s + 128]
            local(da_v.at[pl.ds(32 * k, 24), :], (o_gate, o_lift, o_down)[k], store_sem.at[k]).start()
        else:
            stage = (h2_v, glu_v, dn2_v)[k]
            for i in range(4):
                stage[:24, WM * i:WM * i + WM] = pieces[i]
            local(stage.at[pl.ds(0, 24), pl.ds(0, HALF)], o_in.at[k], store_sem.at[3]).start()
            local(stage.at[pl.ds(0, 24), pl.ds(HALF, WM)], o_out.at[:, pl.ds(WM * k, WM)], store_sem.at[4]).start()

    glu_v[...] = jnp.zeros_like(glu_v)
    dn2_v[...] = jnp.zeros_like(dn2_v)

    def swiglu_step(s):
        slot = (s + 1) % 3
        pair_ready(s)
        w = span(s)
        both = dot_nn(n_v[...], col[slot, :, :2 * w])
        gate_pre, lift_pre = both[:, :w], both[:, w:]
        hidden_grad = da_v[:, SPAN * s:SPAN * s + w]
        sig = jax.nn.sigmoid(gate_pre)
        silu = gate_pre * sig
        hidden = (silu * lift_pre).astype(BF16)
        d_lift = (hidden_grad * silu).astype(BF16)
        d_gate = (hidden_grad * lift_pre * sig * (1.0 + gate_pre * (1.0 - sig))).astype(BF16)
        for k, values in enumerate((d_gate, d_lift, hidden)):
            for i in range(4):
                part = values[:, 128 * i:128 * i + 128] if 128 * i < w else jnp.zeros((BLK, 128), BF16)
                act[k, i, :, 128 * s:128 * s + 128] = part
        down_ready(STEPS + s)
        glu_v[...] += dot_nn(hidden, down_ring[(STEPS + s) % 3, :w, :])
        dn2_v[...] += dot_nt(jnp.concatenate([d_gate, d_lift], axis=1), col[slot, :, :2 * w])
        if s + 3 < STEPS:
            started(pair_loads(s + 3))
            started(down_loads(STEPS + s + 3))

    def left_ready(job):
        cross(others(job), others(job), f_send.at[job], f_recv.at[job]).wait()

    hidden_grads(6, STEPS)
    for s in range(2):
        swiglu_step(s)
    send_right(0, 0)
    swiglu_step(2)
    hand_on()
    swiglu_step(3)
    send_right(0, 1)
    forward_left(0)
    swiglu_step(4)
    left_ready(0)
    right_ready(0, 0)
    for k in range(3):
        start_b(0, k, 0)
    swiglu_step(5)
    send_right(0, 2)
    right_ready(0, 1)
    for k in range(3):
        start_b(0, k, 1)
    b_ready(0, 0, 0)
    for k in range(3):
        pass_on(0, k, 0)
    swiglu_step(6)
    send_right(0, 3)
    started(in_loads)

    xh_send[0] = dn2_v[...].astype(BF16)
    swap_dn2 = cross(xh_send.at[0], xh_recv.at[0], x_send.at[1], x_recv.at[1])
    swap_dn2.start()
    xh_send[1] = glu_v[...].astype(BF16)
    swap_glu = cross(xh_send.at[1], xh_recv.at[1], x_send.at[2], x_recv.at[2])
    swap_glu.start()
    swap_dn2.wait()
    h2 = h2_v[...]
    z2 = h2 * scale_b
    dn2 = xh_send[0].astype(F32) + xh_recv[0].astype(F32)
    glu_term = jnp.sum(dn2 * z2, axis=0, keepdims=True)
    scaled = dn2 * glugain[...]
    glu_v[...] = cot_v[...].astype(F32) + scale_b * (scaled - z2 * jnp.mean(scaled * z2, axis=1, keepdims=True))
    n_v[...] = glu_v[...].astype(BF16)
    dy = dot_nt(n_v[...], out_v[...])
    d_c = (dy * u_v[...]).astype(BF16)
    du = dy * c_v[...]
    v0, v1, v2 = shifted()
    tap_terms = [jnp.sum(du * v, axis=0, keepdims=True) for v in (v0, v1, v2)]
    w1, w2 = tap1 * (du * mask1), tap2 * (du * mask2)
    two = jnp.concatenate([w2[0:1], w1[0:1] + w2[1:2]], axis=0)
    put_halo(heads, two)
    started(halo_links(heads, 1, 0))
    dv = (tap0 * du + jnp.where(rows < 127, pltpu.roll(w1, 127, 0), 0.0)
          + jnp.where(rows < 126, pltpu.roll(w2, 126, 0), 0.0))
    mixed_r[0, :, :HALF] = (dv * x_v[...]).astype(BF16)
    mixed_r[1, :, :HALF] = d_c
    mixed_r[2, :, :HALF] = (dv * b_v[...]).astype(BF16)
    y_out = y_v[...]
    for k in range(3):
        mixed_r[k, :, HALF:] = y_out[:, 256 * k:256 * k + 256]
    share = jnp.concatenate([two, jnp.zeros((14, HALF), F32)], axis=0)
    none = jnp.zeros((16, WM), BF16)
    for n, other in enumerate((ex_v, eb_v)):
        er_src[n] = jnp.concatenate([(share * other[...]).astype(BF16), none], axis=1)
        er_two[n] = er_src[n].astype(F32)[0:2]
    send_right(1, 0)
    for n in range(2):
        started(edge_own(n))
        started(edge_left_links(n))
        started(edge_right_links(n))
    m_src[1] = n_v[...].T
    for k in range(3):
        send_left_m(k, 1)
        m_left[k, :, :128] = m_src[jnp.where(place[k] == 3, 1, 0)]
    b_ready(0, 1, 0)
    for k in range(3):
        pass_on(0, k, 1)
    right_ready(0, 2)
    for k in range(3):
        start_b(0, k, 2)
    swap_glu.wait()
    xh_send[1] = (h2_v[...] + (xh_send[1].astype(F32) + xh_recv[1].astype(F32))).astype(BF16)
    stores = started([local(xh_send.at[1], o_layer, load_sem.at[5])])
    b_ready(0, 0, 1)
    for k in range(3):
        start_c(0, k, 0)

    def my_half(row):
        return jnp.where(core == 0, row[:, :HALF], row[:, HALF:])

    def gain_links(axis):
        view = gain_land.at[axis, place[axis]]
        return [link(view, view, gain_send.at[axis], gain_recv.at[axis], axis, step) for step in range(1, 4)]

    def gain_sum(axis):
        all_links(gain_land.at[axis, pl.ds(0, 3)], gain_send.at[axis], gain_recv.at[axis])
        return (gain_land[axis, 0] + gain_land[axis, 1]) + (gain_land[axis, 2] + gain_land[axis, 3])

    def input_rows(dn1, first):
        z1 = tok_v[first:, :].astype(F32) * scale_a[first:]
        scaled = dn1 * mixgain[...]
        n_v[first:, :] = (glu_v[first:, :] + scale_a[first:] * (scaled - z1 * jnp.mean(scaled * z1, axis=1, keepdims=True))).astype(BF16)
        return z1

    waited(in_loads)
    for k in range(3):
        part = dot_nt(mixed_r[k, :, :HALF], col[k, :, :HALF])
        if k == 0:
            dn2_v[...] = part
        else:
            dn2_v[...] += part
    ahead = dot_nt(er_src[0, :, :HALF], col[0, :, :HALF]) + dot_nt(er_src[1, :, :HALF], col[2, :, :HALF])
    swap_dn1 = cross(dn2_v, da_v.at[:, pl.ds(0, D)], x_send.at[3], x_recv.at[3])
    swap_dn1.start()
    xs_send[0] = jnp.concatenate([jnp.sum(ahead * xs_send[1], axis=0, keepdims=True), jnp.zeros((15, D), F32)], axis=0)
    swap_row = cross(xs_send.at[0], da_v.at[pl.ds(0, 16), pl.ds(D, D)], x_send.at[4], x_recv.at[4])
    swap_row.start()
    right_ready(0, 3)
    for k in range(3):
        start_b(0, k, 3)
    swap_dn1.wait()
    swap_row.wait()
    dn1 = dn2_v[...] + da_v[:, :D]
    z1 = input_rows(dn1, 0)
    mix_term = jnp.sum(dn1 * z1, axis=0, keepdims=True) + (xs_send[0, 0:1] + da_v[0:1, D:2 * D])
    gain_land[0, place[0]] = jnp.concatenate(
        [my_half(mix_term), my_half(glu_term), *tap_terms, jnp.zeros((3, HALF), F32)], axis=0)
    started(gain_links(0))
    forward_left(1)
    halo_ready(heads, 1, 0)
    started(halo_links(heads, 1, 1))
    left_ready(1)
    right_ready(1, 0)
    edges_ready()
    for k in range(3):
        start_b(1, k, 0)
    b_ready(0, 2, 0)
    for k in range(3):
        pass_on(0, k, 2)
    b_ready(0, 1, 1)
    for k in range(3):
        start_c(0, k, 1)
    b_ready(0, 3, 0)
    for k in range(3):
        pass_on(0, k, 3)
    halo_ready(heads, 1, 1)
    started(halo_links(heads, 1, 2))
    gain_land[1, place[1]] = gain_sum(0)
    started(gain_links(1))
    b_ready(1, 0, 0)
    for k in range(3):
        pass_on(1, k, 0)
    b_ready(0, 2, 1)
    for k in range(3):
        start_c(0, k, 2)
    b_ready(0, 3, 1)
    for k in range(3):
        start_c(0, k, 3)
    gain_land[2, place[2]] = gain_sum(1)
    started(gain_links(2))
    halo_ready(heads, 1, 2)
    incoming = jnp.concatenate([jnp.zeros((14, HALF), F32), halo_rows(heads, after) * has_after], axis=0)
    xs_send[1] = (dot_nt((incoming * x_v[BLK - 16:, :]).astype(BF16), col[0, :, :HALF])
                  + dot_nt((incoming * b_v[BLK - 16:, :]).astype(BF16), col[2, :, :HALF]))
    swap = cross(xs_send.at[1], da_v.at[pl.ds(16, 16), pl.ds(D, D)], x_send.at[5], x_recv.at[5])
    swap.start()
    b_ready(1, 0, 1)
    for k in range(3):
        start_c(1, k, 0)
    swap.wait()
    input_rows((dn2_v[BLK - 16:, :] + da_v[BLK - 16:, :D]) + (xs_send[1] + da_v[16:32, D:2 * D]), BLK - 16)
    stores += started([local(n_v, o_input, load_sem.at[6])])
    v_v[0:8, :] = gain_sum(2)
    stores += started([local(v_v.at[pl.ds(0, 8), :], o_gains, load_sem.at[7])])
    for g in range(4):
        c_ready(0, g)
    for k in range(3):
        start_d(0, k)
    c_ready(1, 0)
    for k in range(3):
        start_d(1, k)
    for job in range(2):
        all_links(dlands[job].at[:, pl.ds(1, 3)], d_send.at[job], d_recv.at[job])
        for k in range(3):
            finish(job, k)
    for n, out in enumerate((o_gate, o_lift, o_down, o_in, o_out)):
        all_of(out, store_sem.at[n])
    waited(stores)


def run_layer(seq_lengths, block_slots, mixgain, glugain, taps, tokens, cotangent, inproj, outproj, gate_w, lift_w, down_w):
    vm = pl.BlockSpec(memory_space=pltpu.VMEM)
    sm = pl.BlockSpec(memory_space=pltpu.SMEM)
    hbm = pl.BlockSpec(memory_space=pl.ANY)
    dma = pltpu.SemaphoreType.DMA
    shape = jax.ShapeDtypeStruct
    row, full16, full32, half32 = (
        pltpu.VMEM((1, D), F32), pltpu.VMEM((BLK, D), BF16), pltpu.VMEM((BLK, D), F32), pltpu.VMEM((BLK, HALF), F32))
    return pl.pallas_call(
        layer_kernel,
        out_shape=[shape((BLK, D), BF16), shape((BLK, D), BF16), shape((8, HALF), F32)]
        + [shape(s, F32) for s in ((24, FF), (24, FF), (24, FF), (3, 24, HALF), (24, HALF))],
        in_specs=[sm, sm, hbm, hbm, vm] + [hbm] * 7,
        out_specs=[hbm] * 8,
        scratch_shapes=[
            row, row, full16, full16, full16,
            half32, half32, half32, half32, half32, pltpu.VMEM((BLK, HALF), BF16),
            full32, full32, full32,
            pltpu.VMEM((3, D, 2 * SPAN), BF16), pltpu.VMEM((3, SPAN, D), BF16), pltpu.VMEM((HALF, D), BF16),
            pltpu.VMEM((BLK, FF), F32), pltpu.VMEM((3, 4, BLK, WS), BF16), pltpu.VMEM((3, BLK, 4 * WM), BF16),
            pltpu.VMEM((2, D, BLK), BF16), pltpu.VMEM((2, D, BLK), BF16),
            pltpu.VMEM((2, D), F32), pltpu.VMEM((16, HALF), F32), pltpu.VMEM((16, HALF), F32),
            pltpu.VMEM((2, 16, 4 * WM), BF16), pltpu.VMEM((2, 2, 4 * WM), F32), pltpu.VMEM((2, 4, 2, D), F32), pltpu.VMEM((2, 4, 2, WM), F32),
            pltpu.VMEM((2, BLK, D), BF16), pltpu.VMEM((2, BLK, D), BF16), pltpu.VMEM((2, 16, D), F32),
            pltpu.VMEM((3, 4, 4, 4, 2, 512), F32), pltpu.VMEM((3, 4, 4, 4, 2, 256), F32),
            pltpu.VMEM((3, 4, 8, HALF), F32),
            pltpu.VMEM((3, D, 512), BF16), pltpu.VMEM((3, 512, WS), BF16), pltpu.VMEM((3, 4, 384, WS), BF16),
            pltpu.VMEM((3, 3, 384, WS), BF16), pltpu.VMEM((3, 3, 96, WS), BF16),
            pltpu.VMEM((3, 4, 32, WS), BF16), pltpu.VMEM((3, 4, 32, WS), BF16),
            pltpu.VMEM((3, D, 512), BF16), pltpu.VMEM((3, 512, WM), BF16),
            pltpu.VMEM((3, 4, 32, WM), BF16), pltpu.VMEM((3, 4, 32, WM), BF16),
            dma((8,)), dma((6,)), dma((3,)), dma((5,)), dma((6,)), dma((6,)),
            dma((2, 3)), dma((2, 3)), dma((3,)), dma((3,)),
            dma((4,)), dma((4,)), dma((2,)), dma((2,)), dma((5,)), dma((5,)),
            dma((10,)), dma((10,)), dma((5,)), dma((5,)), dma((2,)), dma((2,)),
            dma((2,)), dma((2,)), dma((2,)),
        ],
        compiler_params=pltpu.CompilerParams(collective_id=1, has_side_effects=True, vmem_limit_bytes=LIMIT),
        name="layer",
    )(seq_lengths, block_slots, mixgain, glugain, taps, tokens, cotangent, inproj, outproj, gate_w, lift_w, down_w)


def place_kernel(*refs):
    ins, outs, held, in_sems, out_sems = refs[:8], refs[8:18], refs[18:26], refs[26], refs[27]
    loads = [pltpu.make_async_copy(a, b, in_sems.at[i]) for i, (a, b) in enumerate(zip(ins, held))]
    for c in loads:
        c.start()
    gains = held[2]
    parts = [held[0], held[1], gains.at[0], gains.at[1], gains.at[pl.ds(2, 3)], *held[3:]]
    stores = []
    for i, (a, b) in enumerate(zip(parts, outs)):
        if i not in (3, 4):
            loads[i if i < 3 else i - 2].wait()
        stores.append(pltpu.make_async_copy(a, b, out_sems.at[i]))
        stores[-1].start()
    for c in stores:
        c.wait()


def place_outputs(results):
    hbm = pl.BlockSpec(memory_space=pl.ANY)
    shape = jax.ShapeDtypeStruct
    return pl.pallas_call(
        place_kernel,
        out_shape=[shape((BLK, D), BF16), shape((BLK, D), BF16), shape((HALF,), F32), shape((HALF,), F32), shape((3, HALF), F32)]
        + [shape(s, F32) for s in ((24, FF), (24, FF), (24, FF), (3, 24, HALF), (24, HALF))],
        in_specs=[hbm] * 8,
        out_specs=[hbm] * 10,
        scratch_shapes=[pltpu.VMEM(r.shape, r.dtype) for r in results] + [pltpu.SemaphoreType.DMA((8,)), pltpu.SemaphoreType.DMA((10,))],
        name="place",
    )(*results)


def on_device(
    tokens, cotangent, seq_lengths, block_slots, mixgain, inproj, conv_taps, outproj, glugain, gate_weight, lift_weight, down_weight
):
    results = run_layer(
        seq_lengths, block_slots, mixgain, glugain, conv_taps,
        tokens, cotangent, inproj, outproj, gate_weight, lift_weight, down_weight,
    )
    layer_out, input_grad, mixgain_grad, glugain_grad, taps_grad, gate_grad, lift_grad, down_rows, inproj_grad, out_rows = place_outputs(results)
    return (
        layer_out, input_grad, mixgain_grad, inproj_grad, taps_grad, out_rows.T, glugain_grad, gate_grad, lift_grad, down_rows.T,
    )


def solution(mesh):
    in_specs = (
        P("seq", None), P("seq", None), P(), P(), P(), P(None, None, "ch"), P(None, "ch"), P("ch", None),
        P(), P(None, "ch"), P(None, "ch"), P("ch", None),
    )
    out_specs = (
        P("seq", None), P("seq", None), P("ch"), P(None, "seq", "ch"), P(None, "ch"), P("ch", "seq"),
        P("ch"), P("seq", "ch"), P("seq", "ch"), P("ch", "seq"),
    )
    return jax.shard_map(on_device, mesh=mesh, in_specs=in_specs, out_specs=out_specs, check_vma=False)
```

```python
import jax
import jax.numpy as jnp
from jax import lax
from jax.experimental import pallas as pl
from jax.experimental.pallas import tpu as pltpu
from jax.sharding import PartitionSpec as P

MESH = pl.DeviceIdType.MESH
F32, BF16 = jnp.float32, jnp.bfloat16
BLK, D, HALF, FF = 128, 1536, 768, 3456
WS, WM = 896, 256
STEPS, SPAN = 7, 512
EPS = 1e-05
LIMIT = 64 * 1024 * 1024 - 256 * 1024
ROUTES = ((2, 1, 0), (0, 2, 1), (1, 0, 2))
GROUPS = (((0, 256), (256, 256), (512, 256), (768, 128)), ((0, 256),))


def dot_nt(a, b):
    return lax.dot_general(a, b, (((1,), (1,)), ((), ())), preferred_element_type=F32)


def outer(a, b):
    return lax.dot_general(a, b, (((0,), (0,)), ((), ())), preferred_element_type=F32)


def dot_nn(a, b):
    return jnp.dot(a, b, preferred_element_type=F32)


def span(s):
    return min(SPAN, FF - SPAN * s)


def layer_kernel(
    seq_lengths, block_slots, mixgain_1d, glugain_1d, taps,
    tokens, cotangent, inproj, outproj, gate_w, lift_w, down_w,
    o_layer, o_input, o_gains, o_gate, o_lift, o_down, o_in, o_out,
    mixgain, glugain, tok_v, cot_v, n_v, b_v, c_v, x_v, v_v, u_v, y_v, h2_v, glu_v, dn2_v,
    col, down_ring, out_v, da_v, act, mixed_r, s_src, m_src, e_src, eb_v, ex_v, er_src, er_two, e_left, e_right, xh_send, xh_recv, xs_send, tails, heads, gain_land,
    s_left, s_right, s_bsend, s_bland, s_cland, s_dsend, s_dland, m_left, m_right, m_dsend, m_dland,
    load_sem, col_sem, down_sem, store_sem, x_send, x_recv, halo_send, halo_recv, gain_send, gain_recv,
    l_send, l_recv, f_send, f_recv, r_send, r_recv,
    b_send, b_recv, c_send, c_recv, d_send, d_recv, e_send, e_recv, own_edge,
):
    seq, core = lax.axis_index("seq"), lax.axis_index("ch")
    place = (seq // 16, (seq // 4) % 4, seq % 4)

    def peer(axis, step):
        at = [(place[i] + step) % 4 if i == axis else place[i] for i in range(3)]
        return at[0] * 16 + at[1] * 4 + at[2]

    def local(src, dst, sem):
        return pltpu.make_async_copy(src, dst, sem)

    def link(src, dst, send, recv, axis, step):
        return pltpu.make_async_remote_copy(
            src_ref=src, dst_ref=dst, send_sem=send, recv_sem=recv,
            device_id=(peer(axis, step), core), device_id_type=MESH)

    def cross(src, dst, send, recv):
        return pltpu.make_async_remote_copy(
            src_ref=src, dst_ref=dst, send_sem=send, recv_sem=recv,
            device_id=(seq, 1 - core), device_id_type=MESH)

    def started(copies):
        for c in copies:
            c.start()
        return copies

    def waited(copies):
        for c in copies:
            c.wait()

    def all_of(view, sem):
        local(view, view, sem).wait()

    def all_links(view, send, recv):
        link(view, view, send, recv, 0, 1).wait()

    tok_load = local(tokens, tok_v, load_sem.at[0])
    cot_load = local(cotangent, cot_v, load_sem.at[1])
    out_load = local(outproj, out_v, load_sem.at[2])
    gain_loads = [local(mixgain_1d, mixgain.at[0], load_sem.at[3]), local(glugain_1d, glugain.at[0], load_sem.at[4])]
    in_loads = [local(inproj.at[k], col.at[k, :, pl.ds(0, HALF)], col_sem.at[3 + k]) for k in range(3)]
    tok_load.start()
    started(gain_loads)
    in_loads[0].start()
    in_loads[2].start()
    in_loads[1].start()

    def pair_loads(s):
        slot, w = (s + 1) % 3, span(s)
        return [
            local(weight.at[:, pl.ds(SPAN * s, w)], col.at[slot, :, pl.ds(w * m, w)], col_sem.at[slot])
            for m, weight in enumerate((gate_w, lift_w))]

    def down_loads(t):
        s, slot = t % STEPS, t % 3
        return [local(down_w.at[pl.ds(SPAN * s, span(s)), :], down_ring.at[slot, pl.ds(0, span(s)), :], down_sem.at[slot])]

    def pair_ready(s):
        all_of(col.at[(s + 1) % 3, :, pl.ds(0, 2 * span(s))], col_sem.at[(s + 1) % 3])

    def down_ready(t):
        all_of(down_ring.at[t % 3, pl.ds(0, span(t % STEPS)), :], down_sem.at[t % 3])

    barrier = pltpu.get_barrier_semaphore()
    for axis in range(3):
        for step in range(1, 4):
            pl.semaphore_signal(barrier, inc=1, device_id=(peer(axis, step), core), device_id_type=MESH)
    pl.semaphore_signal(barrier, inc=1, device_id=(seq, 1 - core), device_id_type=MESH)

    block = jnp.int32(0)
    for i in range(64):
        block = jnp.where(block_slots[i] == seq, i, block)
    before = block_slots[jnp.maximum(block - 1, 0)]
    after = block_slots[jnp.minimum(block + 1, 63)]
    has_after = (block < 63).astype(F32)
    rows = lax.broadcasted_iota(jnp.int32, (BLK, 1), 0)
    positions = block * BLK + rows
    start = jnp.zeros((BLK, 1), jnp.int32)
    offset = jnp.int32(0)
    for i in range(4):
        start = jnp.where(offset <= positions, offset, start)
        offset = offset + seq_lengths[i]
    mask1 = (positions - 1 >= start).astype(F32)
    mask2 = (positions - 2 >= start).astype(F32)

    def halo_links(land, job, phase):
        out = []
        for k in range(3):
            where = [pl.ds(0, 4) if axis in ROUTES[k][:phase] else pl.ds(place[axis], 1) for axis in range(3)]
            view = land.at[k, where[0], where[1], where[2]]
            axis = ROUTES[k][phase]
            for step in range(1, 4):
                out.append(link(view, view, halo_send.at[job, phase], halo_recv.at[job, phase], axis, step))
        return out

    def halo_ready(land, job, phase):
        view = (land.at[:, pl.ds(0, 3), 0, 0], land.at[:, pl.ds(0, 3), :, 0], land.at[:, pl.ds(0, 3)])[phase]
        all_links(view, halo_send.at[job, phase], halo_recv.at[job, phase])

    def halo_rows(land, slot):
        at = (slot // 16, (slot // 4) % 4, slot % 4)
        return jnp.concatenate([land[k, at[0], at[1], at[2]] for k in range(3)], axis=1)

    def put_halo(land, two):
        width = two.shape[1] // 3
        for k in range(3):
            land[k, place[0], place[1], place[2]] = two[:, width * k:width * k + width]

    def first_norm(values):
        scale = lax.rsqrt(jnp.mean(values * values, axis=1, keepdims=True) + EPS)
        return scale, values * scale * mixgain[...]

    tok_load.wait()
    put_halo(tails, tok_v[BLK - 16:BLK, :].astype(F32)[14:16])
    pl.semaphore_wait(barrier, 10)
    started(halo_links(tails, 0, 0))
    waited(gain_loads)
    scale_a, n1 = first_norm(tok_v[...].astype(F32))
    n_v[...] = n1.astype(BF16)
    in_loads[0].wait()
    b_v[...] = dot_nn(n_v[...], col[0, :, :HALF])
    started([cot_load])
    for s in range(3):
        started(down_loads(s))
    halo_ready(tails, 0, 0)
    started(halo_links(tails, 0, 1))
    in_loads[2].wait()
    x_v[...] = dot_nn(n_v[...], col[2, :, :HALF])
    v_v[...] = (b_v[...] * x_v[...]).astype(BF16).astype(F32)
    in_loads[1].wait()
    c_v[...] = dot_nn(n_v[...], col[1, :, :HALF])
    started(pair_loads(0))
    cot_load.wait()

    def hidden_grads(first, end):
        for s in range(first, end):
            down_ready(s)
            da_v[:, SPAN * s:SPAN * s + span(s)] = dot_nt(cot_v[...], down_ring[s % 3, :span(s), :])
            started(down_loads(s + 3))

    halo_ready(tails, 0, 1)
    started(halo_links(tails, 0, 2))
    s_src[1] = cot_v[...].T
    m_src[0] = n_v[...].T

    half = pl.ds(pl.multiple_of(core * HALF, HALF), HALF)

    def left_link(job, k, src, step):
        left = (s_left, m_left)[job]
        sem = 1 if job == 1 else 2 + step // 2
        return link(src.at[half, :], left.at[k, half, pl.ds(128 * step, 128)],
                    l_send.at[sem], l_recv.at[sem], k, step)

    def send_left_s(k):
        src = s_src.at[1 if k == 2 else 0]
        s_left[k, :, :128] = src[...]
        for step in (1, 3):
            left_link(0, k, src, step).start()

    def hand_on():
        for n, step in enumerate((1, 3)):
            all_links(s_left.at[:, half, pl.ds(128 * step, 128)], l_send.at[2 + n], l_recv.at[2 + n])
            part = pl.ds(pl.multiple_of(core * HALF + 384 * n, 384), 384)
            for k in range(3):
                link(s_left.at[k, part, pl.ds(128 * step, 128)], s_left.at[k, part, pl.ds(256, 128)],
                     l_send.at[0], l_recv.at[0], k, step).start()

    def send_left_m(k, which):
        for step in range(1, 4):
            @pl.when(((place[k] + step) % 4 == 3) == (which == 1))
            def _():
                left_link(1, k, m_src.at[which], step).start()

    def others(job):
        return (s_left, m_left)[job].at[:, half, pl.ds(128, 384)]

    def forward_left(job):
        if job == 0:
            all_links(s_left.at[:, half, pl.ds(256, 128)], l_send.at[0], l_recv.at[0])
        else:
            all_links(others(1), l_send.at[1], l_recv.at[1])
        cross(others(job), others(job), f_send.at[job], f_recv.at[job]).start()

    started([out_load])
    hidden_grads(0, 4)

    halo_ready(tails, 0, 2)
    send_left_s(2)
    for k in range(3):
        send_left_m(k, 0)
    last_two = jnp.concatenate([halo_rows(tails, before), jnp.zeros((14, D), F32)], axis=0)
    edge_scale, edge = first_norm(last_two)
    xs_send[1] = last_two * edge_scale
    edge = edge.astype(BF16)
    edge_b, edge_x = dot_nn(edge, col[0, :, :HALF]), dot_nn(edge, col[2, :, :HALF])
    carried = (edge_b * edge_x).astype(BF16).astype(F32)
    e_src[...] = edge.astype(F32)[0:2]
    eb_v[...] = edge_b
    ex_v[...] = edge_x

    def edge_left_links(n):
        return [
            link(e_src, e_left.at[n, step], e_send.at[0], e_recv.at[0], 2 * n, step)
            for step in range(1, 4)]

    def edge_piece(n, i):
        return er_two.at[n, :, pl.ds(pl.multiple_of(i * WM, WM), WM)]

    def edge_right_links(n):
        return [
            link(edge_piece(n, (place[2 * n] + step) % 4), e_right.at[n, step],
                 e_send.at[1], e_recv.at[1], 2 * n, step)
            for step in range(1, 4)]

    def edge_own(n):
        return [
            local(e_src, e_left.at[n, 0], own_edge.at[0]),
            local(edge_piece(n, place[2 * n]), e_right.at[n, 0], own_edge.at[1])]
    for s in range(1, 3):
        started(pair_loads(s))
    row_is0, row_is1 = rows == 0, rows == 1
    tap0, tap1, tap2 = taps[0:1, :], taps[1:2, :], taps[2:3, :]

    def shifted():
        v = v_v[...]
        one = jnp.where(row_is0, carried[1:2], pltpu.roll(v, 1, 0)) * mask1
        two = jnp.where(row_is0, carried[0:1], jnp.where(row_is1, carried[1:2], pltpu.roll(v, 2, 0))) * mask2
        return v, one, two

    v0, v1, v2 = shifted()
    u_v[...] = tap0 * v0 + tap1 * v1 + tap2 * v2
    y_v[...] = (c_v[...] * u_v[...]).astype(BF16)
    out_load.wait()
    dn2_v[...] = dot_nn(y_v[...], out_v[...])
    swap = cross(dn2_v, h2_v, x_send.at[0], x_recv.at[0])
    swap.start()
    hidden_grads(4, 6)
    swap.wait()
    h2_v[...] = tok_v[...].astype(F32) + (dn2_v[...] + h2_v[...])
    h2 = h2_v[...]
    scale_b = lax.rsqrt(jnp.mean(h2 * h2, axis=1, keepdims=True) + EPS)
    n_v[...] = (h2 * scale_b * glugain[...]).astype(BF16)
    s_src[0] = n_v[...].T
    send_left_s(0)
    send_left_s(1)

    lefts, rights, dsends, dlands = (s_left, m_left), (s_right, m_right), (s_dsend, m_dsend), (s_dland, m_dland)

    def right_piece(job, k, i, g):
        if job == 0:
            return act.at[k, i, :, pl.ds(*GROUPS[0][g])]
        return mixed_r.at[k, :, pl.ds(pl.multiple_of(i * WM, WM), WM)]

    def right_links(job, k, g):
        lanes = pl.ds(*GROUPS[job][g])
        return [
            link(right_piece(job, k, (place[k] + step) % 4, g), rights[job].at[k, pl.ds(128 * step, 128), lanes],
                 r_send.at[4 * job + g], r_recv.at[4 * job + g], k, step)
            for step in range(1, 4)]

    def send_right(job, g):
        for k in range(3):
            started(right_links(job, k, g))
        first, width = GROUPS[job][g]
        for k in range(3):
            rights[job][k, :128, first:first + width] = right_piece(job, k, place[k], g)[...]

    def b_out(job, k, j, g, row=0, count=384):
        lanes = pl.ds(*GROUPS[job][g])
        if job == 0:
            return s_bsend.at[k, j, pl.ds(row, count), lanes]
        return col.at[1, pl.ds(pl.multiple_of(384 * j + row, 96), count), pl.ds(WM * k, WM)]

    def b_in(job, k, i, g, row=0, count=384):
        if job == 0:
            return s_bland.at[k, i, pl.ds(row, count), pl.ds(*GROUPS[job][g])]
        return down_ring.at[i, pl.ds(row, count), pl.ds(WM * k, WM)]

    def c_out(job, k, j, g, row=0, count=96):
        return rights[job].at[k, pl.ds(pl.multiple_of(96 * j + row, 48), count), pl.ds(*GROUPS[job][g])]

    def c_in(job, k, i, g):
        if job == 0:
            return s_cland.at[k, i, :, pl.ds(*GROUPS[job][g])]
        return down_ring.at[i, pl.ds(0, 96), pl.ds(HALF + WM * k, WM)]

    LOW, HIGH = 0, 192

    def b_links(job, k, g, which):
        axis = (k + 1) % 3
        me = place[axis]
        opposite, ahead, behind = (me + 2) % 4, (me + 1) % 4, (me + 3) % 4
        table = (
            (opposite, LOW, 2, 1), (ahead, HIGH, 0, 1), (opposite, HIGH, 2, 3),
            (behind, LOW, 1, 3), (ahead, LOW, 0, 1), (behind, HIGH, 1, 3))
        out = []
        for n in which:
            part, row, land, step = table[n]
            sem = 2 * (4 * job + g) + (land != 2)
            out.append(link(b_out(job, k, part, g, row, 192), b_in(job, k, land, g, row, 192),
                            b_send.at[sem], b_recv.at[sem], axis, step))
        return out

    def c_links(job, k, g):
        axis = (k + 2) % 3
        return [
            link(c_out(job, k, (place[axis] + step) % 4, g), c_in(job, k, step - 1, g),
                 c_send.at[4 * job + g], c_recv.at[4 * job + g], axis, step)
            for step in range(1, 4)]

    def right_ready(job, g):
        lanes, n = pl.ds(*GROUPS[job][g]), 4 * job + g
        all_links(rights[job].at[:, pl.ds(128, 384), lanes], r_send.at[n], r_recv.at[n])

    def edges_ready():
        all_of(e_left.at[:, 0], own_edge.at[0])
        all_of(e_right.at[:, 0], own_edge.at[1])
        all_links(e_left.at[:, pl.ds(1, 3)], e_send.at[0], e_recv.at[0])
        all_links(e_right.at[:, pl.ds(1, 3)], e_send.at[1], e_recv.at[1])

    def edge_tile(parts):
        return jnp.concatenate([*parts, jnp.zeros((8, parts[0].shape[1]), F32)], axis=0).astype(BF16)

    def start_b(job, k, g):
        lanes = pl.ds(*GROUPS[job][g])
        edges = job == 1 and k != 1

        def slab(x, carry):
            at = pl.ds(pl.multiple_of(x * 384, 384), 384)
            acc = dot_nn(lefts[job][k, at, :], rights[job][k, :, lanes])
            if edges:
                acc = acc + outer(edge_tile([e_left[k // 2, i, :, at] for i in range(4)]), edge_tile([e_right[k // 2, i] for i in range(4)]))
            row = pl.multiple_of(96 * x, 96)
            for j in range(4):
                if k == 0:
                    b_out(job, k, j, g, row, 96)[...] = acc[96 * j:96 * j + 96].astype(BF16)
                elif k == 1:
                    parts = [acc[96 * y + 24 * j:96 * y + 24 * j + 24] for y in range(4)]
                    b_out(job, k, j, g, row, 96)[...] = jnp.concatenate(parts, axis=0).astype(BF16)
                else:
                    b_out(job, k, x, g, 96 * j, 96)[...] = acc[96 * j:96 * j + 96].astype(BF16)
            return carry

        lax.fori_loop(0, 4, slab, 0)
        started(b_links(job, k, g, range(4)))

    def b_ready(job, g, last):
        sem = 2 * (4 * job + g) + last
        if job == 0:
            view = s_bland.at[:, pl.ds(0, 2) if last else pl.ds(2, 1), :, pl.ds(*GROUPS[job][g])]
        else:
            view = down_ring.at[pl.ds(0, 2) if last else pl.ds(2, 1), pl.ds(0, 384), pl.ds(0, HALF)]
        all_links(view, b_send.at[sem], b_recv.at[sem])

    def pass_on(job, k, g):
        me = place[(k + 1) % 3]
        for step, row in ((1, LOW), (3, HIGH)):
            own, via = b_out(job, k, (me + step) % 4, g, row, 192), b_in(job, k, 2, g, row, 192)
            own[...] = (own[...].astype(F32) + via[...].astype(F32)).astype(BF16)
        started(b_links(job, k, g, (4, 5)))

    def c_halves(k, g, which):
        axis = (k + 2) % 3
        me = place[axis]
        opposite, ahead, behind = (me + 2) % 4, (me + 1) % 4, (me + 3) % 4
        table = ((opposite, 0, 2, 1), (ahead, 48, 0, 1), (opposite, 48, 2, 3), (behind, 0, 1, 3), (ahead, 0, 0, 1), (behind, 48, 1, 3))
        out = []
        for n in which:
            part, row, land, step = table[n]
            sem = 5 + g if land == 2 else g
            out.append(link(c_out(0, k, part, g, row, 48), s_cland.at[k, land, pl.ds(row, 48), pl.ds(*GROUPS[0][g])],
                            c_send.at[sem], c_recv.at[sem], axis, step))
        return out

    def pass_on_c(g):
        lanes = pl.ds(*GROUPS[0][g])
        all_links(s_cland.at[:, pl.ds(2, 1), :, lanes], c_send.at[5 + g], c_recv.at[5 + g])
        for k in range(3):
            for step, row in ((1, 0), (3, 48)):
                mine, via = c_out(0, k, (place[(k + 2) % 3] + step) % 4, g, row, 48), s_cland.at[k, 2, pl.ds(row, 48), lanes]
                mine[...] = (mine[...].astype(F32) + via[...].astype(F32)).astype(BF16)
            started(c_halves(k, g, (4, 5)))

    def c_ready(job, g):
        if job == 0:
            view = s_cland.at[:, pl.ds(0, 2 if g < 3 else 3), :, pl.ds(*GROUPS[job][g])]
        else:
            view = down_ring.at[:, pl.ds(0, 96), pl.ds(HALF, HALF)]
        all_links(view, c_send.at[4 * job + g], c_recv.at[4 * job + g])

    def start_c(job, k, g):
        me = place[(k + 1) % 3]

        def summed(q):
            total = b_out(job, k, me, g, 96 * q, 96)[...].astype(F32)
            for i in range(2):
                total = total + b_in(job, k, i, g, 96 * q, 96)[...].astype(F32)
            return total

        if k == 0:
            for p in range(2):
                a, b = summed(2 * p), summed(2 * p + 1)
                for j in range(4):
                    both = jnp.concatenate([a[24 * j:24 * j + 24], b[24 * j:24 * j + 24]], axis=0)
                    c_out(job, k, j, g, 48 * p, 48)[...] = both.astype(BF16)
        else:
            for q in range(4):
                c_out(job, k, q, g)[...] = summed(q).astype(BF16)
        started(c_halves(k, g, range(4)) if job == 0 and g < 3 else c_links(job, k, g))

    def d_links(job, k):
        return [
            link(dsends[job].at[k, (place[k] + step) % 4], dlands[job].at[k, step],
                 d_send.at[job], d_recv.at[job], k, step)
            for step in range(1, 4)]

    def start_d(job, k):
        dsend, dland = dsends[job], dlands[job]
        for g, (first, width) in enumerate(GROUPS[job]):
            total = c_out(job, k, place[(k + 2) % 3], g)[...].astype(F32)
            for i in range(2 if job == 0 and g < 3 else 3):
                total = total + c_in(job, k, i, g)[...].astype(F32)
            pad = jnp.zeros((8, width), F32)
            for j in range(4):
                dsend[k, j, :, first:first + width] = jnp.concatenate([total[24 * j:24 * j + 24], pad], axis=0).astype(BF16)
        dland[k, 0] = dsend[k, place[k]]
        started(d_links(job, k))

    def finish(job, k):
        pieces = [dlands[job][k, (place[k] - i + 4) % 4].astype(F32)[:24] for i in range(4)]
        if job == 0:
            for i in range(4):
                for s in range(STEPS):
                    if SPAN * s + 128 * i < FF:
                        da_v[32 * k:32 * k + 24, SPAN * s + 128 * i:SPAN * s + 128 * i + 128] = pieces[i][:, 128 * s:128 * s + 128]
            local(da_v.at[pl.ds(32 * k, 24), :], (o_gate, o_lift, o_down)[k], store_sem.at[k]).start()
        else:
            stage = (h2_v, glu_v, dn2_v)[k]
            for i in range(4):
                stage[:24, WM * i:WM * i + WM] = pieces[i]
            local(stage.at[pl.ds(0, 24), pl.ds(0, HALF)], o_in.at[k], store_sem.at[3]).start()
            local(stage.at[pl.ds(0, 24), pl.ds(HALF, WM)], o_out.at[:, pl.ds(WM * k, WM)], store_sem.at[4]).start()

    glu_v[...] = jnp.zeros_like(glu_v)
    dn2_v[...] = jnp.zeros_like(dn2_v)

    def swiglu_step(s):
        slot = (s + 1) % 3
        pair_ready(s)
        w = span(s)
        both = dot_nn(n_v[...], col[slot, :, :2 * w])
        gate_pre, lift_pre = both[:, :w], both[:, w:]
        hidden_grad = da_v[:, SPAN * s:SPAN * s + w]
        sig = jax.nn.sigmoid(gate_pre)
        silu = gate_pre * sig
        hidden = (silu * lift_pre).astype(BF16)
        d_lift = (hidden_grad * silu).astype(BF16)
        d_gate = (hidden_grad * lift_pre * sig * (1.0 + gate_pre * (1.0 - sig))).astype(BF16)
        for k, values in enumerate((d_gate, d_lift, hidden)):
            for i in range(4):
                part = values[:, 128 * i:128 * i + 128] if 128 * i < w else jnp.zeros((BLK, 128), BF16)
                act[k, i, :, 128 * s:128 * s + 128] = part
        down_ready(STEPS + s)
        glu_v[...] += dot_nn(hidden, down_ring[(STEPS + s) % 3, :w, :])
        dn2_v[...] += dot_nt(jnp.concatenate([d_gate, d_lift], axis=1), col[slot, :, :2 * w])
        if s + 3 < STEPS:
            started(pair_loads(s + 3))
            started(down_loads(STEPS + s + 3))

    def left_ready(job):
        cross(others(job), others(job), f_send.at[job], f_recv.at[job]).wait()

    hidden_grads(6, STEPS)
    for s in range(2):
        swiglu_step(s)
    send_right(0, 0)
    swiglu_step(2)
    hand_on()
    swiglu_step(3)
    send_right(0, 1)
    forward_left(0)
    swiglu_step(4)
    left_ready(0)
    right_ready(0, 0)
    for k in range(3):
        start_b(0, k, 0)
    swiglu_step(5)
    send_right(0, 2)
    right_ready(0, 1)
    for k in range(3):
        start_b(0, k, 1)
    b_ready(0, 0, 0)
    for k in range(3):
        pass_on(0, k, 0)
    swiglu_step(6)
    send_right(0, 3)
    started(in_loads)

    xh_send[0] = dn2_v[...].astype(BF16)
    swap_dn2 = cross(xh_send.at[0], xh_recv.at[0], x_send.at[1], x_recv.at[1])
    swap_dn2.start()
    xh_send[1] = glu_v[...].astype(BF16)
    swap_glu = cross(xh_send.at[1], xh_recv.at[1], x_send.at[2], x_recv.at[2])
    swap_glu.start()
    swap_dn2.wait()
    h2 = h2_v[...]
    z2 = h2 * scale_b
    dn2 = xh_send[0].astype(F32) + xh_recv[0].astype(F32)
    glu_term = jnp.sum(dn2 * z2, axis=0, keepdims=True)
    scaled = dn2 * glugain[...]
    glu_v[...] = cot_v[...].astype(F32) + scale_b * (scaled - z2 * jnp.mean(scaled * z2, axis=1, keepdims=True))
    n_v[...] = glu_v[...].astype(BF16)
    dy = dot_nt(n_v[...], out_v[...])
    d_c = (dy * u_v[...]).astype(BF16)
    du = dy * c_v[...]
    v0, v1, v2 = shifted()
    tap_terms = [jnp.sum(du * v, axis=0, keepdims=True) for v in (v0, v1, v2)]
    w1, w2 = tap1 * (du * mask1), tap2 * (du * mask2)
    two = jnp.concatenate([w2[0:1], w1[0:1] + w2[1:2]], axis=0)
    put_halo(heads, two)
    started(halo_links(heads, 1, 0))
    dv = (tap0 * du + jnp.where(rows < 127, pltpu.roll(w1, 127, 0), 0.0)
          + jnp.where(rows < 126, pltpu.roll(w2, 126, 0), 0.0))
    mixed_r[0, :, :HALF] = (dv * x_v[...]).astype(BF16)
    mixed_r[1, :, :HALF] = d_c
    mixed_r[2, :, :HALF] = (dv * b_v[...]).astype(BF16)
    y_out = y_v[...]
    for k in range(3):
        mixed_r[k, :, HALF:] = y_out[:, 256 * k:256 * k + 256]
    share = jnp.concatenate([two, jnp.zeros((14, HALF), F32)], axis=0)
    none = jnp.zeros((16, WM), BF16)
    for n, other in enumerate((ex_v, eb_v)):
        er_src[n] = jnp.concatenate([(share * other[...]).astype(BF16), none], axis=1)
        er_two[n] = er_src[n].astype(F32)[0:2]
    send_right(1, 0)
    for n in range(2):
        started(edge_own(n))
        started(edge_left_links(n))
        started(edge_right_links(n))
    m_src[1] = n_v[...].T
    for k in range(3):
        send_left_m(k, 1)
        m_left[k, :, :128] = m_src[jnp.where(place[k] == 3, 1, 0)]
    b_ready(0, 1, 0)
    for k in range(3):
        pass_on(0, k, 1)
    right_ready(0, 2)
    for k in range(3):
        start_b(0, k, 2)
    swap_glu.wait()
    xh_send[1] = (h2_v[...] + (xh_send[1].astype(F32) + xh_recv[1].astype(F32))).astype(BF16)
    stores = started([local(xh_send.at[1], o_layer, load_sem.at[5])])
    b_ready(0, 0, 1)
    for k in range(3):
        start_c(0, k, 0)

    def my_half(row):
        return jnp.where(core == 0, row[:, :HALF], row[:, HALF:])

    def gain_links(axis):
        view = gain_land.at[axis, place[axis]]
        return [link(view, view, gain_send.at[axis], gain_recv.at[axis], axis, step) for step in range(1, 4)]

    def gain_sum(axis):
        all_links(gain_land.at[axis, pl.ds(0, 3)], gain_send.at[axis], gain_recv.at[axis])
        return (gain_land[axis, 0] + gain_land[axis, 1]) + (gain_land[axis, 2] + gain_land[axis, 3])

    def input_rows(dn1, first):
        z1 = tok_v[first:, :].astype(F32) * scale_a[first:]
        scaled = dn1 * mixgain[...]
        n_v[first:, :] = (glu_v[first:, :] + scale_a[first:] * (scaled - z1 * jnp.mean(scaled * z1, axis=1, keepdims=True))).astype(BF16)
        return z1

    waited(in_loads)
    for k in range(3):
        part = dot_nt(mixed_r[k, :, :HALF], col[k, :, :HALF])
        if k == 0:
            dn2_v[...] = part
        else:
            dn2_v[...] += part
    ahead = dot_nt(er_src[0, :, :HALF], col[0, :, :HALF]) + dot_nt(er_src[1, :, :HALF], col[2, :, :HALF])
    swap_dn1 = cross(dn2_v, da_v.at[:, pl.ds(0, D)], x_send.at[3], x_recv.at[3])
    swap_dn1.start()
    xs_send[0] = jnp.concatenate([jnp.sum(ahead * xs_send[1], axis=0, keepdims=True), jnp.zeros((15, D), F32)], axis=0)
    swap_row = cross(xs_send.at[0], da_v.at[pl.ds(0, 16), pl.ds(D, D)], x_send.at[4], x_recv.at[4])
    swap_row.start()
    right_ready(0, 3)
    for k in range(3):
        start_b(0, k, 3)
    swap_dn1.wait()
    swap_row.wait()
    dn1 = dn2_v[...] + da_v[:, :D]
    z1 = input_rows(dn1, 0)
    mix_term = jnp.sum(dn1 * z1, axis=0, keepdims=True) + (xs_send[0, 0:1] + da_v[0:1, D:2 * D])
    gain_land[0, place[0]] = jnp.concatenate(
        [my_half(mix_term), my_half(glu_term), *tap_terms, jnp.zeros((3, HALF), F32)], axis=0)
    started(gain_links(0))
    forward_left(1)
    halo_ready(heads, 1, 0)
    started(halo_links(heads, 1, 1))
    left_ready(1)
    right_ready(1, 0)
    edges_ready()
    for k in range(3):
        start_b(1, k, 0)
    b_ready(0, 2, 0)
    for k in range(3):
        pass_on(0, k, 2)
    b_ready(0, 1, 1)
    for k in range(3):
        start_c(0, k, 1)
    b_ready(0, 3, 0)
    for k in range(3):
        pass_on(0, k, 3)
    pass_on_c(0)
    halo_ready(heads, 1, 1)
    started(halo_links(heads, 1, 2))
    gain_land[1, place[1]] = gain_sum(0)
    started(gain_links(1))
    b_ready(1, 0, 0)
    for k in range(3):
        pass_on(1, k, 0)
    pass_on_c(1)
    b_ready(0, 2, 1)
    for k in range(3):
        start_c(0, k, 2)
    b_ready(0, 3, 1)
    for k in range(3):
        start_c(0, k, 3)
    gain_land[2, place[2]] = gain_sum(1)
    started(gain_links(2))
    halo_ready(heads, 1, 2)
    incoming = jnp.concatenate([jnp.zeros((14, HALF), F32), halo_rows(heads, after) * has_after], axis=0)
    xs_send[1] = (dot_nt((incoming * x_v[BLK - 16:, :]).astype(BF16), col[0, :, :HALF])
                  + dot_nt((incoming * b_v[BLK - 16:, :]).astype(BF16), col[2, :, :HALF]))
    swap = cross(xs_send.at[1], da_v.at[pl.ds(16, 16), pl.ds(D, D)], x_send.at[5], x_recv.at[5])
    swap.start()
    b_ready(1, 0, 1)
    for k in range(3):
        start_c(1, k, 0)
    pass_on_c(2)
    swap.wait()
    input_rows((dn2_v[BLK - 16:, :] + da_v[BLK - 16:, :D]) + (xs_send[1] + da_v[16:32, D:2 * D]), BLK - 16)
    stores += started([local(n_v, o_input, load_sem.at[6])])
    v_v[0:8, :] = gain_sum(2)
    stores += started([local(v_v.at[pl.ds(0, 8), :], o_gains, load_sem.at[7])])
    for g in range(4):
        c_ready(0, g)
    for k in range(3):
        start_d(0, k)
    c_ready(1, 0)
    for k in range(3):
        start_d(1, k)
    for job in range(2):
        all_links(dlands[job].at[:, pl.ds(1, 3)], d_send.at[job], d_recv.at[job])
        for k in range(3):
            finish(job, k)
    for n, out in enumerate((o_gate, o_lift, o_down, o_in, o_out)):
        all_of(out, store_sem.at[n])
    waited(stores)


def run_layer(seq_lengths, block_slots, mixgain, glugain, taps, tokens, cotangent, inproj, outproj, gate_w, lift_w, down_w):
    vm = pl.BlockSpec(memory_space=pltpu.VMEM)
    sm = pl.BlockSpec(memory_space=pltpu.SMEM)
    hbm = pl.BlockSpec(memory_space=pl.ANY)
    dma = pltpu.SemaphoreType.DMA
    shape = jax.ShapeDtypeStruct
    row, full16, full32, half32 = (
        pltpu.VMEM((1, D), F32), pltpu.VMEM((BLK, D), BF16), pltpu.VMEM((BLK, D), F32), pltpu.VMEM((BLK, HALF), F32))
    return pl.pallas_call(
        layer_kernel,
        out_shape=[shape((BLK, D), BF16), shape((BLK, D), BF16), shape((8, HALF), F32)]
        + [shape(s, F32) for s in ((24, FF), (24, FF), (24, FF), (3, 24, HALF), (24, HALF))],
        in_specs=[sm, sm, hbm, hbm, vm] + [hbm] * 7,
        out_specs=[hbm] * 8,
        scratch_shapes=[
            row, row, full16, full16, full16,
            half32, half32, half32, half32, half32, pltpu.VMEM((BLK, HALF), BF16),
            full32, full32, full32,
            pltpu.VMEM((3, D, 2 * SPAN), BF16), pltpu.VMEM((3, SPAN, D), BF16), pltpu.VMEM((HALF, D), BF16),
            pltpu.VMEM((BLK, FF), F32), pltpu.VMEM((3, 4, BLK, WS), BF16), pltpu.VMEM((3, BLK, 4 * WM), BF16),
            pltpu.VMEM((2, D, BLK), BF16), pltpu.VMEM((2, D, BLK), BF16),
            pltpu.VMEM((2, D), F32), pltpu.VMEM((16, HALF), F32), pltpu.VMEM((16, HALF), F32),
            pltpu.VMEM((2, 16, 4 * WM), BF16), pltpu.VMEM((2, 2, 4 * WM), F32), pltpu.VMEM((2, 4, 2, D), F32), pltpu.VMEM((2, 4, 2, WM), F32),
            pltpu.VMEM((2, BLK, D), BF16), pltpu.VMEM((2, BLK, D), BF16), pltpu.VMEM((2, 16, D), F32),
            pltpu.VMEM((3, 4, 4, 4, 2, 512), F32), pltpu.VMEM((3, 4, 4, 4, 2, 256), F32),
            pltpu.VMEM((3, 4, 8, HALF), F32),
            pltpu.VMEM((3, D, 512), BF16), pltpu.VMEM((3, 512, WS), BF16), pltpu.VMEM((3, 4, 384, WS), BF16),
            pltpu.VMEM((3, 3, 384, WS), BF16), pltpu.VMEM((3, 3, 96, WS), BF16),
            pltpu.VMEM((3, 4, 32, WS), BF16), pltpu.VMEM((3, 4, 32, WS), BF16),
            pltpu.VMEM((3, D, 512), BF16), pltpu.VMEM((3, 512, WM), BF16),
            pltpu.VMEM((3, 4, 32, WM), BF16), pltpu.VMEM((3, 4, 32, WM), BF16),
            dma((8,)), dma((6,)), dma((3,)), dma((5,)), dma((6,)), dma((6,)),
            dma((2, 3)), dma((2, 3)), dma((3,)), dma((3,)),
            dma((4,)), dma((4,)), dma((2,)), dma((2,)), dma((5,)), dma((5,)),
            dma((10,)), dma((10,)), dma((8,)), dma((8,)), dma((2,)), dma((2,)),
            dma((2,)), dma((2,)), dma((2,)),
        ],
        compiler_params=pltpu.CompilerParams(collective_id=1, has_side_effects=True, vmem_limit_bytes=LIMIT),
        name="layer",
    )(seq_lengths, block_slots, mixgain, glugain, taps, tokens, cotangent, inproj, outproj, gate_w, lift_w, down_w)


def place_kernel(*refs):
    ins, outs, held, in_sems, out_sems = refs[:8], refs[8:18], refs[18:26], refs[26], refs[27]
    loads = [pltpu.make_async_copy(a, b, in_sems.at[i]) for i, (a, b) in enumerate(zip(ins, held))]
    for c in loads:
        c.start()
    gains = held[2]
    parts = [held[0], held[1], gains.at[0], gains.at[1], gains.at[pl.ds(2, 3)], *held[3:]]
    stores = []
    for i, (a, b) in enumerate(zip(parts, outs)):
        if i not in (3, 4):
            loads[i if i < 3 else i - 2].wait()
        stores.append(pltpu.make_async_copy(a, b, out_sems.at[i]))
        stores[-1].start()
    for c in stores:
        c.wait()


def place_outputs(results):
    hbm = pl.BlockSpec(memory_space=pl.ANY)
    shape = jax.ShapeDtypeStruct
    return pl.pallas_call(
        place_kernel,
        out_shape=[shape((BLK, D), BF16), shape((BLK, D), BF16), shape((HALF,), F32), shape((HALF,), F32), shape((3, HALF), F32)]
        + [shape(s, F32) for s in ((24, FF), (24, FF), (24, FF), (3, 24, HALF), (24, HALF))],
        in_specs=[hbm] * 8,
        out_specs=[hbm] * 10,
        scratch_shapes=[pltpu.VMEM(r.shape, r.dtype) for r in results] + [pltpu.SemaphoreType.DMA((8,)), pltpu.SemaphoreType.DMA((10,))],
        name="place",
    )(*results)


def on_device(
    tokens, cotangent, seq_lengths, block_slots, mixgain, inproj, conv_taps, outproj, glugain, gate_weight, lift_weight, down_weight
):
    results = run_layer(
        seq_lengths, block_slots, mixgain, glugain, conv_taps,
        tokens, cotangent, inproj, outproj, gate_weight, lift_weight, down_weight,
    )
    layer_out, input_grad, mixgain_grad, glugain_grad, taps_grad, gate_grad, lift_grad, down_rows, inproj_grad, out_rows = place_outputs(results)
    return (
        layer_out, input_grad, mixgain_grad, inproj_grad, taps_grad, out_rows.T, glugain_grad, gate_grad, lift_grad, down_rows.T,
    )


def solution(mesh):
    in_specs = (
        P("seq", None), P("seq", None), P(), P(), P(), P(None, None, "ch"), P(None, "ch"), P("ch", None),
        P(), P(None, "ch"), P(None, "ch"), P("ch", None),
    )
    out_specs = (
        P("seq", None), P("seq", None), P("ch"), P(None, "seq", "ch"), P(None, "ch"), P("ch", "seq"),
        P("ch"), P("seq", "ch"), P("seq", "ch"), P("ch", "seq"),
    )
    return jax.shard_map(on_device, mesh=mesh, in_specs=in_specs, out_specs=out_specs, check_vma=False)
```

```python
import jax
import jax.numpy as jnp
from jax import lax
from jax.experimental import pallas as pl
from jax.experimental.pallas import tpu as pltpu
from jax.sharding import PartitionSpec as P

MESH = pl.DeviceIdType.MESH
F32, BF16 = jnp.float32, jnp.bfloat16
BLK, D, HALF, FF = 128, 1536, 768, 3456
WS, WM = 896, 256
STEPS, SPAN = 7, 512
EPS = 1e-05
LIMIT = 64 * 1024 * 1024 - 256 * 1024
ROUTES = ((2, 1, 0), (0, 2, 1), (1, 0, 2))
GROUPS = (((0, 256), (256, 256), (512, 256), (768, 128)), ((0, 256),))


def dot_nt(a, b):
    return lax.dot_general(a, b, (((1,), (1,)), ((), ())), preferred_element_type=F32)


def outer(a, b):
    return lax.dot_general(a, b, (((0,), (0,)), ((), ())), preferred_element_type=F32)


def dot_nn(a, b):
    return jnp.dot(a, b, preferred_element_type=F32)


def span(s):
    return min(SPAN, FF - SPAN * s)


def layer_kernel(
    seq_lengths, block_slots, mixgain_1d, glugain_1d, taps,
    tokens, cotangent, inproj, outproj, gate_w, lift_w, down_w,
    o_layer, o_input, o_gains, o_gate, o_lift, o_down, o_in, o_out,
    mixgain, glugain, tok_v, cot_v, n_v, b_v, c_v, x_v, v_v, u_v, y_v, h2_v, glu_v, dn2_v,
    col, down_ring, out_v, da_v, act, mixed_r, s_src, m_src, e_src, eb_v, ex_v, er_src, er_two, e_left, e_right, xh_send, xh_recv, xs_send, tails, heads, gain_land,
    s_left, s_right, s_bsend, s_bland, s_cland, s_dsend, s_dland, m_left, m_right, m_dsend, m_dland,
    load_sem, col_sem, down_sem, store_sem, x_send, x_recv, halo_send, halo_recv, gain_send, gain_recv,
    l_send, l_recv, f_send, f_recv, r_send, r_recv,
    b_send, b_recv, c_send, c_recv, d_send, d_recv, e_send, e_recv, own_edge,
):
    seq, core = lax.axis_index("seq"), lax.axis_index("ch")
    place = (seq // 16, (seq // 4) % 4, seq % 4)

    def peer(axis, step):
        at = [(place[i] + step) % 4 if i == axis else place[i] for i in range(3)]
        return at[0] * 16 + at[1] * 4 + at[2]

    def local(src, dst, sem):
        return pltpu.make_async_copy(src, dst, sem)

    def link(src, dst, send, recv, axis, step):
        return pltpu.make_async_remote_copy(
            src_ref=src, dst_ref=dst, send_sem=send, recv_sem=recv,
            device_id=(peer(axis, step), core), device_id_type=MESH)

    def cross(src, dst, send, recv):
        return pltpu.make_async_remote_copy(
            src_ref=src, dst_ref=dst, send_sem=send, recv_sem=recv,
            device_id=(seq, 1 - core), device_id_type=MESH)

    def started(copies):
        for c in copies:
            c.start()
        return copies

    def waited(copies):
        for c in copies:
            c.wait()

    def all_of(view, sem):
        local(view, view, sem).wait()

    def all_links(view, send, recv):
        link(view, view, send, recv, 0, 1).wait()

    tok_load = local(tokens, tok_v, load_sem.at[0])
    cot_load = local(cotangent, cot_v, load_sem.at[1])
    out_load = local(outproj, out_v, load_sem.at[2])
    gain_loads = [local(mixgain_1d, mixgain.at[0], load_sem.at[3]), local(glugain_1d, glugain.at[0], load_sem.at[4])]
    in_loads = [local(inproj.at[k], col.at[k, :, pl.ds(0, HALF)], col_sem.at[3 + k]) for k in range(3)]
    tok_load.start()
    started(gain_loads)
    in_loads[0].start()
    in_loads[2].start()
    in_loads[1].start()

    def pair_loads(s):
        slot, w = (s + 1) % 3, span(s)
        return [
            local(weight.at[:, pl.ds(SPAN * s, w)], col.at[slot, :, pl.ds(w * m, w)], col_sem.at[slot])
            for m, weight in enumerate((gate_w, lift_w))]

    def down_loads(t):
        s, slot = t % STEPS, t % 3
        return [local(down_w.at[pl.ds(SPAN * s, span(s)), :], down_ring.at[slot, pl.ds(0, span(s)), :], down_sem.at[slot])]

    def pair_ready(s):
        all_of(col.at[(s + 1) % 3, :, pl.ds(0, 2 * span(s))], col_sem.at[(s + 1) % 3])

    def down_ready(t):
        all_of(down_ring.at[t % 3, pl.ds(0, span(t % STEPS)), :], down_sem.at[t % 3])

    barrier = pltpu.get_barrier_semaphore()
    for axis in range(3):
        for step in range(1, 4):
            pl.semaphore_signal(barrier, inc=1, device_id=(peer(axis, step), core), device_id_type=MESH)
    pl.semaphore_signal(barrier, inc=1, device_id=(seq, 1 - core), device_id_type=MESH)

    block = jnp.int32(0)
    for i in range(64):
        block = jnp.where(block_slots[i] == seq, i, block)
    before = block_slots[jnp.maximum(block - 1, 0)]
    after = block_slots[jnp.minimum(block + 1, 63)]
    has_after = (block < 63).astype(F32)
    rows = lax.broadcasted_iota(jnp.int32, (BLK, 1), 0)
    positions = block * BLK + rows
    start = jnp.zeros((BLK, 1), jnp.int32)
    offset = jnp.int32(0)
    for i in range(4):
        start = jnp.where(offset <= positions, offset, start)
        offset = offset + seq_lengths[i]
    mask1 = (positions - 1 >= start).astype(F32)
    mask2 = (positions - 2 >= start).astype(F32)

    def halo_links(land, job, phase):
        out = []
        for k in range(3):
            where = [pl.ds(0, 4) if axis in ROUTES[k][:phase] else pl.ds(place[axis], 1) for axis in range(3)]
            view = land.at[k, where[0], where[1], where[2]]
            axis = ROUTES[k][phase]
            for step in range(1, 4):
                out.append(link(view, view, halo_send.at[job, phase], halo_recv.at[job, phase], axis, step))
        return out

    def halo_ready(land, job, phase):
        view = (land.at[:, pl.ds(0, 3), 0, 0], land.at[:, pl.ds(0, 3), :, 0], land.at[:, pl.ds(0, 3)])[phase]
        all_links(view, halo_send.at[job, phase], halo_recv.at[job, phase])

    def halo_rows(land, slot):
        at = (slot // 16, (slot // 4) % 4, slot % 4)
        return jnp.concatenate([land[k, at[0], at[1], at[2]] for k in range(3)], axis=1)

    def put_halo(land, two):
        width = two.shape[1] // 3
        for k in range(3):
            land[k, place[0], place[1], place[2]] = two[:, width * k:width * k + width]

    def first_norm(values):
        scale = lax.rsqrt(jnp.mean(values * values, axis=1, keepdims=True) + EPS)
        return scale, values * scale * mixgain[...]

    tok_load.wait()
    put_halo(tails, tok_v[BLK - 16:BLK, :].astype(F32)[14:16])
    pl.semaphore_wait(barrier, 10)
    started(halo_links(tails, 0, 0))
    waited(gain_loads)
    scale_a, n1 = first_norm(tok_v[...].astype(F32))
    n_v[...] = n1.astype(BF16)
    in_loads[0].wait()
    b_v[...] = dot_nn(n_v[...], col[0, :, :HALF])
    started([cot_load])
    for s in range(3):
        started(down_loads(s))
    halo_ready(tails, 0, 0)
    started(halo_links(tails, 0, 1))
    in_loads[2].wait()
    x_v[...] = dot_nn(n_v[...], col[2, :, :HALF])
    v_v[...] = (b_v[...] * x_v[...]).astype(BF16).astype(F32)
    in_loads[1].wait()
    c_v[...] = dot_nn(n_v[...], col[1, :, :HALF])
    started(pair_loads(0))
    cot_load.wait()

    def hidden_grads(first, end):
        for s in range(first, end):
            down_ready(s)
            da_v[:, SPAN * s:SPAN * s + span(s)] = dot_nt(cot_v[...], down_ring[s % 3, :span(s), :])
            started(down_loads(s + 3))

    halo_ready(tails, 0, 1)
    started(halo_links(tails, 0, 2))
    s_src[1] = cot_v[...].T
    m_src[0] = n_v[...].T

    half = pl.ds(pl.multiple_of(core * HALF, HALF), HALF)

    def left_link(job, k, src, step):
        left = (s_left, m_left)[job]
        sem = 1 if job == 1 else 2 + step // 2
        return link(src.at[half, :], left.at[k, half, pl.ds(128 * step, 128)],
                    l_send.at[sem], l_recv.at[sem], k, step)

    def send_left_s(k):
        src = s_src.at[1 if k == 2 else 0]
        s_left[k, :, :128] = src[...]
        for step in (1, 3):
            left_link(0, k, src, step).start()

    def hand_on():
        for n, step in enumerate((1, 3)):
            all_links(s_left.at[:, half, pl.ds(128 * step, 128)], l_send.at[2 + n], l_recv.at[2 + n])
            part = pl.ds(pl.multiple_of(core * HALF + 384 * n, 384), 384)
            for k in range(3):
                link(s_left.at[k, part, pl.ds(128 * step, 128)], s_left.at[k, part, pl.ds(256, 128)],
                     l_send.at[0], l_recv.at[0], k, step).start()

    def send_left_m(k, which):
        for step in range(1, 4):
            @pl.when(((place[k] + step) % 4 == 3) == (which == 1))
            def _():
                left_link(1, k, m_src.at[which], step).start()

    def others(job):
        return (s_left, m_left)[job].at[:, half, pl.ds(128, 384)]

    def forward_left(job):
        if job == 0:
            all_links(s_left.at[:, half, pl.ds(256, 128)], l_send.at[0], l_recv.at[0])
        else:
            all_links(others(1), l_send.at[1], l_recv.at[1])
        cross(others(job), others(job), f_send.at[job], f_recv.at[job]).start()

    started([out_load])
    hidden_grads(0, 4)

    halo_ready(tails, 0, 2)
    send_left_s(2)
    for k in range(3):
        send_left_m(k, 0)
    last_two = jnp.concatenate([halo_rows(tails, before), jnp.zeros((14, D), F32)], axis=0)
    edge_scale, edge = first_norm(last_two)
    xs_send[1] = last_two * edge_scale
    edge = edge.astype(BF16)
    edge_b, edge_x = dot_nn(edge, col[0, :, :HALF]), dot_nn(edge, col[2, :, :HALF])
    carried = (edge_b * edge_x).astype(BF16).astype(F32)
    e_src[...] = edge.astype(F32)[0:2]
    eb_v[...] = edge_b
    ex_v[...] = edge_x

    def edge_left_links(n):
        return [
            link(e_src, e_left.at[n, step], e_send.at[0], e_recv.at[0], 2 * n, step)
            for step in range(1, 4)]

    def edge_piece(n, i):
        return er_two.at[n, :, pl.ds(pl.multiple_of(i * WM, WM), WM)]

    def edge_right_links(n):
        return [
            link(edge_piece(n, (place[2 * n] + step) % 4), e_right.at[n, step],
                 e_send.at[1], e_recv.at[1], 2 * n, step)
            for step in range(1, 4)]

    def edge_own(n):
        return [
            local(e_src, e_left.at[n, 0], own_edge.at[0]),
            local(edge_piece(n, place[2 * n]), e_right.at[n, 0], own_edge.at[1])]
    for s in range(1, 3):
        started(pair_loads(s))
    row_is0, row_is1 = rows == 0, rows == 1
    tap0, tap1, tap2 = taps[0:1, :], taps[1:2, :], taps[2:3, :]

    def shifted():
        v = v_v[...]
        one = jnp.where(row_is0, carried[1:2], pltpu.roll(v, 1, 0)) * mask1
        two = jnp.where(row_is0, carried[0:1], jnp.where(row_is1, carried[1:2], pltpu.roll(v, 2, 0))) * mask2
        return v, one, two

    v0, v1, v2 = shifted()
    u_v[...] = tap0 * v0 + tap1 * v1 + tap2 * v2
    y_v[...] = (c_v[...] * u_v[...]).astype(BF16)
    out_load.wait()
    xh_send[0] = dot_nn(y_v[...], out_v[...]).astype(BF16)
    swap = cross(xh_send.at[0], xh_recv.at[0], x_send.at[0], x_recv.at[0])
    swap.start()
    hidden_grads(4, 6)
    swap.wait()
    h2_v[...] = tok_v[...].astype(F32) + (xh_send[0].astype(F32) + xh_recv[0].astype(F32))
    h2 = h2_v[...]
    scale_b = lax.rsqrt(jnp.mean(h2 * h2, axis=1, keepdims=True) + EPS)
    n_v[...] = (h2 * scale_b * glugain[...]).astype(BF16)
    s_src[0] = n_v[...].T
    send_left_s(0)
    send_left_s(1)

    lefts, rights, dsends, dlands = (s_left, m_left), (s_right, m_right), (s_dsend, m_dsend), (s_dland, m_dland)

    def right_piece(job, k, i, g):
        if job == 0:
            return act.at[k, i, :, pl.ds(*GROUPS[0][g])]
        return mixed_r.at[k, :, pl.ds(pl.multiple_of(i * WM, WM), WM)]

    def right_links(job, k, g):
        lanes = pl.ds(*GROUPS[job][g])
        return [
            link(right_piece(job, k, (place[k] + step) % 4, g), rights[job].at[k, pl.ds(128 * step, 128), lanes],
                 r_send.at[4 * job + g], r_recv.at[4 * job + g], k, step)
            for step in range(1, 4)]

    def send_right(job, g):
        for k in range(3):
            started(right_links(job, k, g))
        first, width = GROUPS[job][g]
        for k in range(3):
            rights[job][k, :128, first:first + width] = right_piece(job, k, place[k], g)[...]

    def b_out(job, k, j, g, row=0, count=384):
        lanes = pl.ds(*GROUPS[job][g])
        if job == 0:
            return s_bsend.at[k, j, pl.ds(row, count), lanes]
        return col.at[1, pl.ds(pl.multiple_of(384 * j + row, 96), count), pl.ds(WM * k, WM)]

    def b_in(job, k, i, g, row=0, count=384):
        if job == 0:
            return s_bland.at[k, i, pl.ds(row, count), pl.ds(*GROUPS[job][g])]
        return down_ring.at[i, pl.ds(row, count), pl.ds(WM * k, WM)]

    def c_out(job, k, j, g, row=0, count=96):
        return rights[job].at[k, pl.ds(pl.multiple_of(96 * j + row, 48), count), pl.ds(*GROUPS[job][g])]

    def c_in(job, k, i, g):
        if job == 0:
            return s_cland.at[k, i, :, pl.ds(*GROUPS[job][g])]
        return down_ring.at[i, pl.ds(0, 96), pl.ds(HALF + WM * k, WM)]

    LOW, HIGH = 0, 192

    def b_links(job, k, g, which):
        axis = (k + 1) % 3
        me = place[axis]
        opposite, ahead, behind = (me + 2) % 4, (me + 1) % 4, (me + 3) % 4
        table = (
            (opposite, LOW, 2, 1), (ahead, HIGH, 0, 1), (opposite, HIGH, 2, 3),
            (behind, LOW, 1, 3), (ahead, LOW, 0, 1), (behind, HIGH, 1, 3))
        out = []
        for n in which:
            part, row, land, step = table[n]
            sem = 2 * (4 * job + g) + (land != 2)
            out.append(link(b_out(job, k, part, g, row, 192), b_in(job, k, land, g, row, 192),
                            b_send.at[sem], b_recv.at[sem], axis, step))
        return out

    def c_links(job, k, g):
        axis = (k + 2) % 3
        return [
            link(c_out(job, k, (place[axis] + step) % 4, g), c_in(job, k, step - 1, g),
                 c_send.at[4 * job + g], c_recv.at[4 * job + g], axis, step)
            for step in range(1, 4)]

    def right_ready(job, g):
        lanes, n = pl.ds(*GROUPS[job][g]), 4 * job + g
        all_links(rights[job].at[:, pl.ds(128, 384), lanes], r_send.at[n], r_recv.at[n])

    def edges_ready():
        all_of(e_left.at[:, 0], own_edge.at[0])
        all_of(e_right.at[:, 0], own_edge.at[1])
        all_links(e_left.at[:, pl.ds(1, 3)], e_send.at[0], e_recv.at[0])
        all_links(e_right.at[:, pl.ds(1, 3)], e_send.at[1], e_recv.at[1])

    def edge_tile(parts):
        return jnp.concatenate([*parts, jnp.zeros((8, parts[0].shape[1]), F32)], axis=0).astype(BF16)

    def start_b(job, k, g):
        lanes = pl.ds(*GROUPS[job][g])
        edges = job == 1 and k != 1

        def slab(x, carry):
            at = pl.ds(pl.multiple_of(x * 384, 384), 384)
            acc = dot_nn(lefts[job][k, at, :], rights[job][k, :, lanes])
            if edges:
                acc = acc + outer(edge_tile([e_left[k // 2, i, :, at] for i in range(4)]), edge_tile([e_right[k // 2, i] for i in range(4)]))
            row = pl.multiple_of(96 * x, 96)
            for j in range(4):
                if k == 0:
                    b_out(job, k, j, g, row, 96)[...] = acc[96 * j:96 * j + 96].astype(BF16)
                elif k == 1:
                    parts = [acc[96 * y + 24 * j:96 * y + 24 * j + 24] for y in range(4)]
                    b_out(job, k, j, g, row, 96)[...] = jnp.concatenate(parts, axis=0).astype(BF16)
                else:
                    b_out(job, k, x, g, 96 * j, 96)[...] = acc[96 * j:96 * j + 96].astype(BF16)
            return carry

        lax.fori_loop(0, 4, slab, 0)
        started(b_links(job, k, g, range(4)))

    def b_ready(job, g, last):
        sem = 2 * (4 * job + g) + last
        if job == 0:
            view = s_bland.at[:, pl.ds(0, 2) if last else pl.ds(2, 1), :, pl.ds(*GROUPS[job][g])]
        else:
            view = down_ring.at[pl.ds(0, 2) if last else pl.ds(2, 1), pl.ds(0, 384), pl.ds(0, HALF)]
        all_links(view, b_send.at[sem], b_recv.at[sem])

    def pass_on(job, k, g):
        me = place[(k + 1) % 3]
        for step, row in ((1, LOW), (3, HIGH)):
            own, via = b_out(job, k, (me + step) % 4, g, row, 192), b_in(job, k, 2, g, row, 192)
            own[...] = (own[...].astype(F32) + via[...].astype(F32)).astype(BF16)
        started(b_links(job, k, g, (4, 5)))

    def c_halves(k, g, which):
        axis = (k + 2) % 3
        me = place[axis]
        opposite, ahead, behind = (me + 2) % 4, (me + 1) % 4, (me + 3) % 4
        table = ((opposite, 0, 2, 1), (ahead, 48, 0, 1), (opposite, 48, 2, 3), (behind, 0, 1, 3), (ahead, 0, 0, 1), (behind, 48, 1, 3))
        out = []
        for n in which:
            part, row, land, step = table[n]
            sem = 5 + g if land == 2 else g
            out.append(link(c_out(0, k, part, g, row, 48), s_cland.at[k, land, pl.ds(row, 48), pl.ds(*GROUPS[0][g])],
                            c_send.at[sem], c_recv.at[sem], axis, step))
        return out

    def pass_on_c(g):
        lanes = pl.ds(*GROUPS[0][g])
        all_links(s_cland.at[:, pl.ds(2, 1), :, lanes], c_send.at[5 + g], c_recv.at[5 + g])
        for k in range(3):
            for step, row in ((1, 0), (3, 48)):
                mine, via = c_out(0, k, (place[(k + 2) % 3] + step) % 4, g, row, 48), s_cland.at[k, 2, pl.ds(row, 48), lanes]
                mine[...] = (mine[...].astype(F32) + via[...].astype(F32)).astype(BF16)
            started(c_halves(k, g, (4, 5)))

    def c_ready(job, g):
        if job == 0:
            view = s_cland.at[:, pl.ds(0, 2 if g < 3 else 3), :, pl.ds(*GROUPS[job][g])]
        else:
            view = down_ring.at[:, pl.ds(0, 96), pl.ds(HALF, HALF)]
        all_links(view, c_send.at[4 * job + g], c_recv.at[4 * job + g])

    def start_c(job, k, g):
        me = place[(k + 1) % 3]

        def summed(q):
            total = b_out(job, k, me, g, 96 * q, 96)[...].astype(F32)
            for i in range(2):
                total = total + b_in(job, k, i, g, 96 * q, 96)[...].astype(F32)
            return total

        if k == 0:
            for p in range(2):
                a, b = summed(2 * p), summed(2 * p + 1)
                for j in range(4):
                    both = jnp.concatenate([a[24 * j:24 * j + 24], b[24 * j:24 * j + 24]], axis=0)
                    c_out(job, k, j, g, 48 * p, 48)[...] = both.astype(BF16)
        else:
            for q in range(4):
                c_out(job, k, q, g)[...] = summed(q).astype(BF16)
        started(c_halves(k, g, range(4)) if job == 0 and g < 3 else c_links(job, k, g))

    def d_links(job, k):
        return [
            link(dsends[job].at[k, (place[k] + step) % 4], dlands[job].at[k, step],
                 d_send.at[job], d_recv.at[job], k, step)
            for step in range(1, 4)]

    def start_d(job, k):
        dsend, dland = dsends[job], dlands[job]
        for g, (first, width) in enumerate(GROUPS[job]):
            total = c_out(job, k, place[(k + 2) % 3], g)[...].astype(F32)
            for i in range(2 if job == 0 and g < 3 else 3):
                total = total + c_in(job, k, i, g)[...].astype(F32)
            pad = jnp.zeros((8, width), F32)
            for j in range(4):
                dsend[k, j, :, first:first + width] = jnp.concatenate([total[24 * j:24 * j + 24], pad], axis=0).astype(BF16)
        dland[k, 0] = dsend[k, place[k]]
        started(d_links(job, k))

    def finish(job, k):
        pieces = [dlands[job][k, (place[k] - i + 4) % 4].astype(F32)[:24] for i in range(4)]
        if job == 0:
            for i in range(4):
                for s in range(STEPS):
                    if SPAN * s + 128 * i < FF:
                        da_v[32 * k:32 * k + 24, SPAN * s + 128 * i:SPAN * s + 128 * i + 128] = pieces[i][:, 128 * s:128 * s + 128]
            local(da_v.at[pl.ds(32 * k, 24), :], (o_gate, o_lift, o_down)[k], store_sem.at[k]).start()
        else:
            stage = (h2_v, glu_v, dn2_v)[k]
            for i in range(4):
                stage[:24, WM * i:WM * i + WM] = pieces[i]
            local(stage.at[pl.ds(0, 24), pl.ds(0, HALF)], o_in.at[k], store_sem.at[3]).start()
            local(stage.at[pl.ds(0, 24), pl.ds(HALF, WM)], o_out.at[:, pl.ds(WM * k, WM)], store_sem.at[4]).start()

    glu_v[...] = jnp.zeros_like(glu_v)
    dn2_v[...] = jnp.zeros_like(dn2_v)

    def swiglu_step(s):
        slot = (s + 1) % 3
        pair_ready(s)
        w = span(s)
        both = dot_nn(n_v[...], col[slot, :, :2 * w])
        gate_pre, lift_pre = both[:, :w], both[:, w:]
        hidden_grad = da_v[:, SPAN * s:SPAN * s + w]
        sig = jax.nn.sigmoid(gate_pre)
        silu = gate_pre * sig
        hidden = (silu * lift_pre).astype(BF16)
        d_lift = (hidden_grad * silu).astype(BF16)
        d_gate = (hidden_grad * lift_pre * sig * (1.0 + gate_pre * (1.0 - sig))).astype(BF16)
        for k, values in enumerate((d_gate, d_lift, hidden)):
            for i in range(4):
                part = values[:, 128 * i:128 * i + 128] if 128 * i < w else jnp.zeros((BLK, 128), BF16)
                act[k, i, :, 128 * s:128 * s + 128] = part
        down_ready(STEPS + s)
        glu_v[...] += dot_nn(hidden, down_ring[(STEPS + s) % 3, :w, :])
        dn2_v[...] += dot_nt(jnp.concatenate([d_gate, d_lift], axis=1), col[slot, :, :2 * w])
        if s + 3 < STEPS:
            started(pair_loads(s + 3))
            started(down_loads(STEPS + s + 3))

    def left_ready(job):
        cross(others(job), others(job), f_send.at[job], f_recv.at[job]).wait()

    hidden_grads(6, STEPS)
    for s in range(2):
        swiglu_step(s)
    send_right(0, 0)
    swiglu_step(2)
    hand_on()
    swiglu_step(3)
    send_right(0, 1)
    forward_left(0)
    swiglu_step(4)
    left_ready(0)
    right_ready(0, 0)
    for k in range(3):
        start_b(0, k, 0)
    swiglu_step(5)
    send_right(0, 2)
    right_ready(0, 1)
    for k in range(3):
        start_b(0, k, 1)
    b_ready(0, 0, 0)
    for k in range(3):
        pass_on(0, k, 0)
    swiglu_step(6)
    send_right(0, 3)
    started(in_loads)

    xh_send[0] = dn2_v[...].astype(BF16)
    swap_dn2 = cross(xh_send.at[0], xh_recv.at[0], x_send.at[1], x_recv.at[1])
    swap_dn2.start()
    xh_send[1] = glu_v[...].astype(BF16)
    swap_glu = cross(xh_send.at[1], xh_recv.at[1], x_send.at[2], x_recv.at[2])
    swap_glu.start()
    swap_dn2.wait()
    h2 = h2_v[...]
    z2 = h2 * scale_b
    dn2 = xh_send[0].astype(F32) + xh_recv[0].astype(F32)
    glu_term = jnp.sum(dn2 * z2, axis=0, keepdims=True)
    scaled = dn2 * glugain[...]
    glu_v[...] = cot_v[...].astype(F32) + scale_b * (scaled - z2 * jnp.mean(scaled * z2, axis=1, keepdims=True))
    n_v[...] = glu_v[...].astype(BF16)
    dy = dot_nt(n_v[...], out_v[...])
    d_c = (dy * u_v[...]).astype(BF16)
    du = dy * c_v[...]
    v0, v1, v2 = shifted()
    tap_terms = [jnp.sum(du * v, axis=0, keepdims=True) for v in (v0, v1, v2)]
    w1, w2 = tap1 * (du * mask1), tap2 * (du * mask2)
    two = jnp.concatenate([w2[0:1], w1[0:1] + w2[1:2]], axis=0)
    put_halo(heads, two)
    started(halo_links(heads, 1, 0))
    dv = (tap0 * du + jnp.where(rows < 127, pltpu.roll(w1, 127, 0), 0.0)
          + jnp.where(rows < 126, pltpu.roll(w2, 126, 0), 0.0))
    mixed_r[0, :, :HALF] = (dv * x_v[...]).astype(BF16)
    mixed_r[1, :, :HALF] = d_c
    mixed_r[2, :, :HALF] = (dv * b_v[...]).astype(BF16)
    y_out = y_v[...]
    for k in range(3):
        mixed_r[k, :, HALF:] = y_out[:, 256 * k:256 * k + 256]
    share = jnp.concatenate([two, jnp.zeros((14, HALF), F32)], axis=0)
    none = jnp.zeros((16, WM), BF16)
    for n, other in enumerate((ex_v, eb_v)):
        er_src[n] = jnp.concatenate([(share * other[...]).astype(BF16), none], axis=1)
        er_two[n] = er_src[n].astype(F32)[0:2]
    send_right(1, 0)
    for n in range(2):
        started(edge_own(n))
        started(edge_left_links(n))
        started(edge_right_links(n))
    m_src[1] = n_v[...].T
    for k in range(3):
        send_left_m(k, 1)
        m_left[k, :, :128] = m_src[jnp.where(place[k] == 3, 1, 0)]
    b_ready(0, 1, 0)
    for k in range(3):
        pass_on(0, k, 1)
    right_ready(0, 2)
    for k in range(3):
        start_b(0, k, 2)
    swap_glu.wait()
    xh_send[1] = (h2_v[...] + (xh_send[1].astype(F32) + xh_recv[1].astype(F32))).astype(BF16)
    stores = started([local(xh_send.at[1], o_layer, load_sem.at[5])])
    b_ready(0, 0, 1)
    for k in range(3):
        start_c(0, k, 0)

    def my_half(row):
        return jnp.where(core == 0, row[:, :HALF], row[:, HALF:])

    def gain_links(axis):
        view = gain_land.at[axis, place[axis]]
        return [link(view, view, gain_send.at[axis], gain_recv.at[axis], axis, step) for step in range(1, 4)]

    def gain_sum(axis):
        all_links(gain_land.at[axis, pl.ds(0, 3)], gain_send.at[axis], gain_recv.at[axis])
        return (gain_land[axis, 0] + gain_land[axis, 1]) + (gain_land[axis, 2] + gain_land[axis, 3])

    def input_rows(dn1, first):
        z1 = tok_v[first:, :].astype(F32) * scale_a[first:]
        scaled = dn1 * mixgain[...]
        n_v[first:, :] = (glu_v[first:, :] + scale_a[first:] * (scaled - z1 * jnp.mean(scaled * z1, axis=1, keepdims=True))).astype(BF16)
        return z1

    waited(in_loads)
    for k in range(3):
        part = dot_nt(mixed_r[k, :, :HALF], col[k, :, :HALF])
        if k == 0:
            dn2_v[...] = part
        else:
            dn2_v[...] += part
    ahead = dot_nt(er_src[0, :, :HALF], col[0, :, :HALF]) + dot_nt(er_src[1, :, :HALF], col[2, :, :HALF])
    swap_dn1 = cross(dn2_v, da_v.at[:, pl.ds(0, D)], x_send.at[3], x_recv.at[3])
    swap_dn1.start()
    xs_send[0] = jnp.concatenate([jnp.sum(ahead * xs_send[1], axis=0, keepdims=True), jnp.zeros((15, D), F32)], axis=0)
    swap_row = cross(xs_send.at[0], da_v.at[pl.ds(0, 16), pl.ds(D, D)], x_send.at[4], x_recv.at[4])
    swap_row.start()
    right_ready(0, 3)
    for k in range(3):
        start_b(0, k, 3)
    swap_dn1.wait()
    swap_row.wait()
    dn1 = dn2_v[...] + da_v[:, :D]
    z1 = input_rows(dn1, 0)
    mix_term = jnp.sum(dn1 * z1, axis=0, keepdims=True) + (xs_send[0, 0:1] + da_v[0:1, D:2 * D])
    gain_land[0, place[0]] = jnp.concatenate(
        [my_half(mix_term), my_half(glu_term), *tap_terms, jnp.zeros((3, HALF), F32)], axis=0)
    started(gain_links(0))
    forward_left(1)
    halo_ready(heads, 1, 0)
    started(halo_links(heads, 1, 1))
    left_ready(1)
    right_ready(1, 0)
    edges_ready()
    for k in range(3):
        start_b(1, k, 0)
    b_ready(0, 2, 0)
    for k in range(3):
        pass_on(0, k, 2)
    b_ready(0, 1, 1)
    for k in range(3):
        start_c(0, k, 1)
    b_ready(0, 3, 0)
    for k in range(3):
        pass_on(0, k, 3)
    pass_on_c(0)
    halo_ready(heads, 1, 1)
    started(halo_links(heads, 1, 2))
    gain_land[1, place[1]] = gain_sum(0)
    started(gain_links(1))
    b_ready(1, 0, 0)
    for k in range(3):
        pass_on(1, k, 0)
    pass_on_c(1)
    b_ready(0, 2, 1)
    for k in range(3):
        start_c(0, k, 2)
    b_ready(0, 3, 1)
    for k in range(3):
        start_c(0, k, 3)
    gain_land[2, place[2]] = gain_sum(1)
    started(gain_links(2))
    halo_ready(heads, 1, 2)
    incoming = jnp.concatenate([jnp.zeros((14, HALF), F32), halo_rows(heads, after) * has_after], axis=0)
    xs_send[1] = (dot_nt((incoming * x_v[BLK - 16:, :]).astype(BF16), col[0, :, :HALF])
                  + dot_nt((incoming * b_v[BLK - 16:, :]).astype(BF16), col[2, :, :HALF]))
    swap = cross(xs_send.at[1], da_v.at[pl.ds(16, 16), pl.ds(D, D)], x_send.at[5], x_recv.at[5])
    swap.start()
    b_ready(1, 0, 1)
    for k in range(3):
        start_c(1, k, 0)
    pass_on_c(2)
    swap.wait()
    input_rows((dn2_v[BLK - 16:, :] + da_v[BLK - 16:, :D]) + (xs_send[1] + da_v[16:32, D:2 * D]), BLK - 16)
    stores += started([local(n_v, o_input, load_sem.at[6])])
    v_v[0:8, :] = gain_sum(2)
    stores += started([local(v_v.at[pl.ds(0, 8), :], o_gains, load_sem.at[7])])
    for g in range(4):
        c_ready(0, g)
    for k in range(3):
        start_d(0, k)
    c_ready(1, 0)
    for k in range(3):
        start_d(1, k)
    for job in range(2):
        all_links(dlands[job].at[:, pl.ds(1, 3)], d_send.at[job], d_recv.at[job])
        for k in range(3):
            finish(job, k)
    for n, out in enumerate((o_gate, o_lift, o_down, o_in, o_out)):
        all_of(out, store_sem.at[n])
    waited(stores)


def run_layer(seq_lengths, block_slots, mixgain, glugain, taps, tokens, cotangent, inproj, outproj, gate_w, lift_w, down_w):
    vm = pl.BlockSpec(memory_space=pltpu.VMEM)
    sm = pl.BlockSpec(memory_space=pltpu.SMEM)
    hbm = pl.BlockSpec(memory_space=pl.ANY)
    dma = pltpu.SemaphoreType.DMA
    shape = jax.ShapeDtypeStruct
    row, full16, full32, half32 = (
        pltpu.VMEM((1, D), F32), pltpu.VMEM((BLK, D), BF16), pltpu.VMEM((BLK, D), F32), pltpu.VMEM((BLK, HALF), F32))
    return pl.pallas_call(
        layer_kernel,
        out_shape=[shape((BLK, D), BF16), shape((BLK, D), BF16), shape((8, HALF), F32)]
        + [shape(s, F32) for s in ((24, FF), (24, FF), (24, FF), (3, 24, HALF), (24, HALF))],
        in_specs=[sm, sm, hbm, hbm, vm] + [hbm] * 7,
        out_specs=[hbm] * 8,
        scratch_shapes=[
            row, row, full16, full16, full16,
            half32, half32, half32, half32, half32, pltpu.VMEM((BLK, HALF), BF16),
            full32, full32, full32,
            pltpu.VMEM((3, D, 2 * SPAN), BF16), pltpu.VMEM((3, SPAN, D), BF16), pltpu.VMEM((HALF, D), BF16),
            pltpu.VMEM((BLK, FF), F32), pltpu.VMEM((3, 4, BLK, WS), BF16), pltpu.VMEM((3, BLK, 4 * WM), BF16),
            pltpu.VMEM((2, D, BLK), BF16), pltpu.VMEM((2, D, BLK), BF16),
            pltpu.VMEM((2, D), F32), pltpu.VMEM((16, HALF), F32), pltpu.VMEM((16, HALF), F32),
            pltpu.VMEM((2, 16, 4 * WM), BF16), pltpu.VMEM((2, 2, 4 * WM), F32), pltpu.VMEM((2, 4, 2, D), F32), pltpu.VMEM((2, 4, 2, WM), F32),
            pltpu.VMEM((2, BLK, D), BF16), pltpu.VMEM((2, BLK, D), BF16), pltpu.VMEM((2, 16, D), F32),
            pltpu.VMEM((3, 4, 4, 4, 2, 512), F32), pltpu.VMEM((3, 4, 4, 4, 2, 256), F32),
            pltpu.VMEM((3, 4, 8, HALF), F32),
            pltpu.VMEM((3, D, 512), BF16), pltpu.VMEM((3, 512, WS), BF16), pltpu.VMEM((3, 4, 384, WS), BF16),
            pltpu.VMEM((3, 3, 384, WS), BF16), pltpu.VMEM((3, 3, 96, WS), BF16),
            pltpu.VMEM((3, 4, 32, WS), BF16), pltpu.VMEM((3, 4, 32, WS), BF16),
            pltpu.VMEM((3, D, 512), BF16), pltpu.VMEM((3, 512, WM), BF16),
            pltpu.VMEM((3, 4, 32, WM), BF16), pltpu.VMEM((3, 4, 32, WM), BF16),
            dma((8,)), dma((6,)), dma((3,)), dma((5,)), dma((6,)), dma((6,)),
            dma((2, 3)), dma((2, 3)), dma((3,)), dma((3,)),
            dma((4,)), dma((4,)), dma((2,)), dma((2,)), dma((5,)), dma((5,)),
            dma((10,)), dma((10,)), dma((8,)), dma((8,)), dma((2,)), dma((2,)),
            dma((2,)), dma((2,)), dma((2,)),
        ],
        compiler_params=pltpu.CompilerParams(collective_id=1, has_side_effects=True, vmem_limit_bytes=LIMIT),
        name="layer",
    )(seq_lengths, block_slots, mixgain, glugain, taps, tokens, cotangent, inproj, outproj, gate_w, lift_w, down_w)


def place_kernel(*refs):
    ins, outs, held, in_sems, out_sems = refs[:8], refs[8:18], refs[18:26], refs[26], refs[27]
    loads = [pltpu.make_async_copy(a, b, in_sems.at[i]) for i, (a, b) in enumerate(zip(ins, held))]
    for c in loads:
        c.start()
    gains = held[2]
    parts = [held[0], held[1], gains.at[0], gains.at[1], gains.at[pl.ds(2, 3)], *held[3:]]
    stores = []
    for i, (a, b) in enumerate(zip(parts, outs)):
        if i not in (3, 4):
            loads[i if i < 3 else i - 2].wait()
        stores.append(pltpu.make_async_copy(a, b, out_sems.at[i]))
        stores[-1].start()
    for c in stores:
        c.wait()


def place_outputs(results):
    hbm = pl.BlockSpec(memory_space=pl.ANY)
    shape = jax.ShapeDtypeStruct
    return pl.pallas_call(
        place_kernel,
        out_shape=[shape((BLK, D), BF16), shape((BLK, D), BF16), shape((HALF,), F32), shape((HALF,), F32), shape((3, HALF), F32)]
        + [shape(s, F32) for s in ((24, FF), (24, FF), (24, FF), (3, 24, HALF), (24, HALF))],
        in_specs=[hbm] * 8,
        out_specs=[hbm] * 10,
        scratch_shapes=[pltpu.VMEM(r.shape, r.dtype) for r in results] + [pltpu.SemaphoreType.DMA((8,)), pltpu.SemaphoreType.DMA((10,))],
        name="place",
    )(*results)


def on_device(
    tokens, cotangent, seq_lengths, block_slots, mixgain, inproj, conv_taps, outproj, glugain, gate_weight, lift_weight, down_weight
):
    results = run_layer(
        seq_lengths, block_slots, mixgain, glugain, conv_taps,
        tokens, cotangent, inproj, outproj, gate_weight, lift_weight, down_weight,
    )
    layer_out, input_grad, mixgain_grad, glugain_grad, taps_grad, gate_grad, lift_grad, down_rows, inproj_grad, out_rows = place_outputs(results)
    return (
        layer_out, input_grad, mixgain_grad, inproj_grad, taps_grad, out_rows.T, glugain_grad, gate_grad, lift_grad, down_rows.T,
    )


def solution(mesh):
    in_specs = (
        P("seq", None), P("seq", None), P(), P(), P(), P(None, None, "ch"), P(None, "ch"), P("ch", None),
        P(), P(None, "ch"), P(None, "ch"), P("ch", None),
    )
    out_specs = (
        P("seq", None), P("seq", None), P("ch"), P(None, "seq", "ch"), P(None, "ch"), P("ch", "seq"),
        P("ch"), P("seq", "ch"), P("seq", "ch"), P("ch", "seq"),
    )
    return jax.shard_map(on_device, mesh=mesh, in_specs=in_specs, out_specs=out_specs, check_vma=False)
```
